32 devices in a mesh: dp: 8 (over z, y), tensor: 4 (over x, core).
Axes of the slice: x: 2, y: 2, z: 4, core: 2. Of those that a mesh axis runs over, the one named last changes fastest.
Arguments:
- hidden_in: bfloat16 [16384, 768], P(('dp', 'tensor')), may hold values from -33 to 33
- positions: int32 [16384], P('dp'), may hold values from 0 to 2047, as said below
- mixer_gain: float32 [768], replicated, may hold values from 0.5 to 1.5
- mixer_shift: float32 [768], replicated, may hold values from -2 to 2
- feed_gain: float32 [768], replicated, may hold values from 0.5 to 1.5
- feed_shift: float32 [768], replicated, may hold values from -2 to 2
- triple_weight: bfloat16 [768, 3, 768], P('dp', None, 'tensor'), may hold values from -3 to 3
- pair_bias: float32 [2, 768], P(None, 'tensor'), may hold values from -2 to 2
- output_weight: bfloat16 [768, 768], P('tensor', 'dp'), may hold values from -1.75 to 1.75
- up_weight: bfloat16 [768, 3072], P('dp', 'tensor'), may hold values from -0.21875 to 0.21875
- up_bias: float32 [3072], P('tensor'), may hold values from -2 to 2
- down_weight: bfloat16 [3072, 768], P('tensor', 'dp'), may hold values from -0.109375 to 0.109375
- out_bias: float32 [768], replicated, may hold values from -2 to 2
- out_grad: bfloat16 [16384, 768], P(('dp', 'tensor')), may hold values from -6 to 6
Outputs:
- result: float32 [16384, 768], P(('dp', 'tensor'))
- grad_hidden: float32 [16384, 768], P(('dp', 'tensor'))
- grad_mixer_gain: float32 [768], replicated
- grad_mixer_shift: float32 [768], replicated
- grad_feed_gain: float32 [768], replicated
- grad_feed_shift: float32 [768], replicated
- grad_triple: float32 [768, 3, 768], P('dp', None, 'tensor')
- grad_pair_bias: float32 [2, 768], P(None, 'tensor')
- grad_output: float32 [768, 768], P('tensor', 'dp')
- grad_up: float32 [768, 3072], P('dp', 'tensor')
- grad_up_bias: float32 [3072], P('tensor')
- grad_down: float32 [3072, 768], P('tensor', 'dp')
- grad_out_bias: float32 [768], replicated
The draws below stay inside these ranges and needn't reach their ends.
Inputs may be any that keep to these rules, and one draw needn't show every extreme that they name: `positions`: documents follow one another without gaps from the stream's first token; each has an eighth of 2048 to 2048 tokens (the last one may be cut by the stream's end) and one has exactly 2048; a token's position counts from its document's first token.
All inputs are finite; a program needn't handle non-finite values.
Results may differ from the reference program's by a relative error of at most 0.0086.
Values may be sent and summed in bfloat16 or wider, within the bound.
No kernel may reach another device: no remote copies, remote signals or barrier semaphores. Data moves between devices by JAX's collectives and lax.ppermute only.
A program may use at most 192 MiB of HBM per device.

```python
import math
import jax
import jax.numpy as jnp
from jax import lax

D = 768
H = 12
HD = 64
FF = 3072
ROT = 16
DOC_MOST = 2048
TOKENS = 16384


def draw_positions(key, part):
    key = jax.random.fold_in(key, 11)
    least_len = DOC_MOST // 8
    doc_count = TOKENS // least_len + 2
    lengths = jax.random.randint(jax.random.fold_in(key, 1), (doc_count,), least_len, DOC_MOST + 1)
    chosen = jax.random.randint(jax.random.fold_in(key, 2), (), 0, TOKENS // DOC_MOST)
    lengths = jnp.where(jnp.arange(doc_count, dtype=jnp.int32) == chosen, DOC_MOST, lengths).astype(jnp.int32)
    doc_ends = jnp.cumsum(lengths)
    doc_starts = doc_ends - lengths
    index_rows = jnp.arange(TOKENS, dtype=jnp.int32)
    owner_doc = jnp.searchsorted(doc_ends, index_rows, side='right')
    return (index_rows - doc_starts[owner_doc]).astype(jnp.int32)


def draw_hidden_in(key, part):
    key = jax.random.fold_in(key, 12)
    base = jax.random.truncated_normal(jax.random.fold_in(key, 1), -4.0, 4.0, (TOKENS, D), jnp.float32)
    row_scale = jnp.exp(jax.random.uniform(jax.random.fold_in(key, 2), (TOKENS, 1), jnp.float32, math.log(0.3), math.log(3.0)))
    col_scale = jnp.exp(jax.random.uniform(jax.random.fold_in(key, 3), (1, D), jnp.float32, math.log(0.5), math.log(2.0)))
    return (base * row_scale * col_scale).astype(jnp.bfloat16)


def draw_triple_weight(key, part):
    key = jax.random.fold_in(key, 13)
    base = jax.random.truncated_normal(jax.random.fold_in(key, 1), -4.0, 4.0, (D, 3, D), jnp.float32)
    return (base * (1.0 / math.sqrt(D))).astype(jnp.bfloat16)


def with_spikes(array, rng, source, target, shards_of, factor):
    def block_of(dim):
        return (jnp.arange(array.shape[dim]) // (array.shape[dim] // shards_of)).reshape((-1,) + (1,) * (array.ndim - 1 - dim))

    first = jax.random.permutation(rng, shards_of)[block_of(target)]
    far = (block_of(target) + shards_of // 2) % shards_of
    return jnp.where((block_of(source) == first) | (block_of(source) == far), factor * array, array)


def shard_levels(stream_key, dims, cuts, least, largest):
    level = 1.0
    for axis_at, parts in cuts:
        draws = jax.random.uniform(jax.random.fold_in(jax.random.fold_in(stream_key, 6), axis_at), (parts,), jnp.float32, least / len(cuts), largest / len(cuts))
        level = level * jnp.repeat(jnp.exp(draws), dims[axis_at] // parts).reshape((-1,) + (1,) * (len(dims) - 1 - axis_at))
    return level


def gaussian(own_key, dims, width, limit, pieces=(), held_as=jnp.bfloat16):
    values = width * jax.random.normal(own_key, dims, jnp.float32)
    if pieces:
        values = values * shard_levels(own_key, dims, pieces, -0.22, 0.18)
    return jnp.clip(values, -limit, limit).astype(held_as)


def noise_with(stream_key, dims, spread, bound, split, heavy, held_as=jnp.bfloat16):
    values = spread * jax.random.normal(stream_key, dims, jnp.float32)
    if split:
        values = values * shard_levels(stream_key, dims, split, -0.22, 0.18)
    return jnp.clip(with_spikes(values, jax.random.fold_in(stream_key, 3), *heavy), -bound, bound).astype(held_as)


def setup_inputs(seed: int = 0) -> dict:
    key_of = jax.random.split(jax.random.key(seed), 15)
    return {
        "hidden_in": draw_hidden_in(jax.random.fold_in(key_of[14], 71), 0),
        "positions": draw_positions(jax.random.fold_in(key_of[14], 71), 0),
        "mixer_gain": jnp.clip(1.0 + 0.1 * jax.random.normal(key_of[2], (D,), jnp.float32), 0.5, 1.5),
        "mixer_shift": gaussian(key_of[3], (D,), 0.3, 2.0, (), jnp.float32),
        "feed_gain": jnp.clip(1.0 + 0.1 * jax.random.normal(key_of[4], (D,), jnp.float32), 0.5, 1.5),
        "feed_shift": gaussian(key_of[5], (D,), 0.3, 2.0, (), jnp.float32),
        "triple_weight": draw_triple_weight(jax.random.fold_in(key_of[14], 71), 0),
        "pair_bias": gaussian(key_of[7], (2, D), 0.3, 2.0, ((1, 4),), jnp.float32),
        "output_weight": gaussian(key_of[8], (D, D), (D // 64) ** -0.5, 1.75, ((0, 4), (1, 8))),
        "up_weight": gaussian(key_of[9], (D, FF), D ** -0.5, 0.21875, ((0, 8), (1, 4))),
        "up_bias": gaussian(key_of[10], (FF,), 0.3, 2.0, ((0, 4),), jnp.float32),
        "down_weight": gaussian(key_of[11], (FF, D), FF ** -0.5, 0.109375, ((0, 4), (1, 8))),
        "out_bias": gaussian(key_of[12], (D,), 0.3, 2.0, (), jnp.float32),
        "out_grad": noise_with(key_of[13], (TOKENS, D), 1.0, 6.0, ((0, 32),), (0, 1, 32, 2.75)),
    }


@jax.custom_vjp
def low(v):
    return lax.optimization_barrier(v.astype(jnp.bfloat16)).astype(jnp.float32)

@jax.custom_vjp
def low_back(v):
    return v

def low_keep(v):
    return (low(v), None)

def low_pass(kept, grad):
    return (grad,)

def back_keep(v):
    return (v, None)

def back_low(kept, grad):
    return (low(grad),)
low.defvjp(low_keep, low_pass)
low_back.defvjp(back_keep, back_low)
EPSILON = 1e-05

def matmul_high(left, right):
    return jnp.dot(left, right, precision=lax.Precision.HIGHEST, preferred_element_type=jnp.float32)

def normalize(values):
    row_mean = lax.optimization_barrier(jnp.mean(values, axis=-1, keepdims=True))
    centred = values - row_mean
    variance = lax.optimization_barrier(jnp.mean(centred * centred, axis=-1, keepdims=True))
    return centred * lax.rsqrt(variance + EPSILON)

def rotary_tables(positions):
    half_rot = ROT // 2
    inverse = 1.0 / 10000.0 ** (jnp.arange(half_rot, dtype=jnp.float32) * (2.0 / ROT))
    angles = positions.astype(jnp.float32)[:, None] * inverse[None, :]
    return (jnp.cos(angles), jnp.sin(angles))

def rotate(values, cosine_table, sine_table):
    half_rot = ROT // 2
    first_half = values[..., :half_rot]
    second_half = values[..., half_rot:ROT]
    cos_rows = cosine_table[:, None, :]
    sin_rows = sine_table[:, None, :]
    return jnp.concatenate([first_half * cos_rows - second_half * sin_rows, second_half * cos_rows + first_half * sin_rows, values[..., ROT:]], axis=-1)

def attention(queries, key_rows, value_rows, positions):
    block_rows = min(512, TOKENS)
    span_rows = block_rows + DOC_MOST
    scale_factor = 1.0 / math.sqrt(HD)
    padding = jnp.zeros((DOC_MOST, H, HD), jnp.float32)
    keys_ext = jnp.concatenate([padding, key_rows], axis=0)
    values_ext = jnp.concatenate([padding, value_rows], axis=0)
    row_steps = jnp.arange(block_rows, dtype=jnp.int32)
    col_steps = jnp.arange(span_rows, dtype=jnp.int32)

    def one_block(block_index):
        start_row = block_index * block_rows
        query_block = lax.dynamic_slice_in_dim(queries, start_row, block_rows, 0)
        key_block = lax.dynamic_slice_in_dim(keys_ext, start_row, span_rows, 0)
        value_block = lax.dynamic_slice_in_dim(values_ext, start_row, span_rows, 0)
        pos_block = lax.dynamic_slice_in_dim(positions, start_row, block_rows, 0)
        allowed = (col_steps[None, :] <= row_steps[:, None] + DOC_MOST) & (col_steps[None, :] >= (row_steps + DOC_MOST - pos_block)[:, None])
        raw_scores = jnp.einsum('qhd,khd->hqk', query_block, key_block, precision=lax.Precision.HIGHEST) * scale_factor
        scores = jnp.where(allowed[None], low_back(raw_scores), -1e+30)
        row_max = lax.optimization_barrier(jnp.max(scores, axis=-1, keepdims=True))
        weights = jnp.exp(scores - row_max)
        prob_low = low(weights / lax.optimization_barrier(jnp.sum(weights, axis=-1, keepdims=True)))
        mixture = jnp.einsum('hqk,khd->qhd', prob_low, value_block, precision=lax.Precision.HIGHEST)
        return mixture.reshape(block_rows, H * HD)
    blocks = lax.map(jax.checkpoint(one_block), jnp.arange(TOKENS // block_rows, dtype=jnp.int32))
    return blocks.reshape(TOKENS, H * HD)

def reference(hidden_in, positions, mixer_gain, mixer_shift, feed_gain, feed_shift, triple_weight, pair_bias, output_weight, up_weight, up_bias, down_weight, out_bias, out_grad):
    cosine_table, sine_table = rotary_tables(positions)

    def forward(residual, gain_one, shift_one, gain_two, shift_two, triple, pair_terms, output, upper, upper_bias, lower, final_bias):
        normed = normalize(residual)
        mixer_in = low(normed * gain_one + shift_one)
        feed_in = low(normed * gain_two + shift_two)
        projected = matmul_high(mixer_in, triple.reshape(D, 3 * D))
        queries = low_back(projected[:, :D] + pair_terms[0])
        key_rows = low_back(projected[:, D:2 * D])
        value_rows = low(low_back(projected[:, 2 * D:] + pair_terms[1]))
        queries = low(rotate(queries.reshape(TOKENS, H, HD), cosine_table, sine_table))
        key_rows = low(rotate(key_rows.reshape(TOKENS, H, HD), cosine_table, sine_table))
        attended = low(low_back(attention(queries, key_rows, value_rows.reshape(TOKENS, H, HD), positions)))
        hidden = low_back(matmul_high(feed_in, upper) + upper_bias)
        active = low(jax.nn.gelu(hidden, approximate=False))
        return residual + matmul_high(attended, output) + matmul_high(active, lower) + final_bias
    primals = (hidden_in.astype(jnp.float32), mixer_gain, mixer_shift, feed_gain, feed_shift, triple_weight.astype(jnp.float32), pair_bias, output_weight.astype(jnp.float32), up_weight.astype(jnp.float32), up_bias, down_weight.astype(jnp.float32), out_bias)
    result, pullback = jax.vjp(forward, *primals)
    grads = pullback(out_grad.astype(jnp.float32))
    return (result, grads[0], grads[1], grads[2], grads[3], grads[4], grads[5], grads[6], grads[7], grads[8], grads[9], grads[10], grads[11])
```

```python
import functools
import math

import jax
import jax.numpy as jnp
from jax import lax
from jax.experimental import pallas as pl
from jax.experimental.pallas import tpu as pltpu
from jax.sharding import PartitionSpec as P

HD = 64
ROT = 16
DOC_MOST = 2048
EPSILON = 1e-05
NEG = -1e30
TQ = 512
TK = 256
TR = 256
bf16 = jnp.bfloat16
f32 = jnp.float32
NN = (((1,), (0,)), ((), ()))
NT = (((1,), (1,)), ((), ()))
TN = (((0,), (0,)), ((), ()))
TT = (((0,), (1,)), ((), ()))
VMEM_LIMIT = 56 * 2**20


def mm(left, right, dims=NN):
    return lax.dot_general(left, right, dims, preferred_element_type=f32)


def swap(value, axis, mask):
    count = lax.axis_size(axis)
    return lax.ppermute(value, axis, [(i, i ^ mask) for i in range(count)])


def shift(value, axis, distance):
    count = lax.axis_size(axis)
    route = [(i, i + distance) for i in range(count) if 0 <= i + distance < count]
    return lax.ppermute(value, axis, route)


def bits_of(axis):
    return range(lax.axis_size(axis).bit_length() - 1)


def after(value, *others):
    return lax.optimization_barrier((value, *others))[0]


def gather_tensor(own):
    near = swap(own, "tensor", 1)
    far = swap(own, "tensor", 2)
    diagonal = swap(far, "tensor", 1)
    return jnp.concatenate([own, near, far, diagonal], axis=0)


def scatter_tensor(blocks, rows):
    back = jnp.concatenate([blocks[rows : 2 * rows], blocks[3 * rows :]], axis=0)
    near = swap(back, "tensor", 1).astype(f32)
    far = (blocks[2 * rows : 3 * rows].astype(f32) + near[rows:]).astype(bf16)
    mine = blocks[:rows].astype(f32) + near[:rows]
    return mine + swap(far, "tensor", 2).astype(f32)


def gather_dp(own):
    me = lax.axis_index("dp")
    rows, cols = own.shape
    held = own[None]
    for bit in reversed(bits_of("dp")):
        other = swap(held, "dp", 1 << bit)
        high = ((me >> bit) & 1) == 1
        held = jnp.stack([jnp.where(high, other, held), jnp.where(high, held, other)], axis=1)
        held = held.reshape(-1, rows, cols)
    return held.reshape(-1, cols)


def scatter_dp(whole, rows):
    me = lax.axis_index("dp")
    cols = whole.shape[1]
    held = whole.reshape(-1, rows, cols)
    for bit in bits_of("dp"):
        pairs = held.reshape(-1, 2, rows, cols)
        high = ((me >> bit) & 1) == 1
        send = jnp.where(high, pairs[:, 0], pairs[:, 1]).astype(bf16)
        keep = jnp.where(high, pairs[:, 1], pairs[:, 0]).astype(f32)
        held = keep + swap(send, "dp", 1 << bit).astype(f32)
    return held.reshape(rows, cols)


def sum_over(value, axis):
    for bit in bits_of(axis):
        value = value + swap(value, axis, 1 << bit)
    return value


def normalize(values):
    centred = values - jnp.mean(values, axis=-1, keepdims=True)
    inv_std = lax.rsqrt(jnp.mean(centred * centred, axis=-1, keepdims=True) + EPSILON)
    return (centred * inv_std, inv_std)


def pre_kernel(hid_ref, gains_ref, w_ref, bias_ref, cos_ref, sin_ref, mixer_ref, feed_ref, kv_ref, q_ref):
    heads = kv_ref.shape[0]
    normed, _ = normalize(hid_ref[...].astype(f32))
    mixer = (normed * gains_ref[0:1] + gains_ref[1:2]).astype(bf16)
    mixer_ref[...] = mixer
    feed_ref[...] = (normed * gains_ref[2:3] + gains_ref[3:4]).astype(bf16)
    width = bias_ref.shape[1]
    proj = mm(mixer, w_ref[:, :width]) + bias_ref[...]
    cos, sin = cos_ref[...], sin_ref[...]
    ones = jnp.ones((128 - ROT, TR), f32)
    cos_rows = jnp.concatenate([cos, cos, ones], axis=0).T
    sin_rows = jnp.concatenate([-sin, sin, ones * 0.0], axis=0).T
    lane = lax.broadcasted_iota(jnp.int32, (TR, 128), 1)

    def rotate(x):
        partner = jnp.where(lane < ROT // 2, pltpu.roll(x, 128 - ROT // 2, 1), pltpu.roll(x, ROT // 2, 1))
        return x * cos_rows + partner * sin_rows

    for h in range(heads):
        kv_ref[h] = rotate(proj[:, h * 128 : (h + 1) * 128]).astype(bf16)
        at = heads * 128 + (h // 2) * 128
        x = proj[:, at : at + 128]
        if h % 2:
            x = pltpu.roll(x, HD, 1)
        x = jnp.where(lane < HD, rotate(x) * (1.0 / math.sqrt(HD)), 0.0)
        q_ref[h] = x.astype(bf16)


def rows_spec(cols):
    return pl.BlockSpec((TR, cols), lambda i: (i, 0))


def whole_spec(shape):
    return pl.BlockSpec(shape, lambda i: (0,) * len(shape))


def heads_spec(heads):
    return pl.BlockSpec((heads, TR, 128), lambda i: (0, i, 0))


def pre(hid, gains, w, bias, cos, sin, heads):
    T, D = hid.shape
    return pl.pallas_call(
        pre_kernel,
        grid=(T // TR,),
        in_specs=[
            rows_spec(D),
            whole_spec(gains.shape),
            whole_spec(w.shape),
            whole_spec(bias.shape),
            pl.BlockSpec((8, TR), lambda i: (0, i)),
            pl.BlockSpec((8, TR), lambda i: (0, i)),
        ],
        out_specs=[rows_spec(D), rows_spec(D), heads_spec(heads), heads_spec(heads)],
        out_shape=[
            jax.ShapeDtypeStruct((T, D), bf16),
            jax.ShapeDtypeStruct((T, D), bf16),
            jax.ShapeDtypeStruct((heads, T, 128), bf16),
            jax.ShapeDtypeStruct((heads, T, 128), bf16),
        ],
        compiler_params=pltpu.CompilerParams(vmem_limit_bytes=VMEM_LIMIT),
        cost_estimate=pl.CostEstimate(flops=2 * T * D * 640, bytes_accessed=T * D * 10, transcendentals=T),
        name="pre",
    )(hid, gains, w, bias, cos, sin)


def gelu_parts(h):
    mag = jnp.abs(h) * (1.0 / math.sqrt(2.0))
    t = 1.0 / (1.0 + 0.3275911 * mag)
    poly = t * (0.254829592 + t * (-0.284496736 + t * (1.421413741 + t * (-1.453152027 + t * 1.061405429))))
    bell = jnp.exp(-0.5 * h * h)
    tail = 0.5 * poly * bell
    return (jnp.where(h >= 0, 1.0 - tail, tail), bell * (1.0 / math.sqrt(2.0 * math.pi)))


def ffn_kernel(hid_ref, feed_ref, g_ref, gain_ref, wu_ref, wd_ref, wo_ref, bias_ref,
               act_ref, hg_ref, branch_ref, back_ref, do_ref, sums_ref, hsum_ref):
    heads = do_ref.shape[0]
    g = g_ref[...]
    hidden = mm(feed_ref[...], wu_ref[...]) + bias_ref[...]
    cumulative, density = gelu_parts(hidden)
    act = (hidden * cumulative).astype(bf16)
    act_ref[...] = act
    hg = (mm(g, wd_ref[...]) * (cumulative + hidden * density)).astype(bf16)
    hg_ref[...] = hg
    branch_ref[...] = mm(act, wd_ref[...], NT).astype(bf16)
    back = mm(hg, wu_ref[...], NT)
    back_ref[...] = (back * gain_ref[...]).astype(bf16)
    normed, _ = normalize(hid_ref[...].astype(f32))

    @pl.when(pl.program_id(0) == 0)
    def _():
        sums_ref[...] = jnp.zeros_like(sums_ref)
        hsum_ref[...] = jnp.zeros_like(hsum_ref)

    sums_ref[0:1] += jnp.sum(back * normed, axis=0, keepdims=True)
    sums_ref[1:2] += jnp.sum(back, axis=0, keepdims=True)
    hsum_ref[...] += jnp.sum(hg.astype(f32), axis=0, keepdims=True)
    do = mm(g, wo_ref[...])
    do = jnp.concatenate([do, jnp.zeros((TR, 128), f32)], axis=1)
    lane = lax.broadcasted_iota(jnp.int32, (TR, 128), 1)
    for h in range(heads):
        at = (h // 2) * 128
        x = do[:, at : at + 128]
        if h % 2 == 0:
            x = pltpu.roll(x, HD, 1)
        do_ref[h] = jnp.where(lane < HD, 0.0, x).astype(bf16)


def ffn(hid, feed, g, gain, wu, wd, wo, bias, heads):
    T, D = hid.shape
    F = wu.shape[1]
    return pl.pallas_call(
        ffn_kernel,
        grid=(T // TR,),
        in_specs=[
            rows_spec(D), rows_spec(D), rows_spec(D),
            whole_spec(gain.shape), whole_spec(wu.shape), whole_spec(wd.shape), whole_spec(wo.shape), whole_spec(bias.shape),
        ],
        out_specs=[rows_spec(F), rows_spec(F), rows_spec(D), rows_spec(D), heads_spec(heads), whole_spec((2, D)), whole_spec((1, F))],
        out_shape=[
            jax.ShapeDtypeStruct((T, F), bf16),
            jax.ShapeDtypeStruct((T, F), bf16),
            jax.ShapeDtypeStruct((T, D), bf16),
            jax.ShapeDtypeStruct((T, D), bf16),
            jax.ShapeDtypeStruct((heads, T, 128), bf16),
            jax.ShapeDtypeStruct((2, D), f32),
            jax.ShapeDtypeStruct((1, F), f32),
        ],
        compiler_params=pltpu.CompilerParams(vmem_limit_bytes=VMEM_LIMIT),
        cost_estimate=pl.CostEstimate(flops=2 * T * D * F * 4, bytes_accessed=T * D * 14, transcendentals=T * F * 2),
        name="ffn",
    )(hid, feed, g, gain, wu, wd, wo, bias)


def attn_kernel(place_ref, first_ref, start_ref, tail_ref, kv_ref, q_ref, do_ref, cos_ref, sin_ref,
                o_ref, dq_ref, dtail_ref, dkv_ref, s_scr, dp_scr, kvt_scr, dkv_scr, o_acc, dq_acc, *, T, blk):
    t = place_ref[0]

    def place(row):
        return row ^ (t * blk)

    dkv_scr[...] = jnp.zeros_like(dkv_scr)
    lowest = first_ref[0]

    def load(ki, c):
        r = pl.multiple_of(ki * TK, TK)
        at = pl.multiple_of(place(r & (T - 1)), TK)

        @pl.when(ki < T // TK)
        def _():
            kvt_scr[:, pl.ds(r, TK)] = tail_ref[0, pl.ds(at, TK), :].T

        @pl.when(ki >= T // TK)
        def _():
            kvt_scr[:, pl.ds(r, TK)] = kv_ref[0, pl.ds(at, TK), :].T

        return c

    lax.fori_loop(lowest, 2 * T // TK, load, 0)

    def rows_of(ki):
        at = pl.multiple_of(place((ki * TK) & (T - 1)), TK)
        return jnp.where(ki < T // TK, tail_ref[0, pl.ds(at, TK), :], kv_ref[0, pl.ds(at, TK), :])

    def q_tile(qi, c):
        q0 = pl.multiple_of(qi * TQ, TQ)
        qr = pl.multiple_of(place(q0), TQ)
        qd = jnp.concatenate([q_ref[0, pl.ds(qr, TQ), :], do_ref[0, pl.ds(qr, TQ), :]], axis=0)
        start = start_ref[:, pl.ds(qr, TQ)]
        qidx = q0 + T + lax.broadcasted_iota(jnp.int32, (1, TQ), 1)
        first = first_ref[qi]
        stop = (q0 + T) // TK + TQ // TK

        def pass1(ki, st):
            m8, l8, d8 = st
            sdp = mm(rows_of(ki), qd, NT)
            j = ki * TK + lax.broadcasted_iota(jnp.int32, (TK, TQ), 0)
            s = jnp.where((j >= start) & (j <= qidx), sdp[:, :TQ], NEG)
            dp = sdp[:, TQ:]
            slot = ki - first
            s_scr[slot] = s
            dp_scr[slot] = dp
            s3 = s.reshape(TK // 8, 8, TQ)
            m_new = jnp.maximum(m8, jnp.max(s3, axis=0))
            alpha = jnp.exp(m8 - m_new)
            e = jnp.exp(s3 - m_new[None])
            l8 = l8 * alpha + jnp.sum(e, axis=0)
            d8 = d8 * alpha + jnp.sum(e * dp.reshape(TK // 8, 8, TQ), axis=0)
            return (m_new, l8, d8)

        z8 = jnp.zeros((8, TQ), f32)
        m8, l8, d8 = lax.fori_loop(first, stop, pass1, (jnp.full((8, TQ), NEG, f32), z8, z8))
        m = jnp.max(m8, axis=0, keepdims=True)
        w = jnp.exp(m8 - m)
        total = jnp.sum(l8 * w, axis=0, keepdims=True)
        lse = m + jnp.log(total)
        delta = jnp.sum(d8 * w, axis=0, keepdims=True) / total
        o_acc[...] = jnp.zeros_like(o_acc)
        dq_acc[...] = jnp.zeros_like(dq_acc)

        def pass2(ki, c2):
            slot = ki - first
            p = jnp.exp(s_scr[slot] - lse)
            ds = (p * (dp_scr[slot] - delta)).astype(bf16)
            p = p.astype(bf16)
            r = pl.multiple_of(ki * TK, TK)
            dkv_scr[pl.ds(r, TK), :] += mm(jnp.concatenate([ds, p], axis=1), qd)
            kvt = kvt_scr[:, pl.ds(r, TK)]
            dq_acc[...] += mm(kvt[:HD], ds)
            o_acc[...] += mm(kvt[HD:], p)
            return c2

        lax.fori_loop(first, stop, pass2, 0)
        o_ref[0, :, pl.ds(qr, TQ)] = o_acc[...].astype(bf16)
        dq = dq_acc[...] * (1.0 / math.sqrt(HD))
        cos = cos_ref[:, pl.ds(qr, TQ)]
        sin = sin_ref[:, pl.ds(qr, TQ)]
        a, b = dq[: ROT // 2], dq[ROT // 2 : ROT]
        dq = jnp.concatenate([a * cos + b * sin, b * cos - a * sin, dq[ROT:]], axis=0)
        dq_ref[0, :, pl.ds(qr, TQ)] = dq.astype(bf16)
        return c

    lax.fori_loop(0, T // TQ, q_tile, 0)

    def store(i, c):
        r = pl.multiple_of(i * TQ, TQ)
        at = pl.multiple_of(place(r), TQ)
        dtail_ref[0, pl.ds(at, TQ), :] = dkv_scr[pl.ds(r, TQ), :].astype(bf16)
        dkv_ref[0, pl.ds(at, TQ), :] = dkv_scr[pl.ds(T + r, TQ), :]
        return c

    lax.fori_loop(0, T // TQ, store, 0)


def attention(place, first, start, tail, kv, q, do, cos, sin, blk):
    heads, T, _ = q.shape
    head_spec = pl.BlockSpec((1, T, 128), lambda h, *_: (h, 0, 0))
    flat_spec = pl.BlockSpec((8, T), lambda h, *_: (0, 0))
    back_spec = pl.BlockSpec((1, HD, T), lambda h, *_: (h, 0, 0))
    slots = DOC_MOST // TK + TQ // TK
    return pl.pallas_call(
        functools.partial(attn_kernel, T=T, blk=blk),
        grid_spec=pltpu.PrefetchScalarGridSpec(
            num_scalar_prefetch=2,
            grid=(heads,),
            in_specs=[pl.BlockSpec((1, T), lambda h, *_: (0, 0)), head_spec, head_spec, head_spec, head_spec, flat_spec, flat_spec],
            out_specs=[back_spec, back_spec, head_spec, head_spec],
            scratch_shapes=[
                pltpu.VMEM((slots, TK, TQ), f32),
                pltpu.VMEM((slots, TK, TQ), f32),
                pltpu.VMEM((128, 2 * T), bf16),
                pltpu.VMEM((2 * T, 128), f32),
                pltpu.VMEM((HD, TQ), f32),
                pltpu.VMEM((HD, TQ), f32),
            ],
        ),
        out_shape=[
            jax.ShapeDtypeStruct((heads, HD, T), bf16),
            jax.ShapeDtypeStruct((heads, HD, T), bf16),
            jax.ShapeDtypeStruct((heads, T, 128), bf16),
            jax.ShapeDtypeStruct((heads, T, 128), f32),
        ],
        compiler_params=pltpu.CompilerParams(vmem_limit_bytes=VMEM_LIMIT),
        cost_estimate=pl.CostEstimate(
            flops=heads * T * T * HD * 20, bytes_accessed=heads * T * 128 * 20, transcendentals=heads * T * T
        ),
        name="attn",
    )(place, first, start, tail, kv, q, do, cos, sin)


def shards(
    hidden_in, positions, mixer_gain, mixer_shift, feed_gain, feed_shift, triple_weight,
    pair_bias, output_weight, up_weight, up_bias, down_weight, out_bias, out_grad,
):
    T = positions.shape[0]
    blk, D = hidden_in.shape
    W = pair_bias.shape[1]
    heads = W // HD
    chunk = triple_weight.shape[0]
    t = lax.axis_index("tensor").astype(jnp.int32)

    q_w, k_w, v_w = (triple_weight[:, i].reshape(chunk, heads, HD) for i in range(3))
    kv_w = jnp.concatenate([k_w, v_w], axis=2).reshape(chunk, 2 * W)
    mix_own = jnp.concatenate([kv_w, q_w.reshape(chunk, W), output_weight.T], axis=1)
    mix_w = gather_dp(mix_own)
    hid = gather_tensor(hidden_in)
    g = gather_tensor(after(out_grad, hid))
    mix_w, up_own = lax.optimization_barrier((mix_w, up_weight))
    ffn_w = gather_dp(jnp.concatenate([up_own, down_weight.T], axis=1))
    F = up_weight.shape[1]
    up_w, down_w = ffn_w[:, :F], ffn_w[:, F:]
    out_w = mix_w[:, 3 * W :]

    pos = jnp.concatenate([lax.dynamic_slice(positions, ((r ^ t) * blk,), (blk,)) for r in range(T // blk)])
    inverse = 1.0 / 10000.0 ** (jnp.arange(ROT // 2, dtype=f32) * (2.0 / ROT))
    angles = pos.astype(f32)[None, :] * inverse[:, None]
    cos, sin = jnp.cos(angles), jnp.sin(angles)
    rows = jnp.arange(T, dtype=jnp.int32) ^ (t * blk)
    start = (rows + T - pos)[None]
    q_starts = jnp.arange(0, T, TQ, dtype=jnp.int32)
    first = (q_starts + T - positions[::TQ]) // TK

    gains = jnp.stack([mixer_gain, mixer_shift, feed_gain, feed_shift])
    v_bias = pair_bias[1].reshape(heads, HD)
    kv_bias = jnp.concatenate([jnp.zeros_like(v_bias), v_bias], axis=1).reshape(2 * W)
    pad = (-W) % 128
    bias = jnp.concatenate([kv_bias, pair_bias[0], jnp.zeros((pad,), f32)])[None]
    mixer_in, feed_in, kv, q = pre(hid, gains, mix_w, bias, cos, sin, heads)
    tail = shift(kv, "dp", 1)
    act, hg, branch, back, do, feed_sums, hg_sum = ffn(
        hid, feed_in, g, feed_gain[None], up_w, down_w, out_w, up_bias[None], heads
    )
    grad_up = mm(feed_in, hg, TN)
    grad_down = mm(g, act, TN)
    ffn_grads = scatter_dp(jnp.concatenate([grad_up, grad_down], axis=1).astype(bf16), chunk)
    o, dq, dtail, dkv = attention(t[None], first, start, tail, kv, q, do, cos, sin, blk)
    ahead = shift(dtail, "dp", -1)
    o = o.reshape(W, T)
    branch = (branch.astype(f32) + mm(o, out_w, TT)).astype(bf16)
    summed = scatter_tensor(branch, blk)
    result = hidden_in.astype(f32) + summed + out_bias
    dkv = dkv + ahead.astype(f32)
    a, b = dkv[..., : ROT // 2], dkv[..., ROT // 2 : ROT]
    cos_t, sin_t = cos.T[None], sin.T[None]
    dkv = jnp.concatenate([a * cos_t + b * sin_t, b * cos_t - a * sin_t, dkv[..., ROT:]], axis=-1).astype(bf16)
    dkv = jnp.transpose(dkv, (1, 0, 2)).reshape(T, 2 * W)
    dq = dq.reshape(W, T)
    part = mm(dkv, mix_w[:, : 2 * W], NT) + mm(dq, mix_w[:, 2 * W : 3 * W], TT)
    normed_all, _ = normalize(hid.astype(f32))
    mixer_sums = jnp.stack([jnp.sum(part * normed_all, axis=0), jnp.sum(part, axis=0)])
    grad_hat = (part * mixer_gain + back.astype(f32)).astype(bf16)
    grad_hat = scatter_tensor(grad_hat, blk)
    normed, inv_std = normalize(hidden_in.astype(f32))
    first_mean = jnp.mean(grad_hat, axis=-1, keepdims=True)
    second_mean = jnp.mean(grad_hat * normed, axis=-1, keepdims=True)
    grad_hidden = out_grad.astype(f32) + inv_std * (grad_hat - first_mean - normed * second_mean)
    mix_grad = jnp.concatenate(
        [mm(mixer_in, dkv, TN), lax.dot_general(mixer_in, dq, TT, preferred_element_type=f32),
         lax.dot_general(g, o, TT, preferred_element_type=f32)], axis=1
    )
    mix_grads = scatter_dp(mix_grad.astype(bf16), chunk)
    q_sum = jnp.sum(dq, axis=1, dtype=f32)
    v_sum = jnp.sum(dkv, axis=0, dtype=f32).reshape(heads, 2, HD)[:, 1].reshape(W)
    flat = jnp.concatenate(
        [q_sum, v_sum, hg_sum[0], mixer_sums.reshape(-1), feed_sums.reshape(-1), jnp.sum(out_grad, axis=0, dtype=f32)]
    )
    flat = jnp.pad(flat, (0, (-flat.shape[0]) % 1024)).reshape(-1, 128)
    flat = sum_over(flat, "dp").reshape(-1)
    pair_grad = flat[: 2 * W].reshape(2, W)
    up_bias_grad = flat[2 * W : 2 * W + F]
    at = 2 * W + F
    norm_sums = sum_over(flat[at : at + 5 * D].reshape(5, D), "tensor")
    kv_grad = mix_grads[:, : 2 * W].reshape(chunk, heads, 2, HD)
    triple_grad = jnp.stack(
        [mix_grads[:, 2 * W : 3 * W], kv_grad[:, :, 0].reshape(chunk, W), kv_grad[:, :, 1].reshape(chunk, W)], axis=1
    )
    return (
        result,
        grad_hidden,
        norm_sums[0],
        norm_sums[1],
        norm_sums[2],
        norm_sums[3],
        triple_grad,
        pair_grad,
        mix_grads[:, 3 * W :].T,
        ffn_grads[:, :F],
        up_bias_grad,
        ffn_grads[:, F:].T,
        norm_sums[4],
    )


def solution(mesh):
    rows = P(("dp", "tensor"), None)
    in_specs = (
        rows, P("dp"), P(), P(), P(), P(), P("dp", None, "tensor"), P(None, "tensor"), P("tensor", "dp"),
        P("dp", "tensor"), P("tensor"), P("tensor", "dp"), P(), rows,
    )
    out_specs = (
        rows, rows, P(), P(), P(), P(), P("dp", None, "tensor"), P(None, "tensor"), P("tensor", "dp"),
        P("dp", "tensor"), P("tensor"), P("tensor", "dp"), P(),
    )
    return jax.shard_map(shards, mesh=mesh, in_specs=in_specs, out_specs=out_specs, check_vma=False)
```

```python
import functools
import math

import jax
import jax.numpy as jnp
from jax import lax
from jax.experimental import pallas as pl
from jax.experimental.pallas import tpu as pltpu
from jax.sharding import PartitionSpec as P

HD = 64
ROT = 16
DOC_MOST = 2048
EPSILON = 1e-05
NEG = -1e30
TQ = 256
TK = 256
NK = 2
TR = 512
FR = 512
PR = 512
bf16 = jnp.bfloat16
f32 = jnp.float32
NN = (((1,), (0,)), ((), ()))
NT = (((1,), (1,)), ((), ()))
TN = (((0,), (0,)), ((), ()))
TT = (((0,), (1,)), ((), ()))
VMEM_LIMIT = 56 * 2**20
COST = pl.CostEstimate(flops=1000, bytes_accessed=1000, transcendentals=0)


def mm(left, right, dims=NN):
    return lax.dot_general(left, right, dims, preferred_element_type=f32)


def swap(value, axis, mask):
    count = lax.axis_size(axis)
    return lax.ppermute(value, axis, [(i, i ^ mask) for i in range(count)])


def shift(value, axis, distance):
    count = lax.axis_size(axis)
    route = [(i, i + distance) for i in range(count) if 0 <= i + distance < count]
    return lax.ppermute(value, axis, route)


def bit_count(axis):
    return lax.axis_size(axis).bit_length() - 1


def after(value, *others):
    return lax.optimization_barrier((value, *others))[0]


def gather_tensor(own):
    near = swap(own, "tensor", 1)
    far = swap(own, "tensor", 2)
    diagonal = swap(far, "tensor", 1)
    return [own, near, far, diagonal]


def scatter_core(blocks, rows):
    back = jnp.concatenate([blocks[rows : 2 * rows], blocks[3 * rows :]], axis=0)
    near = swap(back, "tensor", 1).astype(f32)
    far = (blocks[2 * rows : 3 * rows].astype(f32) + near[rows:]).astype(bf16)
    return blocks[:rows].astype(f32) + near[:rows], far


def split(held, rows, left, bit):
    above = 1 << sum(b > bit for b in left)
    return held.reshape(above, 2, -1, held.shape[-1])


def gather_dp(own, order, gates=()):
    me = lax.axis_index("dp")
    rows, cols = own.shape
    held, done = own, []
    parts = []
    for n, bit in enumerate(order):
        if n == 0 and gates and gates[0] is not None:
            held = after(held, gates[0])
        other = swap(held, "dp", 1 << bit)
        if n + 1 < len(gates) and gates[n + 1] is not None:
            other = after(other, gates[n + 1])
        high = ((me >> bit) & 1) == 1
        above = 1 << sum(b > bit for b in done)
        one, two = held.reshape(above, -1, cols), other.reshape(above, -1, cols)
        held = jnp.stack([jnp.where(high, two, one), jnp.where(high, one, two)], axis=1).reshape(-1, cols)
        done.append(bit)
        parts.append(held)
    return held, parts


def two_parts(sums):
    first = lax.reduce_precision(sums, 8, 7)
    return first, lax.reduce_precision(sums - first, 8, 7)


def scatter_dp(whole, rows, order, gates=(), sums=None):
    me = lax.axis_index("dp")
    cols = whole.shape[1]
    left = sorted(order, reverse=True)
    held = whole
    parts = []
    for n, bit in enumerate(order):
        pairs = split(held, rows, left, bit)
        high = ((me >> bit) & 1) == 1
        send = jnp.where(high, pairs[:, 0], pairs[:, 1]).astype(bf16).reshape(-1, cols)
        keep = jnp.where(high, pairs[:, 1], pairs[:, 0]).astype(f32).reshape(-1, cols)
        count = send.shape[0]
        if sums is not None:
            first, second = two_parts(sums)
            send = jnp.concatenate([send, first.astype(bf16), second.astype(bf16)], axis=0)
        if n < len(gates) and gates[n] is not None:
            send = after(send, gates[n])
        other = swap(send, "dp", 1 << bit).astype(f32)
        held = keep + other[:count]
        if sums is not None:
            sums = (first + second) + (other[count : count + 8] + other[count + 8 :])
        left.remove(bit)
        parts.append(held)
    return held, parts, sums


def sum_over(value, axis):
    for bit in range(bit_count(axis)):
        value = value + swap(value, axis, 1 << bit)
    return value


def normalize(values):
    centred = values - jnp.mean(values, axis=-1, keepdims=True)
    inv_std = lax.rsqrt(jnp.mean(centred * centred, axis=-1, keepdims=True) + EPSILON)
    return (centred * inv_std, inv_std)


def rows_spec(cols, tile=TR):
    return pl.BlockSpec((tile, cols), lambda i: (i, 0))


def whole_spec(shape):
    return pl.BlockSpec(shape, lambda i: (0,) * len(shape))


def heads_spec(heads, cols=128, tile=TR):
    return pl.BlockSpec((heads, tile, cols), lambda i: (0, i, 0))


def piece_specs(count, rows, cols, tile=TR):
    per = rows // tile
    return [pl.BlockSpec((tile, cols), lambda i, p=p: (jnp.clip(i - p * per, 0, per - 1), 0)) for p in range(count)]


def pick(refs, rows):
    at = pl.program_id(0) // (rows // refs[0].shape[0])
    value = refs[0][...]
    for n, ref in enumerate(refs[1:]):
        value = jnp.where(at == n + 1, ref[...], value)
    return value


def rotation_rows(cos, sin):
    ones = jnp.ones((128 - ROT, cos.shape[1]), f32)
    return jnp.concatenate([cos, cos, ones], axis=0).T, jnp.concatenate([-sin, sin, ones * 0.0], axis=0).T


def rotate(x, cos_rows, sin_rows):
    lane = lax.broadcasted_iota(jnp.int32, x.shape, 1)
    partner = jnp.where(lane < ROT // 2, pltpu.roll(x, 128 - ROT // 2, 1), pltpu.roll(x, ROT // 2, 1))
    return x * cos_rows + partner * sin_rows


def pre_kernel(*refs, pieces, blk):
    hids, refs = refs[:pieces], refs[pieces:]
    gains_ref, w_ref, bias_ref, cos_ref, sin_ref, mixer_ref, kv_ref, q_ref = refs
    heads = kv_ref.shape[0]
    normed, _ = normalize(pick(hids, blk).astype(f32))
    mixer = (normed * gains_ref[0:1] + gains_ref[1:2]).astype(bf16)
    mixer_ref[...] = mixer
    proj = mm(mixer, w_ref[...]) + bias_ref[...]
    cos_rows, sin_rows = rotation_rows(cos_ref[...], sin_ref[...])
    lane = lax.broadcasted_iota(jnp.int32, (TR, 128), 1)
    for h in range(heads):
        kv_ref[h] = rotate(proj[:, h * 128 : (h + 1) * 128], cos_rows, sin_rows).astype(bf16)
        at = heads * 128 + (h // 2) * 128
        x = proj[:, at : at + 128]
        if h % 2:
            x = pltpu.roll(x, HD, 1)
        x = jnp.where(lane < HD, rotate(x, cos_rows, sin_rows) * (1.0 / math.sqrt(HD)), 0.0)
        q_ref[h] = x.astype(bf16)


def pre(hids, gains, w, bias, cos, sin, heads):
    blk, D = hids[0].shape
    T = blk * len(hids)
    return pl.pallas_call(
        functools.partial(pre_kernel, pieces=len(hids), blk=blk),
        grid=(T // TR,),
        in_specs=piece_specs(len(hids), blk, D) + [
            whole_spec(gains.shape),
            whole_spec(w.shape),
            whole_spec(bias.shape),
            pl.BlockSpec((8, TR), lambda i: (0, i)),
            pl.BlockSpec((8, TR), lambda i: (0, i)),
        ],
        out_specs=[rows_spec(D)] + [heads_spec(heads)] * 2,
        out_shape=[jax.ShapeDtypeStruct((T, D), bf16)] + [jax.ShapeDtypeStruct((heads, T, 128), bf16)] * 2,
        compiler_params=pltpu.CompilerParams(vmem_limit_bytes=VMEM_LIMIT),
        cost_estimate=COST,
        name="pre",
    )(*hids, gains, w, bias, cos, sin)


def gelu_parts(h):
    mag = jnp.abs(h) * (1.0 / math.sqrt(2.0))
    t = 1.0 / (1.0 + 0.3275911 * mag)
    poly = t * (0.254829592 + t * (-0.284496736 + t * (1.421413741 + t * (-1.453152027 + t * 1.061405429))))
    bell = jnp.exp(-0.5 * h * h)
    tail = 0.5 * poly * bell
    return (jnp.where(h >= 0, 1.0 - tail, tail), bell * (1.0 / math.sqrt(2.0 * math.pi)))


def ffn_kernel(*refs, pieces, blk):
    hids, gs, refs = refs[:pieces], refs[pieces : 2 * pieces], refs[2 * pieces :]
    gains_ref, w_ref, bias_ref, normed_ref, g_ref, branch_ref, back_ref, do_ref, grad_ref, sums_ref, acc_ref = refs
    heads = do_ref.shape[0]
    F = bias_ref.shape[1]
    step = pl.program_id(0)
    normed, _ = normalize(pick(hids, blk).astype(f32))
    normed_ref[...] = normed.astype(bf16)
    feed = (normed * gains_ref[0:1] + gains_ref[1:2]).astype(bf16)
    g = pick(gs, blk)
    g_ref[...] = g
    up, down = w_ref[:, :F], w_ref[:, F : 2 * F]
    hidden = mm(feed, up) + bias_ref[...]
    cumulative, density = gelu_parts(hidden)
    act = (hidden * cumulative).astype(bf16)
    hg = (mm(g, down) * (cumulative + hidden * density)).astype(bf16)
    branch_ref[...] = mm(act, down, NT).astype(bf16)
    back = mm(hg, up, NT)
    back_ref[...] = (back * gains_ref[0:1]).astype(bf16)

    @pl.when(step == 0)
    def _():
        sums_ref[...] = jnp.zeros_like(sums_ref)
        acc_ref[...] = jnp.zeros_like(acc_ref)

    acc_ref[:, :F] += mm(feed, hg, TN)
    acc_ref[:, F:] += mm(g, act, TN)
    sums_ref[3:4] += jnp.sum(back * normed, axis=0, keepdims=True)
    sums_ref[4:5] += jnp.sum(back, axis=0, keepdims=True)
    sums_ref[5:6] += jnp.sum(hg.astype(f32), axis=0, keepdims=True)

    @pl.when(step < blk // FR)
    def _():
        sums_ref[6:7] += jnp.sum(g.astype(f32), axis=0, keepdims=True)

    @pl.when(step == pl.num_programs(0) - 1)
    def _():
        grad_ref[...] = acc_ref[...].astype(bf16)

    do = mm(g, w_ref[:, 2 * F :])
    lane = lax.broadcasted_iota(jnp.int32, (FR, 128), 1)
    for h in range(heads):
        at = (h // 2) * 128
        x = do[:, at : at + 128]
        if h % 2 == 0:
            x = pltpu.roll(x, HD, 1)
        do_ref[h] = jnp.where(lane < HD, 0.0, x).astype(bf16)


def ffn(hids, gs, gains, w, bias, heads):
    blk, D = gs[0].shape
    T = blk * len(gs)
    F = bias.shape[1]
    rows = rows_spec(D, FR)
    return pl.pallas_call(
        functools.partial(ffn_kernel, pieces=len(gs), blk=blk),
        grid=(T // FR,),
        in_specs=piece_specs(len(gs), blk, D, FR) * 2 + [whole_spec(gains.shape), whole_spec(w.shape), whole_spec(bias.shape)],
        out_specs=[rows] * 4 + [heads_spec(heads, 128, FR), whole_spec((D, 2 * F)), whole_spec((8, D))],
        out_shape=[jax.ShapeDtypeStruct((T, D), bf16)] * 4
        + [
            jax.ShapeDtypeStruct((heads, T, 128), bf16),
            jax.ShapeDtypeStruct((D, 2 * F), bf16),
            jax.ShapeDtypeStruct((8, D), f32),
        ],
        scratch_shapes=[pltpu.VMEM((D, 2 * F), f32)],
        compiler_params=pltpu.CompilerParams(vmem_limit_bytes=VMEM_LIMIT),
        cost_estimate=COST,
        name="ffn",
    )(*hids, *gs, gains, w, bias)


def attn_kernel(*refs, T, blk, heads, late):
    if late:
        (place_ref, first_ref, start_ref, tail_ref, kv_ref, q_ref, do_ref, cos_ref, sin_ref, carry_ref, o_in, dq_in,
         o_ref, dq_ref, dtail_ref, low_ref, high_ref, *refs) = refs
    else:
        (place_ref, first_ref, start_ref, tail_ref, kv_ref, q_ref, do_ref, cos_ref, sin_ref,
         o_ref, dq_ref, dtail_ref, carry_ref, *refs) = refs
    kv_scr, dkv_scr, s_scr, dp_scr, o_acc, dq_acc, qd_scr = refs
    half = T // 2
    base = half if late else 0
    t = place_ref[0]
    inner = (t & 1) * blk
    H = range(heads)

    def half_at(n):
        return pl.ds(pl.multiple_of((n ^ (t >> 1)) * half, half), half)

    for n, (ref, part) in enumerate([(tail_ref, 1), (kv_ref, 0), (kv_ref, 1)] if late else [(tail_ref, 0), (tail_ref, 1), (kv_ref, 0)]):
        kv_scr[:, n * half : (n + 1) * half] = ref[:, half_at(part), :]
    if late:
        dkv_scr[:, :T] = carry_ref[...]
        dkv_scr[:, T:] = jnp.zeros_like(dkv_scr[:, T:])
        o_ref[:, half_at(0)] = o_in[...]
        dq_ref[:, half_at(0)] = dq_in[...]
    else:
        dkv_scr[...] = jnp.zeros_like(dkv_scr)

    def place(row):
        return (row - base) ^ inner

    def q_tile(qi, c):
        q0 = pl.multiple_of(base + qi * TQ, TQ)
        qr = pl.multiple_of(q0 ^ (t * blk), TQ)
        out = qr if late else pl.multiple_of(place(q0), TQ)
        for h in H:
            qd_scr[h, :TQ] = q_ref[h, pl.ds(qr, TQ), :]
            qd_scr[h, TQ:] = do_ref[h, pl.ds(qr, TQ), :]
        start = start_ref[:, pl.ds(qr, TQ)]
        qidx = q0 + T + lax.broadcasted_iota(jnp.int32, (1, TQ), 1)
        first = first_ref[base // TQ + qi]
        stop = (q0 + T) // TK + TQ // TK
        count = stop - first

        def over(body, init):
            pairs = count // NK
            state = lax.fori_loop(0, pairs, lambda i, c: body(first + i * NK, c, NK), init)
            return lax.fori_loop(first + pairs * NK, stop, lambda i, c: body(i, c, 1), state)

        def pass1(ki, state, nk):
            rows = nk * TK
            slot = ki - first
            j = ki * TK + lax.broadcasted_iota(jnp.int32, (rows, TQ), 0)
            ok = (j >= start) & (j <= qidx)
            ats = [pl.multiple_of(place((ki + n) * TK), TK) for n in range(nk)]
            sdps = [mm(jnp.concatenate([kv_scr[h, pl.ds(at, TK), :] for at in ats], axis=0), qd_scr[h], NT) for h in H]
            stats = []
            for h in H:
                m8, l8, d8 = state[3 * h : 3 * h + 3]
                s = jnp.where(ok, sdps[h][:, :TQ], NEG)
                dp = sdps[h][:, TQ:]
                for n in range(nk):
                    s_scr[slot + n, h] = s[n * TK : (n + 1) * TK]
                    dp_scr[slot + n, h] = dp[n * TK : (n + 1) * TK]
                s3 = s.reshape(rows // 8, 8, TQ)
                m_new = jnp.maximum(m8, jnp.max(s3, axis=0))
                alpha = jnp.exp(m8 - m_new)
                e = jnp.exp(s3 - m_new[None])
                l8 = l8 * alpha + jnp.sum(e, axis=0)
                d8 = d8 * alpha + jnp.sum(e * dp.reshape(rows // 8, 8, TQ), axis=0)
                stats += [m_new, l8, d8]
            return tuple(stats)

        z8 = jnp.zeros((8, TQ), f32)
        state = over(pass1, (jnp.full((8, TQ), NEG, f32), z8, z8) * heads)
        lses, deltas = [], []
        for h in H:
            m8, l8, d8 = state[3 * h : 3 * h + 3]
            m = jnp.max(m8, axis=0, keepdims=True)
            w = jnp.exp(m8 - m)
            total = jnp.sum(l8 * w, axis=0, keepdims=True)
            lses.append(m + jnp.log(total))
            deltas.append(jnp.sum(d8 * w, axis=0, keepdims=True) / total)
        o_acc[...] = jnp.zeros_like(o_acc)
        dq_acc[...] = jnp.zeros_like(dq_acc)

        def pass2(ki, c2, nk):
            slot = ki - first
            ats = [pl.multiple_of(place((ki + n) * TK), TK) for n in range(nk)]
            for h in H:
                dq = dq_acc[h]
                o = o_acc[h]
                for n in range(nk):
                    p = jnp.exp(s_scr[slot + n, h] - lses[h])
                    ds = (p * (dp_scr[slot + n, h] - deltas[h])).astype(bf16)
                    p = p.astype(bf16)
                    dkv_scr[h, pl.ds(ats[n], TK), :] += mm(jnp.concatenate([ds, p], axis=1), qd_scr[h])
                    kvt = kv_scr[h, pl.ds(ats[n], TK), :].T
                    dq += mm(kvt[:HD], ds)
                    o += mm(kvt[HD:], p)
                dq_acc[h] = dq
                o_acc[h] = o
            return c2

        over(pass2, 0)
        cos = cos_ref[:, pl.ds(qr, TQ)]
        sin = sin_ref[:, pl.ds(qr, TQ)]
        for h in H:
            o_ref[h * HD : (h + 1) * HD, pl.ds(out, TQ)] = o_acc[h].astype(bf16)
            dq = dq_acc[h] * (1.0 / math.sqrt(HD))
            a, b = dq[: ROT // 2], dq[ROT // 2 : ROT]
            dq = jnp.concatenate([a * cos + b * sin, b * cos - a * sin, dq[ROT:]], axis=0)
            dq_ref[h * HD : (h + 1) * HD, pl.ds(out, TQ)] = dq.astype(bf16)
        return c

    lax.fori_loop(0, half // TQ, q_tile, 0)
    dtail_ref[...] = dkv_scr[:, :half].astype(bf16)
    if late:
        low_ref[...] = dkv_scr[:, half:T]
        high_ref[...] = dkv_scr[:, T:]
    else:
        carry_ref[...] = dkv_scr[:, half:]


def attention(place, first, start, tail, kv, q, do, cos, sin, blk, early=()):
    heads, T, _ = q.shape
    W = heads * HD
    late = len(early) > 0
    vmem = pl.BlockSpec(memory_space=pltpu.VMEM)
    smem = pl.BlockSpec(memory_space=pltpu.SMEM)
    slots = DOC_MOST // TK + TQ // TK
    span = T if late else T // 2
    outs = [((W, span), bf16), ((W, span), bf16), ((heads, T // 2, 128), bf16)]
    outs += [((heads, T // 2, 128), f32)] * 2 if late else [((heads, T, 128), f32)]
    return pl.pallas_call(
        functools.partial(attn_kernel, T=T, blk=blk, heads=heads, late=late),
        in_specs=[smem, smem] + [vmem] * (7 + len(early)),
        out_specs=[vmem] * len(outs),
        scratch_shapes=[
            pltpu.VMEM((heads, T + T // 2, 128), bf16),
            pltpu.VMEM((heads, T + T // 2, 128), f32),
            pltpu.VMEM((slots, heads, TK, TQ), f32),
            pltpu.VMEM((slots, heads, TK, TQ), f32),
            pltpu.VMEM((heads, HD, TQ), f32),
            pltpu.VMEM((heads, HD, TQ), f32),
            pltpu.VMEM((heads, 2 * TQ, 128), bf16),
        ],
        out_shape=[jax.ShapeDtypeStruct(*out) for out in outs],
        compiler_params=pltpu.CompilerParams(vmem_limit_bytes=VMEM_LIMIT),
        cost_estimate=COST,
        name="attn",
    )(place, first, start, tail, kv, q, do, cos, sin, *early)


def mid_kernel(o_ref, dq_ref, mixer_ref, g_ref, branch_ref, w_ref, out_ref, grad_ref, acc_ref):
    W = o_ref.shape[0]
    step = pl.program_id(0)
    o = o_ref[...]
    rows = o.astype(f32).T.astype(bf16)
    out_ref[...] = (mm(rows, w_ref[:, :W], NT) + branch_ref[...].astype(f32)).astype(bf16)

    @pl.when(step == 0)
    def _():
        acc_ref[...] = jnp.zeros_like(acc_ref)

    acc_ref[:W] += mm(dq_ref[...], mixer_ref[...])
    acc_ref[W:] += mm(o, g_ref[...])

    @pl.when(step == pl.num_programs(0) - 1)
    def _():
        grad_ref[...] = acc_ref[...].T.astype(bf16)


def mid(o, dq, mixer, g, branch, w):
    T, D = mixer.shape
    W = o.shape[0]
    cols = pl.BlockSpec((W, TR), lambda i: (0, i))
    return pl.pallas_call(
        mid_kernel,
        grid=(T // TR,),
        in_specs=[cols, cols, rows_spec(D), rows_spec(D), rows_spec(D), whole_spec(w.shape)],
        out_specs=[rows_spec(D), whole_spec((D, 2 * W))],
        out_shape=[jax.ShapeDtypeStruct((T, D), bf16), jax.ShapeDtypeStruct((D, 2 * W), bf16)],
        scratch_shapes=[pltpu.VMEM((2 * W, D), f32)],
        compiler_params=pltpu.CompilerParams(vmem_limit_bytes=VMEM_LIMIT),
        cost_estimate=COST,
        name="mid",
    )(o, dq, mixer, g, branch, w)


def post_kernel(place_ref, dkv_ref, ahead_ref, dq_ref, cos_ref, sin_ref, normed_ref, mixer_ref, back_ref, gain_ref, w_ref, *refs):
    heads = dkv_ref.shape[0]
    W = heads * HD
    step = pl.program_id(0)
    if len(refs) == 8:
        _, acc_in, sums_in, mid_ref, *refs = refs
    else:
        acc_in = mid_ref = None
        sums_in, *refs = refs
    hat_ref, grad_ref, sums_ref, acc_ref = refs

    @pl.when(step == 0)
    def _():
        sums_ref[...] = sums_in[...]
        acc_ref[...] = jnp.zeros_like(acc_ref) if acc_in is None else acc_in[...]

    cos_rows, sin_rows = rotation_rows(cos_ref[...], sin_ref[...])
    kv = jnp.concatenate(
        [rotate(dkv_ref[h] + ahead_ref[h].astype(f32), cos_rows, -sin_rows).astype(bf16) for h in range(heads)], axis=1
    )
    acc_ref[...] += mm(mixer_ref[...], kv, TN)
    dq = dq_ref[...].astype(f32).T.astype(bf16)
    part = mm(kv, w_ref[:, : 2 * W], NT) + mm(dq, w_ref[:, 2 * W : 3 * W], NT)
    hat_ref[...] = (part * gain_ref[...] + back_ref[...].astype(f32)).astype(bf16)
    sums_ref[0:1] += jnp.sum(part * normed_ref[...].astype(f32), axis=0, keepdims=True)
    sums_ref[1:2] += jnp.sum(part, axis=0, keepdims=True)
    sums_ref[2:3, : 2 * W] += jnp.sum(kv.astype(f32), axis=0, keepdims=True)
    sums_ref[2:3, 2 * W : 3 * W] += jnp.sum(dq.astype(f32), axis=0, keepdims=True)

    @pl.when(step == pl.num_programs(0) - 1)
    def _():
        grad_ref[:, : 2 * W] = acc_ref[...].astype(grad_ref.dtype)
        if mid_ref is not None:
            grad_ref[:, 2 * W :] = mid_ref[...]


def post(part, place, dkv, ahead, dq, cos, sin, normed, mixer, back, gain, w, early=()):
    T, D = mixer.shape
    heads = dkv.shape[0]
    W = heads * HD
    per = T // 2 // PR

    def at(i, place):
        return (part ^ (place[0] >> 1)) * per + i

    def inner(i, place):
        return i

    def rows(index):
        return pl.BlockSpec((PR, D), lambda i, place: (index(i, place), 0))

    def cols(count):
        return pl.BlockSpec((count, PR), lambda i, place: (0, at(i, place)))

    def fixed(shape):
        return pl.BlockSpec(shape, lambda i, place: (0,) * len(shape))

    half = pl.BlockSpec((heads, PR, 128), lambda i, place: (0, i, 0))
    late = len(early) > 1
    specs = [half, half, cols(W), cols(8), cols(8), rows(at), rows(at), rows(at), fixed(gain.shape), fixed(w.shape)]
    if late:
        specs += [pl.BlockSpec(memory_space=pl.ANY), fixed((D, 2 * W)), fixed((8, D)), fixed((D, 2 * W))]
    else:
        specs += [fixed((8, D))]
    return pl.pallas_call(
        post_kernel,
        grid_spec=pltpu.PrefetchScalarGridSpec(
            num_scalar_prefetch=1,
            grid=(per,),
            in_specs=specs,
            out_specs=[rows(at), fixed((D, (4 if late else 2) * W)), fixed((8, D))],
            scratch_shapes=[pltpu.VMEM((D, 2 * W), f32)],
        ),
        out_shape=[
            jax.ShapeDtypeStruct((T, D), bf16),
            jax.ShapeDtypeStruct((D, 4 * W), bf16) if late else jax.ShapeDtypeStruct((D, 2 * W), f32),
            jax.ShapeDtypeStruct((8, D), f32),
        ],
        input_output_aliases={11: 0} if late else {},
        compiler_params=pltpu.CompilerParams(vmem_limit_bytes=VMEM_LIMIT),
        cost_estimate=COST,
        name="post",
    )(place, dkv, ahead, dq, cos, sin, normed, mixer, back, gain, w, *early)


def shards(
    hidden_in, positions, mixer_gain, mixer_shift, feed_gain, feed_shift, triple_weight,
    pair_bias, output_weight, up_weight, up_bias, down_weight, out_bias, out_grad,
):
    T = positions.shape[0]
    blk, D = hidden_in.shape
    W = pair_bias.shape[1]
    heads = W // HD
    chunk = triple_weight.shape[0]
    t = lax.axis_index("tensor").astype(jnp.int32)

    F = up_weight.shape[1]
    bits = bit_count("dp")
    down_order = list(reversed(range(bits)))
    mixed_order = down_order[:-2] + [0, 1]
    q_w, k_w, v_w = (triple_weight[:, i].reshape(chunk, heads, HD) for i in range(3))
    kv_w = jnp.concatenate([k_w, v_w], axis=2).reshape(chunk, 2 * W)
    pad = (-W) % 128
    no_cols = jnp.zeros((chunk, pad), bf16)
    qkv_w, qkv_parts = gather_dp(jnp.concatenate([kv_w, q_w.reshape(chunk, W), no_cols], axis=1), down_order)
    hids = gather_tensor(hidden_in)
    gs = gather_tensor(after(out_grad, hids[2]))

    pos = jnp.concatenate([lax.dynamic_slice(positions, ((r ^ t) * blk,), (blk,)) for r in range(T // blk)])
    inverse = 1.0 / 10000.0 ** (jnp.arange(ROT // 2, dtype=f32) * (2.0 / ROT))
    angles = pos.astype(f32)[None, :] * inverse[:, None]
    cos, sin = jnp.cos(angles), jnp.sin(angles)
    rows = jnp.arange(T, dtype=jnp.int32) ^ (t * blk)
    start = (rows + T - pos)[None]
    q_starts = jnp.arange(0, T, TQ, dtype=jnp.int32)
    first = (q_starts + T - positions[::TQ]) // TK

    gains = jnp.stack([mixer_gain, mixer_shift, feed_gain, feed_shift])
    v_bias = pair_bias[1].reshape(heads, HD)
    kv_bias = jnp.concatenate([jnp.zeros_like(v_bias), v_bias], axis=1).reshape(2 * W)
    bias = jnp.concatenate([kv_bias, pair_bias[0], jnp.zeros((pad,), f32)])[None]
    mixer_in, kv, q = pre(hids, gains, qkv_w, bias, cos, sin, heads)
    tail = shift(kv, "dp", 1)
    ffn_own = jnp.concatenate([up_weight, down_weight.T, output_weight.T, no_cols], axis=1)
    ffn_w, _ = gather_dp(ffn_own, mixed_order, [qkv_parts[-2]] + [qkv_w] * (bits - 2) + [kv])
    normed, g, branch, back, do, ffn_grad, ffn_sums = ffn(hids, gs, gains[2:], ffn_w, up_bias[None], heads)
    spots = t[None]
    attn_args = (spots, first, start, tail, kv, q, do, cos, sin, blk)
    *early, dtail_low, carry = attention(*attn_args)
    ahead_low = shift(dtail_low, "dp", -1)
    o, dq, dtail_high, dkv_low, dkv_high = attention(*attn_args, early=(carry, *early))
    ahead_high = shift(dtail_high, "dp", -1)
    post_args = (dq, cos, sin, normed, mixer_in, back, mixer_gain[None], qkv_w)
    early = post(0, spots, dkv_low, ahead_low, *post_args, early=(ffn_sums,))
    ffn_order = mixed_order[::-1]
    branch, mid_grad = mid(after(o, early[2]), dq, mixer_in, g, branch, ffn_w[:, 2 * F :])
    branch_own, branch_far = scatter_core(branch, blk)
    ffn_grads, ffn_parts, _ = scatter_dp(ffn_grad, chunk, ffn_order, [tail, branch])
    ahead_high = after(ahead_high, branch_far)
    hat, mix_grad, sums = post(1, spots, dkv_high, ahead_high, *post_args, early=(*early, mid_grad))
    hat_own, hat_far = scatter_core(hat, blk)
    summed = branch_own + swap(branch_far, "tensor", 2).astype(f32)
    result = hidden_in.astype(f32) + summed + out_bias
    hat_far = after(hat_far, summed)
    grad_hat = hat_own + swap(hat_far, "tensor", 2).astype(f32)
    mix_grads, _, sums = scatter_dp(mix_grad, chunk, down_order[::-1], [ffn_parts[1], hat_far, grad_hat], sums)
    own, inv_std = normalize(hidden_in.astype(f32))
    first_mean = jnp.mean(grad_hat, axis=-1, keepdims=True)
    second_mean = jnp.mean(grad_hat * own, axis=-1, keepdims=True)
    grad_hidden = out_grad.astype(f32) + inv_std * (grad_hat - first_mean - own * second_mean)
    norm_sums = sum_over(sums, "tensor")
    head_sums = sums[2, : 2 * W].reshape(heads, 2, HD)[:, 1].reshape(W)
    pair_grad = jnp.stack([sums[2, 2 * W : 3 * W], head_sums])
    kv_grads = mix_grads[:, : 2 * W].reshape(chunk, heads, 2, HD)
    triple_grad = jnp.stack(
        [mix_grads[:, 2 * W : 3 * W], kv_grads[:, :, 0].reshape(chunk, W), kv_grads[:, :, 1].reshape(chunk, W)], axis=1
    )
    return (
        result,
        grad_hidden,
        norm_sums[0],
        norm_sums[1],
        norm_sums[3],
        norm_sums[4],
        triple_grad,
        pair_grad,
        mix_grads[:, 3 * W :].T,
        ffn_grads[:, :F],
        sums[5],
        ffn_grads[:, F:].T,
        norm_sums[6],
    )


def solution(mesh):
    rows = P(("dp", "tensor"), None)
    in_specs = (
        rows, P("dp"), P(), P(), P(), P(), P("dp", None, "tensor"), P(None, "tensor"), P("tensor", "dp"),
        P("dp", "tensor"), P("tensor"), P("tensor", "dp"), P(), rows,
    )
    out_specs = (
        rows, rows, P(), P(), P(), P(), P("dp", None, "tensor"), P(None, "tensor"), P("tensor", "dp"),
        P("dp", "tensor"), P("tensor"), P("tensor", "dp"), P(),
    )
    return jax.shard_map(shards, mesh=mesh, in_specs=in_specs, out_specs=out_specs, check_vma=False)
```

```python
import functools
import math

import jax
import jax.numpy as jnp
from jax import lax
from jax.experimental import pallas as pl
from jax.experimental.pallas import tpu as pltpu
from jax.sharding import PartitionSpec as P

HD = 64
ROT = 16
DOC_MOST = 2048
EPSILON = 1e-05
NEG = -1e30
TQ = 256
TK = 256
NK = 2
TR = 512
FR = 512
PR = 512
bf16 = jnp.bfloat16
f32 = jnp.float32
NN = (((1,), (0,)), ((), ()))
NT = (((1,), (1,)), ((), ()))
TN = (((0,), (0,)), ((), ()))
TT = (((0,), (1,)), ((), ()))
VMEM_LIMIT = 56 * 2**20


def cost(us):
    return pl.CostEstimate(flops=int(us * 1.15e9), bytes_accessed=1000, transcendentals=0)


def mm(left, right, dims=NN):
    return lax.dot_general(left, right, dims, preferred_element_type=f32)


def swap(value, axis, mask):
    count = lax.axis_size(axis)
    return lax.ppermute(value, axis, [(i, i ^ mask) for i in range(count)])


def shift(value, axis, distance):
    count = lax.axis_size(axis)
    route = [(i, i + distance) for i in range(count) if 0 <= i + distance < count]
    return lax.ppermute(value, axis, route)


def bit_count(axis):
    return lax.axis_size(axis).bit_length() - 1


def after(value, *others):
    return lax.optimization_barrier((value, others))[0]


def gather_tensor(own):
    near = swap(own, "tensor", 1)
    far = swap(own, "tensor", 2)
    diagonal = swap(far, "tensor", 1)
    return [own, near, far, diagonal]


def scatter_core(blocks, rows):
    back = jnp.concatenate([blocks[rows : 2 * rows], blocks[3 * rows :]], axis=0)
    near = swap(back, "tensor", 1).astype(f32)
    far = (blocks[2 * rows : 3 * rows].astype(f32) + near[rows:]).astype(bf16)
    return blocks[:rows].astype(f32) + near[:rows], far


def split(held, rows, left, bit):
    above = 1 << sum(b > bit for b in left)
    return held.reshape(above, 2, -1, held.shape[-1])


def gather_dp(own, order, gates=()):
    me = lax.axis_index("dp")
    rows, cols = own.shape
    held, done = own, []
    parts = []
    for n, bit in enumerate(order):
        if n == 0 and gates and gates[0] is not None:
            held = after(held, gates[0])
        other = swap(held, "dp", 1 << bit)
        if n + 1 < len(gates) and gates[n + 1] is not None:
            other = after(other, gates[n + 1])
        high = ((me >> bit) & 1) == 1
        above = 1 << sum(b > bit for b in done)
        one, two = held.reshape(above, -1, cols), other.reshape(above, -1, cols)
        held = jnp.stack([jnp.where(high, two, one), jnp.where(high, one, two)], axis=1).reshape(-1, cols)
        done.append(bit)
        parts.append(held)
    return held, parts


def two_parts(sums):
    first = lax.reduce_precision(sums, 8, 7)
    return first, lax.reduce_precision(sums - first, 8, 7)


def scatter_step(held, rows, left, bit, gate=None, landed=None, sums=None):
    cols = held.shape[1]
    pairs = split(held, rows, left, bit)
    high = ((lax.axis_index("dp") >> bit) & 1) == 1
    send = jnp.where(high, pairs[:, 0], pairs[:, 1]).astype(bf16).reshape(-1, cols)
    keep = jnp.where(high, pairs[:, 1], pairs[:, 0]).astype(f32).reshape(-1, cols)
    count = send.shape[0]
    if sums is not None:
        first, second = two_parts(sums)
        send = jnp.concatenate([send, first.astype(bf16), second.astype(bf16)], axis=0)
    if gate is not None:
        send = after(send, gate)
    other = swap(send, "dp", 1 << bit)
    if landed is not None:
        other = after(other, landed)
    other = other.astype(f32)
    held = keep + other[:count]
    if sums is None:
        return held
    return held, (first + second) + (other[count : count + 8] + other[count + 8 :])


def sum_over(value, axis):
    for bit in range(bit_count(axis)):
        value = value + swap(value, axis, 1 << bit)
    return value


def normalize(values):
    centred = values - jnp.mean(values, axis=-1, keepdims=True)
    inv_std = lax.rsqrt(jnp.mean(centred * centred, axis=-1, keepdims=True) + EPSILON)
    return (centred * inv_std, inv_std)


def rows_spec(cols, tile=TR):
    return pl.BlockSpec((tile, cols), lambda i: (i, 0))


def whole_spec(shape):
    return pl.BlockSpec(shape, lambda i: (0,) * len(shape))


def heads_spec(heads, cols=128, tile=TR):
    return pl.BlockSpec((heads, tile, cols), lambda i: (0, i, 0))


def piece_specs(count, rows, cols, tile=TR):
    per = rows // tile
    return [pl.BlockSpec((tile, cols), lambda i, p=p: (jnp.clip(i - p * per, 0, per - 1), 0)) for p in range(count)]


def pick(refs, rows):
    at = pl.program_id(0) // (rows // refs[0].shape[0])
    value = refs[0][...]
    for n, ref in enumerate(refs[1:]):
        value = jnp.where(at == n + 1, ref[...], value)
    return value


def rotation_rows(cos, sin):
    ones = jnp.ones((128 - ROT, cos.shape[1]), f32)
    return jnp.concatenate([cos, cos, ones], axis=0).T, jnp.concatenate([-sin, sin, ones * 0.0], axis=0).T


def rotate(x, cos_rows, sin_rows):
    lane = lax.broadcasted_iota(jnp.int32, x.shape, 1)
    partner = jnp.where(lane < ROT // 2, pltpu.roll(x, 128 - ROT // 2, 1), pltpu.roll(x, ROT // 2, 1))
    return x * cos_rows + partner * sin_rows


def pre_kernel(*refs, pieces, blk):
    hids, refs = refs[:pieces], refs[pieces:]
    gains_ref, w_ref, bias_ref, cos_ref, sin_ref, mixer_ref, kv_ref, q_ref = refs
    heads = kv_ref.shape[0]
    normed, _ = normalize(pick(hids, blk).astype(f32))
    mixer = (normed * gains_ref[0:1] + gains_ref[1:2]).astype(bf16)
    mixer_ref[...] = mixer
    proj = mm(mixer, w_ref[...]) + bias_ref[...]
    cos_rows, sin_rows = rotation_rows(cos_ref[...], sin_ref[...])
    lane = lax.broadcasted_iota(jnp.int32, (TR, 128), 1)
    for h in range(heads):
        kv_ref[h] = rotate(proj[:, h * 128 : (h + 1) * 128], cos_rows, sin_rows).astype(bf16)
        at = heads * 128 + (h // 2) * 128
        x = proj[:, at : at + 128]
        if h % 2:
            x = pltpu.roll(x, HD, 1)
        x = jnp.where(lane < HD, rotate(x, cos_rows, sin_rows) * (1.0 / math.sqrt(HD)), 0.0)
        q_ref[h] = x.astype(bf16)


def pre(hids, gains, w, bias, cos, sin, heads):
    blk, D = hids[0].shape
    T = blk * len(hids)
    return pl.pallas_call(
        functools.partial(pre_kernel, pieces=len(hids), blk=blk),
        grid=(T // TR,),
        in_specs=piece_specs(len(hids), blk, D) + [
            whole_spec(gains.shape),
            whole_spec(w.shape),
            whole_spec(bias.shape),
            pl.BlockSpec((8, TR), lambda i: (0, i)),
            pl.BlockSpec((8, TR), lambda i: (0, i)),
        ],
        out_specs=[rows_spec(D)] + [heads_spec(heads)] * 2,
        out_shape=[jax.ShapeDtypeStruct((T, D), bf16)] + [jax.ShapeDtypeStruct((heads, T, 128), bf16)] * 2,
        compiler_params=pltpu.CompilerParams(vmem_limit_bytes=VMEM_LIMIT),
        cost_estimate=cost(0.5),
        name="pre",
    )(*hids, gains, w, bias, cos, sin)


def gelu_parts(h):
    mag = jnp.abs(h) * (1.0 / math.sqrt(2.0))
    t = 1.0 / (1.0 + 0.3275911 * mag)
    poly = t * (0.254829592 + t * (-0.284496736 + t * (1.421413741 + t * (-1.453152027 + t * 1.061405429))))
    bell = jnp.exp(-0.5 * h * h)
    tail = 0.5 * poly * bell
    return (jnp.where(h >= 0, 1.0 - tail, tail), bell * (1.0 / math.sqrt(2.0 * math.pi)))


def ffn_kernel(*refs, pieces, blk):
    hids, gs, refs = refs[:pieces], refs[pieces : 2 * pieces], refs[2 * pieces :]
    gains_ref, up_ref, down_ref, bias_ref, normed_ref, g_ref, branch_ref, back_ref, do_ref, grad_ref, sums_ref, acc_ref = refs
    heads = do_ref.shape[0]
    F = bias_ref.shape[1]
    step = pl.program_id(0)
    normed, _ = normalize(pick(hids, blk).astype(f32))
    normed_ref[...] = normed.astype(bf16)
    feed = (normed * gains_ref[0:1] + gains_ref[1:2]).astype(bf16)
    g = pick(gs, blk)
    g_ref[...] = g
    up, down = up_ref[...], down_ref[:, :F]
    hidden = mm(feed, up) + bias_ref[...]
    cumulative, density = gelu_parts(hidden)
    act = (hidden * cumulative).astype(bf16)
    hg = (mm(g, down) * (cumulative + hidden * density)).astype(bf16)
    branch_ref[...] = mm(act, down, NT).astype(bf16)
    back = mm(hg, up, NT)
    back_ref[...] = (back * gains_ref[0:1]).astype(bf16)

    @pl.when(step == 0)
    def _():
        sums_ref[...] = jnp.zeros_like(sums_ref)
        acc_ref[...] = jnp.zeros_like(acc_ref)

    acc_ref[:, :F] += mm(feed, hg, TN)
    acc_ref[:, F:] += mm(g, act, TN)
    sums_ref[3:4] += jnp.sum(back * normed, axis=0, keepdims=True)
    sums_ref[4:5] += jnp.sum(back, axis=0, keepdims=True)
    sums_ref[5:6] += jnp.sum(hg.astype(f32), axis=0, keepdims=True)

    @pl.when(step < blk // FR)
    def _():
        sums_ref[6:7] += jnp.sum(g.astype(f32), axis=0, keepdims=True)

    @pl.when(step == pl.num_programs(0) - 1)
    def _():
        grad_ref[...] = acc_ref[...].astype(bf16)

    do = mm(g, down_ref[:, F:])
    lane = lax.broadcasted_iota(jnp.int32, (FR, 128), 1)
    for h in range(heads):
        at = (h // 2) * 128
        x = do[:, at : at + 128]
        if h % 2 == 0:
            x = pltpu.roll(x, HD, 1)
        do_ref[h] = jnp.where(lane < HD, 0.0, x).astype(bf16)


def ffn(hids, gs, gains, up, down, bias, heads):
    blk, D = gs[0].shape
    T = blk * len(gs)
    F = bias.shape[1]
    rows = rows_spec(D, FR)
    return pl.pallas_call(
        functools.partial(ffn_kernel, pieces=len(gs), blk=blk),
        grid=(T // FR,),
        in_specs=piece_specs(len(gs), blk, D, FR) * 2
        + [whole_spec(array.shape) for array in (gains, up, down, bias)],
        out_specs=[rows] * 4 + [heads_spec(heads, 128, FR), whole_spec((D, 2 * F)), whole_spec((8, D))],
        out_shape=[jax.ShapeDtypeStruct((T, D), bf16)] * 4
        + [
            jax.ShapeDtypeStruct((heads, T, 128), bf16),
            jax.ShapeDtypeStruct((D, 2 * F), bf16),
            jax.ShapeDtypeStruct((8, D), f32),
        ],
        scratch_shapes=[pltpu.VMEM((D, 2 * F), f32)],
        compiler_params=pltpu.CompilerParams(vmem_limit_bytes=VMEM_LIMIT),
        cost_estimate=cost(0.5),
        name="ffn",
    )(*hids, *gs, gains, up, down, bias)


def attn_kernel(*refs, T, blk, heads, late):
    if late:
        (place_ref, first_ref, start_ref, tail_ref, kv_ref, q_ref, do_ref, cos_ref, sin_ref, carry_ref, o_in, dq_in,
         o_ref, dq_ref, dtail_ref, low_ref, high_ref, *refs) = refs
    else:
        (place_ref, first_ref, start_ref, tail_ref, kv_ref, q_ref, do_ref, cos_ref, sin_ref,
         o_ref, dq_ref, dtail_ref, carry_ref, *refs) = refs
    kv_scr, dkv_scr, s_scr, dp_scr, o_acc, dq_acc, qd_scr = refs
    half = T // 2
    base = half if late else 0
    t = place_ref[0]
    inner = (t & 1) * blk
    H = range(heads)

    def half_at(n):
        return pl.ds(pl.multiple_of((n ^ (t >> 1)) * half, half), half)

    for n, (ref, part) in enumerate([(tail_ref, 1), (kv_ref, 0), (kv_ref, 1)] if late else [(tail_ref, 0), (tail_ref, 1), (kv_ref, 0)]):
        kv_scr[:, n * half : (n + 1) * half] = ref[:, half_at(part), :]
    if late:
        dkv_scr[:, :T] = carry_ref[...]
        dkv_scr[:, T:] = jnp.zeros_like(dkv_scr[:, T:])
        o_ref[:, half_at(0)] = o_in[...]
        dq_ref[:, half_at(0)] = dq_in[...]
    else:
        dkv_scr[...] = jnp.zeros_like(dkv_scr)

    def place(row):
        return (row - base) ^ inner

    def q_tile(qi, c):
        q0 = pl.multiple_of(base + qi * TQ, TQ)
        qr = pl.multiple_of(q0 ^ (t * blk), TQ)
        out = qr if late else pl.multiple_of(place(q0), TQ)
        for h in H:
            qd_scr[h, :TQ] = q_ref[h, pl.ds(qr, TQ), :]
            qd_scr[h, TQ:] = do_ref[h, pl.ds(qr, TQ), :]
        start = start_ref[:, pl.ds(qr, TQ)]
        qidx = q0 + T + lax.broadcasted_iota(jnp.int32, (1, TQ), 1)
        first = first_ref[base // TQ + qi]
        stop = (q0 + T) // TK + TQ // TK
        count = stop - first

        def over(body, init):
            pairs = count // NK
            state = lax.fori_loop(0, pairs, lambda i, c: body(first + i * NK, c, NK), init)
            return lax.fori_loop(first + pairs * NK, stop, lambda i, c: body(i, c, 1), state)

        def pass1(ki, state, nk):
            rows = nk * TK
            slot = ki - first
            j = ki * TK + lax.broadcasted_iota(jnp.int32, (rows, TQ), 0)
            ok = (j >= start) & (j <= qidx)
            ats = [pl.multiple_of(place((ki + n) * TK), TK) for n in range(nk)]
            sdps = [mm(jnp.concatenate([kv_scr[h, pl.ds(at, TK), :] for at in ats], axis=0), qd_scr[h], NT) for h in H]
            stats = []
            for h in H:
                m8, l8, d8 = state[3 * h : 3 * h + 3]
                s = jnp.where(ok, sdps[h][:, :TQ], NEG)
                dp = sdps[h][:, TQ:]
                for n in range(nk):
                    s_scr[slot + n, h] = s[n * TK : (n + 1) * TK]
                    dp_scr[slot + n, h] = dp[n * TK : (n + 1) * TK]
                s3 = s.reshape(rows // 8, 8, TQ)
                m_new = jnp.maximum(m8, jnp.max(s3, axis=0))
                alpha = jnp.exp(m8 - m_new)
                e = jnp.exp(s3 - m_new[None])
                l8 = l8 * alpha + jnp.sum(e, axis=0)
                d8 = d8 * alpha + jnp.sum(e * dp.reshape(rows // 8, 8, TQ), axis=0)
                stats += [m_new, l8, d8]
            return tuple(stats)

        z8 = jnp.zeros((8, TQ), f32)
        state = over(pass1, (jnp.full((8, TQ), NEG, f32), z8, z8) * heads)
        lses, deltas = [], []
        for h in H:
            m8, l8, d8 = state[3 * h : 3 * h + 3]
            m = jnp.max(m8, axis=0, keepdims=True)
            w = jnp.exp(m8 - m)
            total = jnp.sum(l8 * w, axis=0, keepdims=True)
            lses.append(m + jnp.log(total))
            deltas.append(jnp.sum(d8 * w, axis=0, keepdims=True) / total)
        o_acc[...] = jnp.zeros_like(o_acc)
        dq_acc[...] = jnp.zeros_like(dq_acc)

        def pass2(ki, c2, nk):
            slot = ki - first
            ats = [pl.multiple_of(place((ki + n) * TK), TK) for n in range(nk)]
            for h in H:
                dq = dq_acc[h]
                o = o_acc[h]
                for n in range(nk):
                    p = jnp.exp(s_scr[slot + n, h] - lses[h])
                    ds = (p * (dp_scr[slot + n, h] - deltas[h])).astype(bf16)
                    p = p.astype(bf16)
                    dkv_scr[h, pl.ds(ats[n], TK), :] += mm(jnp.concatenate([ds, p], axis=1), qd_scr[h])
                    kvt = kv_scr[h, pl.ds(ats[n], TK), :].T
                    dq += mm(kvt[:HD], ds)
                    o += mm(kvt[HD:], p)
                dq_acc[h] = dq
                o_acc[h] = o
            return c2

        over(pass2, 0)
        cos = cos_ref[:, pl.ds(qr, TQ)]
        sin = sin_ref[:, pl.ds(qr, TQ)]
        for h in H:
            o_ref[h * HD : (h + 1) * HD, pl.ds(out, TQ)] = o_acc[h].astype(bf16)
            dq = dq_acc[h] * (1.0 / math.sqrt(HD))
            a, b = dq[: ROT // 2], dq[ROT // 2 : ROT]
            dq = jnp.concatenate([a * cos + b * sin, b * cos - a * sin, dq[ROT:]], axis=0)
            dq_ref[h * HD : (h + 1) * HD, pl.ds(out, TQ)] = dq.astype(bf16)
        return c

    lax.fori_loop(0, half // TQ, q_tile, 0)
    dtail_ref[...] = dkv_scr[:, :half].astype(bf16)
    if late:
        low_ref[...] = dkv_scr[:, half:T]
        high_ref[...] = dkv_scr[:, T:]
    else:
        carry_ref[...] = dkv_scr[:, half:]


def attention(place, first, start, tail, kv, q, do, cos, sin, blk, early=()):
    heads, T, _ = q.shape
    W = heads * HD
    late = len(early) > 0
    vmem = pl.BlockSpec(memory_space=pltpu.VMEM)
    smem = pl.BlockSpec(memory_space=pltpu.SMEM)
    slots = DOC_MOST // TK + TQ // TK
    span = T if late else T // 2
    outs = [((W, span), bf16), ((W, span), bf16), ((heads, T // 2, 128), bf16)]
    outs += [((heads, T // 2, 128), f32)] * 2 if late else [((heads, T, 128), f32)]
    return pl.pallas_call(
        functools.partial(attn_kernel, T=T, blk=blk, heads=heads, late=late),
        in_specs=[smem, smem] + [vmem] * (7 + len(early)),
        out_specs=[vmem] * len(outs),
        scratch_shapes=[
            pltpu.VMEM((heads, T + T // 2, 128), bf16),
            pltpu.VMEM((heads, T + T // 2, 128), f32),
            pltpu.VMEM((slots, heads, TK, TQ), f32),
            pltpu.VMEM((slots, heads, TK, TQ), f32),
            pltpu.VMEM((heads, HD, TQ), f32),
            pltpu.VMEM((heads, HD, TQ), f32),
            pltpu.VMEM((heads, 2 * TQ, 128), bf16),
        ],
        out_shape=[jax.ShapeDtypeStruct(*out) for out in outs],
        compiler_params=pltpu.CompilerParams(vmem_limit_bytes=40 * 2**20),
        cost_estimate=cost(0.1),
        name="attn",
    )(place, first, start, tail, kv, q, do, cos, sin, *early)


def mid_kernel(o_ref, dq_ref, mixer_ref, g_ref, branch_ref, w_ref, out_ref, grad_ref, acc_ref):
    W = o_ref.shape[0]
    step = pl.program_id(0)
    o = o_ref[...]
    rows = o.astype(f32).T.astype(bf16)
    out_ref[...] = (mm(rows, w_ref[:, :W], NT) + branch_ref[...].astype(f32)).astype(bf16)

    @pl.when(step == 0)
    def _():
        acc_ref[...] = jnp.zeros_like(acc_ref)

    acc_ref[:W] += mm(dq_ref[...], mixer_ref[...])
    acc_ref[W:] += mm(o, g_ref[...])

    @pl.when(step == pl.num_programs(0) - 1)
    def _():
        grad_ref[...] = acc_ref[...].T.astype(bf16)


def mid(o, dq, mixer, g, branch, w):
    T, D = mixer.shape
    W = o.shape[0]
    cols = pl.BlockSpec((W, TR), lambda i: (0, i))
    return pl.pallas_call(
        mid_kernel,
        grid=(T // TR,),
        in_specs=[cols, cols, rows_spec(D), rows_spec(D), rows_spec(D), whole_spec(w.shape)],
        out_specs=[rows_spec(D), whole_spec((D, 2 * W))],
        out_shape=[jax.ShapeDtypeStruct((T, D), bf16), jax.ShapeDtypeStruct((D, 2 * W), bf16)],
        scratch_shapes=[pltpu.VMEM((2 * W, D), f32)],
        compiler_params=pltpu.CompilerParams(vmem_limit_bytes=VMEM_LIMIT),
        cost_estimate=cost(9),
        name="mid",
    )(o, dq, mixer, g, branch, w)


def post_kernel(place_ref, dkv_ref, ahead_ref, dq_ref, cos_ref, sin_ref, normed_ref, mixer_ref, back_ref, gain_ref, w_ref, *refs):
    heads = dkv_ref.shape[0]
    W = heads * HD
    step = pl.program_id(0)
    if len(refs) == 8:
        _, acc_in, sums_in, mid_ref, *refs = refs
    else:
        acc_in = mid_ref = None
        sums_in, *refs = refs
    hat_ref, grad_ref, sums_ref, acc_ref = refs

    @pl.when(step == 0)
    def _():
        sums_ref[...] = sums_in[...]
        acc_ref[...] = jnp.zeros_like(acc_ref) if acc_in is None else acc_in[...]

    cos_rows, sin_rows = rotation_rows(cos_ref[...], sin_ref[...])
    kv = jnp.concatenate(
        [rotate(dkv_ref[h] + ahead_ref[h].astype(f32), cos_rows, -sin_rows).astype(bf16) for h in range(heads)], axis=1
    )
    acc_ref[...] += mm(mixer_ref[...], kv, TN)
    dq = dq_ref[...].astype(f32).T.astype(bf16)
    part = mm(kv, w_ref[:, : 2 * W], NT) + mm(dq, w_ref[:, 2 * W : 3 * W], NT)
    hat_ref[...] = (part * gain_ref[...] + back_ref[...].astype(f32)).astype(bf16)
    sums_ref[0:1] += jnp.sum(part * normed_ref[...].astype(f32), axis=0, keepdims=True)
    sums_ref[1:2] += jnp.sum(part, axis=0, keepdims=True)
    sums_ref[2:3, : 2 * W] += jnp.sum(kv.astype(f32), axis=0, keepdims=True)
    sums_ref[2:3, 2 * W : 3 * W] += jnp.sum(dq.astype(f32), axis=0, keepdims=True)

    @pl.when(step == pl.num_programs(0) - 1)
    def _():
        grad_ref[:, : 2 * W] = acc_ref[...].astype(grad_ref.dtype)
        if mid_ref is not None:
            grad_ref[:, 2 * W :] = mid_ref[...]


def post(part, place, dkv, ahead, dq, cos, sin, normed, mixer, back, gain, w, early=()):
    T, D = mixer.shape
    heads = dkv.shape[0]
    W = heads * HD
    per = T // 2 // PR

    def at(i, place):
        return (part ^ (place[0] >> 1)) * per + i

    def inner(i, place):
        return i

    def rows(index):
        return pl.BlockSpec((PR, D), lambda i, place: (index(i, place), 0))

    def cols(count):
        return pl.BlockSpec((count, PR), lambda i, place: (0, at(i, place)))

    def fixed(shape):
        return pl.BlockSpec(shape, lambda i, place: (0,) * len(shape))

    half = pl.BlockSpec((heads, PR, 128), lambda i, place: (0, i, 0))
    late = len(early) > 1
    specs = [half, half, cols(W), cols(8), cols(8), rows(at), rows(at), rows(at), fixed(gain.shape), fixed(w.shape)]
    if late:
        specs += [pl.BlockSpec(memory_space=pl.ANY), fixed((D, 2 * W)), fixed((8, D)), fixed((D, 2 * W))]
    else:
        specs += [fixed((8, D))]
    return pl.pallas_call(
        post_kernel,
        grid_spec=pltpu.PrefetchScalarGridSpec(
            num_scalar_prefetch=1,
            grid=(per,),
            in_specs=specs,
            out_specs=[rows(at), fixed((D, (4 if late else 2) * W)), fixed((8, D))],
            scratch_shapes=[pltpu.VMEM((D, 2 * W), f32)],
        ),
        out_shape=[
            jax.ShapeDtypeStruct((T, D), bf16),
            jax.ShapeDtypeStruct((D, 4 * W), bf16) if late else jax.ShapeDtypeStruct((D, 2 * W), f32),
            jax.ShapeDtypeStruct((8, D), f32),
        ],
        input_output_aliases={11: 0} if late else {},
        compiler_params=pltpu.CompilerParams(vmem_limit_bytes=VMEM_LIMIT),
        cost_estimate=cost(8),
        name="post",
    )(place, dkv, ahead, dq, cos, sin, normed, mixer, back, gain, w, *early)


def shards(
    hidden_in, positions, mixer_gain, mixer_shift, feed_gain, feed_shift, triple_weight,
    pair_bias, output_weight, up_weight, up_bias, down_weight, out_bias, out_grad,
):
    T = positions.shape[0]
    blk, D = hidden_in.shape
    W = pair_bias.shape[1]
    heads = W // HD
    chunk = triple_weight.shape[0]
    t = lax.axis_index("tensor").astype(jnp.int32)

    F = up_weight.shape[1]
    bits = bit_count("dp")
    down_order = list(reversed(range(bits)))
    mixed_order = down_order[:-2] + [0, 1]
    q_w, k_w, v_w = (triple_weight[:, i].reshape(chunk, heads, HD) for i in range(3))
    kv_w = jnp.concatenate([k_w, v_w], axis=2).reshape(chunk, 2 * W)
    pad = (-W) % 128
    no_cols = jnp.zeros((chunk, pad), bf16)
    qkv_w, qkv_parts = gather_dp(jnp.concatenate([kv_w, q_w.reshape(chunk, W), no_cols], axis=1), down_order)
    hids = gather_tensor(hidden_in)
    gs = gather_tensor(after(out_grad, hids[2]))

    pos = jnp.concatenate([lax.dynamic_slice(positions, ((r ^ t) * blk,), (blk,)) for r in range(T // blk)])
    inverse = 1.0 / 10000.0 ** (jnp.arange(ROT // 2, dtype=f32) * (2.0 / ROT))
    angles = pos.astype(f32)[None, :] * inverse[:, None]
    cos, sin = jnp.cos(angles), jnp.sin(angles)
    rows = jnp.arange(T, dtype=jnp.int32) ^ (t * blk)
    start = (rows + T - pos)[None]
    q_starts = jnp.arange(0, T, TQ, dtype=jnp.int32)
    first = (q_starts + T - positions[::TQ]) // TK

    gains = jnp.stack([mixer_gain, mixer_shift, feed_gain, feed_shift])
    v_bias = pair_bias[1].reshape(heads, HD)
    kv_bias = jnp.concatenate([jnp.zeros_like(v_bias), v_bias], axis=1).reshape(2 * W)
    bias = jnp.concatenate([kv_bias, pair_bias[0], jnp.zeros((pad,), f32)])[None]
    mixer_in, kv, q = pre(hids, gains, qkv_w, bias, cos, sin, heads)
    up_w, up_parts = gather_dp(up_weight, down_order, [qkv_parts[-2]] + [None] * (bits - 2) + [qkv_w, kv])
    down_own = jnp.concatenate([down_weight.T, output_weight.T, no_cols], axis=1)
    down_w, _ = gather_dp(down_own, down_order, [up_parts[0]] + [None] * (bits - 2) + [(kv, up_w, gs[2])])
    tail = shift(after(kv, down_w), "dp", 1)
    normed, g, branch, back, do, ffn_grad, ffn_sums = ffn(hids, gs, gains[2:], up_w, down_w, up_bias[None], heads)
    spots = t[None]
    attn_args = (spots, first, start, tail, kv, q, do, cos, sin, blk)
    *early, dtail_low, carry = attention(*attn_args)
    ahead_low = shift(dtail_low, "dp", -1)
    ffn_order = down_order[::-1]
    o, dq, dtail_high, dkv_low, dkv_high = attention(*attn_args, early=(carry, *early))
    ahead_high = shift(after(dtail_high, ahead_low), "dp", -1)
    ffn_first = scatter_step(ffn_grad, chunk, ffn_order, ffn_order[0], tail, o)
    post_args = (dq, cos, sin, normed, mixer_in, back, mixer_gain[None], qkv_w)
    branch, mid_grad = mid(o, dq, mixer_in, g, branch, down_w[:, F:])
    branch_own, branch_far = scatter_core(branch, blk)
    branch_across = swap(branch_far, "tensor", 2)
    result = hidden_in.astype(f32) + branch_own + branch_across.astype(f32) + out_bias
    early = post(0, spots, dkv_low, after(ahead_low, ffn_first, branch_far), *post_args, early=(ffn_sums,))
    hat, mix_grad, sums = post(1, spots, dkv_high, ahead_high, *post_args, early=(*early, mid_grad))
    hat_own, hat_far = scatter_core(hat, blk)
    hat_across = swap(hat_far, "tensor", 2)
    grad_hat = hat_own + hat_across.astype(f32)
    mix_order = down_order[::-1]
    mix_grads = mix_grad
    for n, bit in enumerate(mix_order):
        landed = [(hat_far, branch_across), hat_across][n] if n < 2 else None
        mix_grads, sums = scatter_step(mix_grads, chunk, mix_order[n:], bit, None, landed, sums)
    ffn_grads = scatter_step(ffn_first, chunk, ffn_order[1:], ffn_order[1], None, mid_grad)
    for n in range(2, bits):
        ffn_grads = scatter_step(ffn_grads, chunk, ffn_order[n:], ffn_order[n], None, hat_across)
    own, inv_std = normalize(hidden_in.astype(f32))
    first_mean = jnp.mean(grad_hat, axis=-1, keepdims=True)
    second_mean = jnp.mean(grad_hat * own, axis=-1, keepdims=True)
    grad_hidden = out_grad.astype(f32) + inv_std * (grad_hat - first_mean - own * second_mean)
    norm_sums = sums + swap(sums, "tensor", 1)
    norm_sums = norm_sums + swap(norm_sums, "tensor", 2)
    head_sums = sums[2, : 2 * W].reshape(heads, 2, HD)[:, 1].reshape(W)
    pair_grad = jnp.stack([sums[2, 2 * W : 3 * W], head_sums])
    kv_grads = mix_grads[:, : 2 * W].reshape(chunk, heads, 2, HD)
    triple_grad = jnp.stack(
        [mix_grads[:, 2 * W : 3 * W], kv_grads[:, :, 0].reshape(chunk, W), kv_grads[:, :, 1].reshape(chunk, W)], axis=1
    )
    return (
        result,
        grad_hidden,
        norm_sums[0],
        norm_sums[1],
        norm_sums[3],
        norm_sums[4],
        triple_grad,
        pair_grad,
        mix_grads[:, 3 * W :].T,
        ffn_grads[:, :F],
        sums[5],
        ffn_grads[:, F:].T,
        norm_sums[6],
    )


def solution(mesh):
    rows = P(("dp", "tensor"), None)
    in_specs = (
        rows, P("dp"), P(), P(), P(), P(), P("dp", None, "tensor"), P(None, "tensor"), P("tensor", "dp"),
        P("dp", "tensor"), P("tensor"), P("tensor", "dp"), P(), rows,
    )
    out_specs = (
        rows, rows, P(), P(), P(), P(), P("dp", None, "tensor"), P(None, "tensor"), P("tensor", "dp"),
        P("dp", "tensor"), P("tensor"), P("tensor", "dp"), P(),
    )
    return jax.shard_map(shards, mesh=mesh, in_specs=in_specs, out_specs=out_specs, check_vma=False)
```

```python
import functools
import math

import jax
import jax.numpy as jnp
from jax import lax
from jax.experimental import pallas as pl
from jax.experimental.pallas import tpu as pltpu
from jax.sharding import PartitionSpec as P

HD = 64
ROT = 16
DOC_MOST = 2048
EPSILON = 1e-05
NEG = -1e30
TQ = 256
TK = 256
NK = 2
TR = 512
FR = 512
PR = 512
MR = 512
bf16 = jnp.bfloat16
f32 = jnp.float32
NN = (((1,), (0,)), ((), ()))
NT = (((1,), (1,)), ((), ()))
TN = (((0,), (0,)), ((), ()))
TT = (((0,), (1,)), ((), ()))
VMEM_LIMIT = 56 * 2**20


def cost(us):
    return pl.CostEstimate(flops=int(us * 1.15e9), bytes_accessed=1000, transcendentals=0)


def mm(left, right, dims=NN):
    return lax.dot_general(left, right, dims, preferred_element_type=f32)


def swap(value, axis, mask):
    count = lax.axis_size(axis)
    return lax.ppermute(value, axis, [(i, i ^ mask) for i in range(count)])


def shift(value, axis, distance):
    count = lax.axis_size(axis)
    route = [(i, i + distance) for i in range(count) if 0 <= i + distance < count]
    return lax.ppermute(value, axis, route)


def bit_count(axis):
    return lax.axis_size(axis).bit_length() - 1


def after(value, *others):
    return lax.optimization_barrier((value, others))[0]


def gather_tensor(own):
    near = swap(own, "tensor", 1)
    far = swap(own, "tensor", 2)
    diagonal = swap(far, "tensor", 1)
    return [own, near, far, diagonal]


def scatter_core(blocks):
    rows = blocks.shape[0] // 4
    near = swap(blocks[2 * rows :], "tensor", 1).astype(f32)
    total = blocks[: 2 * rows].astype(f32) + near
    return total[:rows], total[rows:].astype(bf16)


def split(held, rows, left, bit):
    above = 1 << sum(b > bit for b in left)
    return held.reshape(above, 2, -1, held.shape[-1])


def gather_dp(own, order, gates=()):
    me = lax.axis_index("dp")
    rows, cols = own.shape
    held, done = own, []
    parts = []
    for n, bit in enumerate(order):
        if n == 0 and gates and gates[0] is not None:
            held = after(held, gates[0])
        other = swap(held, "dp", 1 << bit)
        if n + 1 < len(gates) and gates[n + 1] is not None:
            other = after(other, gates[n + 1])
        high = ((me >> bit) & 1) == 1
        above = 1 << sum(b > bit for b in done)
        one, two = held.reshape(above, -1, cols), other.reshape(above, -1, cols)
        held = jnp.stack([jnp.where(high, two, one), jnp.where(high, one, two)], axis=1).reshape(-1, cols)
        done.append(bit)
        parts.append(held)
    return held, parts


def two_parts(sums):
    first = lax.reduce_precision(sums, 8, 7)
    return first, lax.reduce_precision(sums - first, 8, 7)


def halves(held, rows, left, bit):
    cols = held.shape[1]
    pairs = split(held, rows, left, bit)
    high = ((lax.axis_index("dp") >> bit) & 1) == 1
    send = jnp.where(high, pairs[:, 0], pairs[:, 1]).astype(bf16).reshape(-1, cols)
    keep = jnp.where(high, pairs[:, 1], pairs[:, 0]).reshape(-1, cols)
    return send, keep


def scatter_step(held, rows, left, bit, landed=None, sums=None):
    send, keep = halves(held, rows, left, bit)
    count = send.shape[0]
    if sums is not None:
        first, second = two_parts(sums)
        send = jnp.concatenate([send, first.astype(bf16), second.astype(bf16)], axis=0)
    other = swap(send, "dp", 1 << bit)
    if landed is not None:
        other = after(other, landed)
    other = other.astype(f32)
    held = keep.astype(f32) + other[:count]
    if sums is None:
        return held
    return held, (first + second) + (other[count : count + 8] + other[count + 8 :])


def sum_over(value, axis):
    for bit in range(bit_count(axis)):
        value = value + swap(value, axis, 1 << bit)
    return value


def normalize(values):
    centred = values - jnp.mean(values, axis=-1, keepdims=True)
    inv_std = lax.rsqrt(jnp.mean(centred * centred, axis=-1, keepdims=True) + EPSILON)
    return (centred * inv_std, inv_std)


def rows_spec(cols, tile=TR):
    return pl.BlockSpec((tile, cols), lambda i: (i, 0))


def whole_spec(shape):
    return pl.BlockSpec(shape, lambda i: (0,) * len(shape))


def heads_spec(heads, cols=128, tile=TR):
    return pl.BlockSpec((heads, tile, cols), lambda i: (0, i, 0))


def piece_specs(count, rows, cols, tile=TR):
    per = rows // tile
    return [pl.BlockSpec((tile, cols), lambda i, p=p: (jnp.clip(i - p * per, 0, per - 1), 0)) for p in range(count)]


def pick(refs, rows):
    at = pl.program_id(0) // (rows // refs[0].shape[0])
    value = refs[0][...]
    for n, ref in enumerate(refs[1:]):
        value = jnp.where(at == n + 1, ref[...], value)
    return value


def rotation_rows(cos, sin):
    ones = jnp.ones((128 - ROT, cos.shape[1]), f32)
    return jnp.concatenate([cos, cos, ones], axis=0).T, jnp.concatenate([-sin, sin, ones * 0.0], axis=0).T


def rotate(x, cos_rows, sin_rows):
    lane = lax.broadcasted_iota(jnp.int32, x.shape, 1)
    partner = jnp.where(lane < ROT // 2, pltpu.roll(x, 128 - ROT // 2, 1), pltpu.roll(x, ROT // 2, 1))
    return x * cos_rows + partner * sin_rows


def pre_kernel(*refs, pieces, blk):
    hids, refs = refs[:pieces], refs[pieces:]
    gains_ref, w_ref, bias_ref, cos_ref, sin_ref, mixer_ref, kv_ref, q_ref = refs
    heads = kv_ref.shape[0]
    normed, _ = normalize(pick(hids, blk).astype(f32))
    mixer = (normed * gains_ref[0:1] + gains_ref[1:2]).astype(bf16)
    mixer_ref[...] = mixer
    proj = mm(mixer, w_ref[...]) + bias_ref[...]
    cos_rows, sin_rows = rotation_rows(cos_ref[...], sin_ref[...])
    lane = lax.broadcasted_iota(jnp.int32, (TR, 128), 1)
    for h in range(heads):
        kv_ref[h] = rotate(proj[:, h * 128 : (h + 1) * 128], cos_rows, sin_rows).astype(bf16)
        at = heads * 128 + (h // 2) * 128
        x = proj[:, at : at + 128]
        if h % 2:
            x = pltpu.roll(x, HD, 1)
        x = jnp.where(lane < HD, rotate(x, cos_rows, sin_rows) * (1.0 / math.sqrt(HD)), 0.0)
        q_ref[h] = x.astype(bf16)


def pre(hids, gains, w, bias, cos, sin, heads):
    blk, D = hids[0].shape
    T = blk * len(hids)
    return pl.pallas_call(
        functools.partial(pre_kernel, pieces=len(hids), blk=blk),
        grid=(T // TR,),
        in_specs=piece_specs(len(hids), blk, D) + [
            whole_spec(gains.shape),
            whole_spec(w.shape),
            whole_spec(bias.shape),
            pl.BlockSpec((8, TR), lambda i: (0, i)),
            pl.BlockSpec((8, TR), lambda i: (0, i)),
        ],
        out_specs=[rows_spec(D)] + [heads_spec(heads)] * 2,
        out_shape=[jax.ShapeDtypeStruct((T, D), bf16)] + [jax.ShapeDtypeStruct((heads, T, 128), bf16)] * 2,
        compiler_params=pltpu.CompilerParams(vmem_limit_bytes=VMEM_LIMIT),
        cost_estimate=cost(0.5),
        name="pre",
    )(*hids, gains, w, bias, cos, sin)


def gelu_parts(h):
    mag = jnp.abs(h) * (1.0 / math.sqrt(2.0))
    t = 1.0 / (1.0 + 0.3275911 * mag)
    poly = t * (0.254829592 + t * (-0.284496736 + t * (1.421413741 + t * (-1.453152027 + t * 1.061405429))))
    bell = jnp.exp(-0.5 * h * h)
    tail = 0.5 * poly * bell
    return (jnp.where(h >= 0, 1.0 - tail, tail), bell * (1.0 / math.sqrt(2.0 * math.pi)))


def store_halves(total, high, chunk, send_ref, keep_ref):
    count = total.shape[0] // chunk
    low, top = (
        jnp.concatenate([total[n * chunk : (n + 1) * chunk] for n in range(side, count, 2)], axis=0) for side in (0, 1)
    )
    send_ref[: total.shape[0] // 2] = jnp.where(high == 1, low, top).astype(bf16)
    keep_ref[...] = jnp.where(high == 1, top, low).astype(bf16)


def ffn_kernel(*refs, pieces, blk, chunk):
    hids, gs, refs = refs[:pieces], refs[pieces : 2 * pieces], refs[2 * pieces :]
    gains_ref, up_ref, down_ref, qkv_ref, bias_ref, high_ref, normed_ref, g_ref, branch_ref, back_ref, do_ref, send_ref, keep_ref, sums_ref, acc_ref = refs
    heads = do_ref.shape[0]
    F = bias_ref.shape[1]
    step = pl.program_id(0)
    normed, _ = normalize(pick(hids, blk).astype(f32))
    normed_ref[...] = normed.astype(bf16)
    feed = (normed * gains_ref[0:1] + gains_ref[1:2]).astype(bf16)
    g = pick(gs, blk)
    g_ref[...] = g
    up, down = up_ref[...], down_ref[:, :F]
    hidden = mm(feed, up) + bias_ref[...]
    cumulative, density = gelu_parts(hidden)
    act = (hidden * cumulative).astype(bf16)
    hg = (mm(g, down) * (cumulative + hidden * density)).astype(bf16)
    branch_ref[...] = mm(act, down, NT).astype(bf16)
    back = mm(hg, up, NT)
    back_ref[...] = (back * gains_ref[0:1]).astype(bf16)

    @pl.when(step == 0)
    def _():
        sums_ref[...] = jnp.zeros_like(sums_ref)
        acc_ref[...] = jnp.zeros_like(acc_ref)

    acc_ref[:, :F] += mm(feed, hg, TN)
    acc_ref[:, F:] += mm(g, act, TN)
    sums_ref[3:4] += jnp.sum(back * normed, axis=0, keepdims=True)
    sums_ref[4:5] += jnp.sum(back, axis=0, keepdims=True)
    sums_ref[5:6] += jnp.sum(hg.astype(f32), axis=0, keepdims=True)

    @pl.when(step < blk // FR)
    def _():
        sums_ref[6:7] += jnp.sum(g.astype(f32), axis=0, keepdims=True)

    @pl.when(step == pl.num_programs(0) - 1)
    def _():
        store_halves(acc_ref[...], high_ref[0], chunk, send_ref, keep_ref)

    do = jnp.concatenate([mm(g, qkv_ref[...]), mm(g, down_ref[:, F:])], axis=1)
    lane = lax.broadcasted_iota(jnp.int32, (FR, 128), 1)
    for h in range(heads):
        at = HD * (h + 1)
        x = do[:, at // 128 * 128 : at // 128 * 128 + 128]
        if at % 128 == 0:
            x = pltpu.roll(x, HD, 1)
        do_ref[h] = jnp.where(lane < HD, 0.0, x).astype(bf16)


def ffn(hids, gs, gains, up, down, qkv, bias, high, heads, chunk):
    blk, D = gs[0].shape
    T = blk * len(gs)
    F = bias.shape[1]
    rows = rows_spec(D, FR)
    return pl.pallas_call(
        functools.partial(ffn_kernel, pieces=len(gs), blk=blk, chunk=chunk),
        grid=(T // FR,),
        in_specs=piece_specs(len(gs), blk, D, FR) * 2
        + [whole_spec(gains.shape), whole_spec(up.shape), whole_spec(down.shape)]
        + [pl.BlockSpec((D, 128), lambda i: (0, qkv.shape[1] // 128 - 1)), whole_spec(bias.shape)]
        + [pl.BlockSpec(memory_space=pltpu.SMEM)],
        out_specs=[rows] * 4 + [heads_spec(heads, 128, FR)] + [whole_spec((D // 2, 2 * F))] * 2 + [whole_spec((8, D))],
        out_shape=[jax.ShapeDtypeStruct((T, D), bf16)] * 4
        + [
            jax.ShapeDtypeStruct((heads, T, 128), bf16),
            jax.ShapeDtypeStruct((D // 2, 2 * F), bf16),
            jax.ShapeDtypeStruct((D // 2, 2 * F), bf16),
            jax.ShapeDtypeStruct((8, D), f32),
        ],
        scratch_shapes=[pltpu.VMEM((D, 2 * F), f32)],
        compiler_params=pltpu.CompilerParams(vmem_limit_bytes=VMEM_LIMIT),
        cost_estimate=cost(0.5),
        name="ffn",
    )(*hids, *gs, gains, up, down, qkv, bias, high)


def attn_kernel(*refs, T, blk, heads, late):
    if late:
        (place_ref, first_ref, start_ref, tail_ref, kv_ref, q_ref, do_ref, cos_ref, sin_ref, carry_ref, o_in, dq_in,
         o_ref, dq_ref, dtail_ref, low_ref, high_ref, *refs) = refs
    else:
        (place_ref, first_ref, start_ref, tail_ref, kv_ref, q_ref, do_ref, cos_ref, sin_ref,
         o_ref, dq_ref, dtail_ref, carry_ref, *refs) = refs
    kv_scr, dkv_scr, s_scr, dp_scr, o_acc, dq_acc, qd_scr = refs
    half = T // 2
    base = half if late else 0
    t = place_ref[0]
    inner = (t & 1) * blk
    H = range(heads)

    def half_at(n):
        return pl.ds(pl.multiple_of((n ^ (t >> 1)) * half, half), half)

    for n, (ref, part) in enumerate([(tail_ref, 1), (kv_ref, 0), (kv_ref, 1)] if late else [(tail_ref, 0), (tail_ref, 1), (kv_ref, 0)]):
        kv_scr[:, n * half : (n + 1) * half] = ref[:, half_at(part), :]
    if late:
        dkv_scr[:, :T] = carry_ref[...]
        dkv_scr[:, T:] = jnp.zeros_like(dkv_scr[:, T:])
        o_ref[:, half_at(0)] = o_in[...]
        dq_ref[:, half_at(0)] = dq_in[...]
    else:
        dkv_scr[...] = jnp.zeros_like(dkv_scr)

    def place(row):
        return (row - base) ^ inner

    def q_tile(qi, c):
        q0 = pl.multiple_of(base + qi * TQ, TQ)
        qr = pl.multiple_of(q0 ^ (t * blk), TQ)
        out = qr if late else pl.multiple_of(place(q0), TQ)
        for h in H:
            qd_scr[h, :TQ] = q_ref[h, pl.ds(qr, TQ), :]
            qd_scr[h, TQ:] = do_ref[h, pl.ds(qr, TQ), :]
        start = start_ref[:, pl.ds(qr, TQ)]
        qidx = q0 + T + lax.broadcasted_iota(jnp.int32, (1, TQ), 1)
        first = first_ref[base // TQ + qi]
        stop = (q0 + T) // TK + TQ // TK
        count = stop - first

        def over(body, init):
            pairs = count // NK
            state = lax.fori_loop(0, pairs, lambda i, c: body(first + i * NK, c, NK), init)
            return lax.fori_loop(first + pairs * NK, stop, lambda i, c: body(i, c, 1), state)

        def pass1(ki, state, nk):
            rows = nk * TK
            slot = ki - first
            j = ki * TK + lax.broadcasted_iota(jnp.int32, (rows, TQ), 0)
            ok = (j >= start) & (j <= qidx)
            ats = [pl.multiple_of(place((ki + n) * TK), TK) for n in range(nk)]
            sdps = [mm(jnp.concatenate([kv_scr[h, pl.ds(at, TK), :] for at in ats], axis=0), qd_scr[h], NT) for h in H]
            stats = []
            for h in H:
                m8, l8, d8 = state[3 * h : 3 * h + 3]
                s = jnp.where(ok, sdps[h][:, :TQ], NEG)
                dp = sdps[h][:, TQ:]
                for n in range(nk):
                    s_scr[slot + n, h] = s[n * TK : (n + 1) * TK]
                    dp_scr[slot + n, h] = dp[n * TK : (n + 1) * TK]
                s3 = s.reshape(rows // 8, 8, TQ)
                m_new = jnp.maximum(m8, jnp.max(s3, axis=0))
                alpha = jnp.exp(m8 - m_new)
                e = jnp.exp(s3 - m_new[None])
                l8 = l8 * alpha + jnp.sum(e, axis=0)
                d8 = d8 * alpha + jnp.sum(e * dp.reshape(rows // 8, 8, TQ), axis=0)
                stats += [m_new, l8, d8]
            return tuple(stats)

        z8 = jnp.zeros((8, TQ), f32)
        state = over(pass1, (jnp.full((8, TQ), NEG, f32), z8, z8) * heads)
        lses, deltas = [], []
        for h in H:
            m8, l8, d8 = state[3 * h : 3 * h + 3]
            m = jnp.max(m8, axis=0, keepdims=True)
            w = jnp.exp(m8 - m)
            total = jnp.sum(l8 * w, axis=0, keepdims=True)
            lses.append(m + jnp.log(total))
            deltas.append(jnp.sum(d8 * w, axis=0, keepdims=True) / total)
        o_acc[...] = jnp.zeros_like(o_acc)
        dq_acc[...] = jnp.zeros_like(dq_acc)

        def pass2(ki, c2, nk):
            slot = ki - first
            ats = [pl.multiple_of(place((ki + n) * TK), TK) for n in range(nk)]
            for h in H:
                dq = dq_acc[h]
                o = o_acc[h]
                for n in range(nk):
                    p = jnp.exp(s_scr[slot + n, h] - lses[h])
                    ds = (p * (dp_scr[slot + n, h] - deltas[h])).astype(bf16)
                    p = p.astype(bf16)
                    dkv_scr[h, pl.ds(ats[n], TK), :] += mm(jnp.concatenate([ds, p], axis=1), qd_scr[h])
                    kvt = kv_scr[h, pl.ds(ats[n], TK), :].T
                    dq += mm(kvt[:HD], ds)
                    o += mm(kvt[HD:], p)
                dq_acc[h] = dq
                o_acc[h] = o
            return c2

        over(pass2, 0)
        cos = cos_ref[:, pl.ds(qr, TQ)]
        sin = sin_ref[:, pl.ds(qr, TQ)]
        for h in H:
            o_ref[h * HD : (h + 1) * HD, pl.ds(out, TQ)] = o_acc[h].astype(bf16)
            dq = dq_acc[h] * (1.0 / math.sqrt(HD))
            a, b = dq[: ROT // 2], dq[ROT // 2 : ROT]
            dq = jnp.concatenate([a * cos + b * sin, b * cos - a * sin, dq[ROT:]], axis=0)
            dq_ref[h * HD : (h + 1) * HD, pl.ds(out, TQ)] = dq.astype(bf16)
        return c

    lax.fori_loop(0, half // TQ, q_tile, 0)
    dtail_ref[...] = dkv_scr[:, :half].astype(bf16)
    if late:
        low_ref[...] = dkv_scr[:, half:T]
        high_ref[...] = dkv_scr[:, T:]
    else:
        carry_ref[...] = dkv_scr[:, half:]


def attention(place, first, start, tail, kv, q, do, cos, sin, blk, early=()):
    heads, T, _ = q.shape
    W = heads * HD
    late = len(early) > 0
    vmem = pl.BlockSpec(memory_space=pltpu.VMEM)
    smem = pl.BlockSpec(memory_space=pltpu.SMEM)
    slots = DOC_MOST // TK + TQ // TK
    span = T if late else T // 2
    outs = [((W, span), bf16), ((W, span), bf16), ((heads, T // 2, 128), bf16)]
    outs += [((heads, T // 2, 128), f32)] * 2 if late else [((heads, T, 128), f32)]
    return pl.pallas_call(
        functools.partial(attn_kernel, T=T, blk=blk, heads=heads, late=late),
        in_specs=[smem, smem] + [vmem] * (7 + len(early)),
        out_specs=[vmem] * len(outs),
        scratch_shapes=[
            pltpu.VMEM((heads, T + T // 2, 128), bf16),
            pltpu.VMEM((heads, T + T // 2, 128), f32),
            pltpu.VMEM((slots, heads, TK, TQ), f32),
            pltpu.VMEM((slots, heads, TK, TQ), f32),
            pltpu.VMEM((heads, HD, TQ), f32),
            pltpu.VMEM((heads, HD, TQ), f32),
            pltpu.VMEM((heads, 2 * TQ, 128), bf16),
        ],
        out_shape=[jax.ShapeDtypeStruct(*out) for out in outs],
        compiler_params=pltpu.CompilerParams(vmem_limit_bytes=40 * 2**20),
        cost_estimate=cost(0.1),
        name="attn",
    )(place, first, start, tail, kv, q, do, cos, sin, *early)


def mid_kernel(o_ref, dq_ref, mixer_ref, g_ref, branch_ref, qkv_ref, down_ref, out_ref, grad_ref, acc_ref):
    W = o_ref.shape[0]
    pad = qkv_ref.shape[1] - HD
    step = pl.program_id(0)
    o = o_ref[...]
    rows = jnp.concatenate([jnp.zeros((pad, o.shape[1]), f32), o.astype(f32)], axis=0).T.astype(bf16)
    out = mm(rows[:, : pad + HD], qkv_ref[...], NT) + mm(rows[:, pad + HD :], down_ref[...], NT)
    out_ref[...] = (out + branch_ref[...].astype(f32)).astype(bf16)

    @pl.when(step == 0)
    def _():
        acc_ref[...] = jnp.zeros_like(acc_ref)

    acc_ref[:W] += mm(dq_ref[...], mixer_ref[...])
    acc_ref[W:] += mm(o, g_ref[...])

    @pl.when(step == pl.num_programs(0) - 1)
    def _():
        grad_ref[...] = acc_ref[...].T.astype(bf16)


def mid(o, dq, mixer, g, branch, qkv, down):
    T, D = mixer.shape
    W = o.shape[0]
    cols = pl.BlockSpec((W, MR), lambda i: (0, i))
    rows = rows_spec(D, MR)
    rest = W - HD
    return pl.pallas_call(
        mid_kernel,
        grid=(T // MR,),
        in_specs=[
            cols, cols, rows, rows, rows,
            pl.BlockSpec((D, 128), lambda i: (0, qkv.shape[1] // 128 - 1)),
            pl.BlockSpec((D, rest), lambda i: (0, down.shape[1] // rest - 1)),
        ],
        out_specs=[pl.BlockSpec((MR, D), lambda i: (i // 2 + i % 2 * 2, 0)), whole_spec((D, 2 * W))],
        out_shape=[jax.ShapeDtypeStruct((T, D), bf16), jax.ShapeDtypeStruct((D, 2 * W), bf16)],
        scratch_shapes=[pltpu.VMEM((2 * W, D), f32)],
        compiler_params=pltpu.CompilerParams(vmem_limit_bytes=VMEM_LIMIT),
        cost_estimate=cost(0.1),
        name="mid",
    )(o, dq, mixer, g, branch, qkv, down)


def post_kernel(place_ref, dkv_ref, ahead_ref, dq_ref, cos_ref, sin_ref, normed_ref, mixer_ref, back_ref, gain_ref, w_ref, *refs, chunk):
    heads = dkv_ref.shape[0]
    W = heads * HD
    step = pl.program_id(0)
    late = chunk is not None
    if late:
        _, acc_in, sums_in, mid_ref, hat_ref, send_ref, keep_ref, sums_ref, acc_ref = refs
    else:
        acc_in = None
        sums_in, hat_ref, grad_ref, sums_ref, acc_ref = refs

    @pl.when(step == 0)
    def _():
        sums_ref[...] = sums_in[...]
        acc_ref[...] = jnp.zeros_like(acc_ref) if acc_in is None else acc_in[...]

    cos_rows, sin_rows = rotation_rows(cos_ref[...], sin_ref[...])
    kv = jnp.concatenate(
        [rotate(dkv_ref[h] + ahead_ref[h].astype(f32), cos_rows, -sin_rows).astype(bf16) for h in range(heads)], axis=1
    )
    acc_ref[...] += mm(mixer_ref[...], kv, TN)
    dq = dq_ref[...].astype(f32).T.astype(bf16)
    part = mm(kv, w_ref[:, : 2 * W], NT) + mm(dq, w_ref[:, 2 * W : 3 * W], NT)
    hat_ref[...] = (part * gain_ref[...] + back_ref[...].astype(f32)).astype(bf16)
    sums_ref[0:1] += jnp.sum(part * normed_ref[...].astype(f32), axis=0, keepdims=True)
    sums_ref[1:2] += jnp.sum(part, axis=0, keepdims=True)
    sums_ref[2:3, : 2 * W] += jnp.sum(kv.astype(f32), axis=0, keepdims=True)
    sums_ref[2:3, 2 * W : 3 * W] += jnp.sum(dq.astype(f32), axis=0, keepdims=True)

    @pl.when(step == pl.num_programs(0) - 1)
    def _():
        if late:
            total = jnp.concatenate([acc_ref[...], mid_ref[...].astype(f32)], axis=1)
            store_halves(total, place_ref[1], chunk, send_ref, keep_ref)
            one = sums_ref[...].astype(bf16).astype(f32)
            two = (sums_ref[...] - one).astype(bf16).astype(f32)
            sums_ref[...] = one + two
            send_ref[total.shape[0] // 2 :] = jnp.concatenate([one, two], axis=0).astype(bf16)
        else:
            grad_ref[...] = acc_ref[...]


def post(part, place, dkv, ahead, dq, cos, sin, normed, mixer, back, gain, w, early=(), chunk=None):
    T, D = mixer.shape
    heads = dkv.shape[0]
    W = heads * HD
    per = T // 2 // PR

    def at(i, place):
        return (part ^ (place[0] >> 1)) * per + i

    def inner(i, place):
        return i

    def rows(index):
        return pl.BlockSpec((PR, D), lambda i, place: (index(i, place), 0))

    def cols(count):
        return pl.BlockSpec((count, PR), lambda i, place: (0, at(i, place)))

    def fixed(shape):
        return pl.BlockSpec(shape, lambda i, place: (0,) * len(shape))

    half = pl.BlockSpec((heads, PR, 128), lambda i, place: (0, i, 0))
    late = len(early) > 1
    specs = [half, half, cols(W), cols(8), cols(8), rows(at), rows(at), rows(at), fixed(gain.shape), fixed(w.shape)]
    if late:
        specs += [pl.BlockSpec(memory_space=pl.ANY), fixed((D, 2 * W)), fixed((8, D)), fixed((D, 2 * W))]
        grads = [fixed((D // 2 + 16, 4 * W)), fixed((D // 2, 4 * W))]
        shapes = [jax.ShapeDtypeStruct((D // 2 + 16, 4 * W), bf16), jax.ShapeDtypeStruct((D // 2, 4 * W), bf16)]
    else:
        specs += [fixed((8, D))]
        grads = [fixed((D, 2 * W))]
        shapes = [jax.ShapeDtypeStruct((D, 2 * W), f32)]
    return pl.pallas_call(
        functools.partial(post_kernel, chunk=chunk),
        grid_spec=pltpu.PrefetchScalarGridSpec(
            num_scalar_prefetch=1,
            grid=(per,),
            in_specs=specs,
            out_specs=[rows(lambda i, place: at(i, place) // 2 + at(i, place) % 2 * 2)] + grads + [fixed((8, D))],
            scratch_shapes=[pltpu.VMEM((D, 2 * W), f32)],
        ),
        out_shape=[
            jax.ShapeDtypeStruct((T, D), bf16),
            *shapes,
            jax.ShapeDtypeStruct((8, D), f32),
        ],
        input_output_aliases={11: 0} if late else {},
        compiler_params=pltpu.CompilerParams(vmem_limit_bytes=VMEM_LIMIT),
        cost_estimate=cost(8 if late else 0.1),
        name="post",
    )(place, dkv, ahead, dq, cos, sin, normed, mixer, back, gain, w, *early)


def mix_finish_kernel(keep_ref, other_ref, own_ref, triple_ref, out_ref, sums_ref):
    rows = keep_ref.shape[0]
    W = out_ref.shape[0]
    other = other_ref[...].astype(f32)
    total = keep_ref[...] + other[:rows]
    sums_ref[...] = own_ref[...] + (other[rows : rows + 8] + other[rows + 8 :])
    triple_ref[:, 0, :] = total[:, 2 * W : 3 * W]
    for n in range(2):
        triple_ref[:, 1 + n, :] = jnp.concatenate(
            [total[:, at + n * HD : at + (n + 1) * HD] for at in range(0, 2 * W, 2 * HD)], axis=1
        )
    out_ref[...] = total[:, 3 * W :].T


def mix_finish(keep, other, own, W):
    rows = keep.shape[0]
    return pl.pallas_call(
        mix_finish_kernel,
        out_shape=[
            jax.ShapeDtypeStruct((rows, 3, W), f32),
            jax.ShapeDtypeStruct((W, rows), f32),
            jax.ShapeDtypeStruct(own.shape, f32),
        ],
        cost_estimate=cost(0.1),
        name="mix_finish",
    )(keep, other, own)


def ffn_finish_kernel(keep_ref, other_ref, up_ref, down_ref):
    F = up_ref.shape[1]
    total = keep_ref[...] + other_ref[...].astype(f32)
    up_ref[...] = total[:, :F]
    down_ref[...] = total[:, F:].T


def ffn_finish(keep, other):
    rows, cols = keep.shape
    F = cols // 2
    return pl.pallas_call(
        ffn_finish_kernel,
        out_shape=[jax.ShapeDtypeStruct((rows, F), f32), jax.ShapeDtypeStruct((F, rows), f32)],
        cost_estimate=cost(0.1),
        name="ffn_finish",
    )(keep, other)


def shards(
    hidden_in, positions, mixer_gain, mixer_shift, feed_gain, feed_shift, triple_weight,
    pair_bias, output_weight, up_weight, up_bias, down_weight, out_bias, out_grad,
):
    T = positions.shape[0]
    blk, D = hidden_in.shape
    W = pair_bias.shape[1]
    heads = W // HD
    chunk = triple_weight.shape[0]
    t = lax.axis_index("tensor").astype(jnp.int32)

    F = up_weight.shape[1]
    bits = bit_count("dp")
    down_order = list(reversed(range(bits)))
    mixed_order = down_order[:-2] + [0, 1]
    q_w, k_w, v_w = (triple_weight[:, i].reshape(chunk, heads, HD) for i in range(3))
    kv_w = jnp.concatenate([k_w, v_w], axis=2).reshape(chunk, 2 * W)
    pad = (-W) % 128
    out_own = output_weight.T
    qkv_w, qkv_parts = gather_dp(jnp.concatenate([kv_w, q_w.reshape(chunk, W), out_own[:, :pad]], axis=1), down_order)
    hids = gather_tensor(hidden_in)
    gs = gather_tensor(after(out_grad, hids[2]))

    pos = jnp.concatenate([lax.dynamic_slice(positions, ((r ^ t) * blk,), (blk,)) for r in range(T // blk)])
    inverse = 1.0 / 10000.0 ** (jnp.arange(ROT // 2, dtype=f32) * (2.0 / ROT))
    angles = pos.astype(f32)[None, :] * inverse[:, None]
    cos, sin = jnp.cos(angles), jnp.sin(angles)
    rows = jnp.arange(T, dtype=jnp.int32) ^ (t * blk)
    start = (rows + T - pos)[None]
    q_starts = jnp.arange(0, T, TQ, dtype=jnp.int32)
    first = (q_starts + T - positions[::TQ]) // TK

    gains = jnp.stack([mixer_gain, mixer_shift, feed_gain, feed_shift])
    v_bias = pair_bias[1].reshape(heads, HD)
    kv_bias = jnp.concatenate([jnp.zeros_like(v_bias), v_bias], axis=1).reshape(2 * W)
    bias = jnp.concatenate([kv_bias, pair_bias[0], jnp.zeros((pad,), f32)])[None]
    high = (lax.axis_index("dp") & 1).astype(jnp.int32)
    spots = jnp.stack([t, high])
    mixer_in, kv, q = pre(hids, gains, qkv_w, bias, cos, sin, heads)
    feed_gains, feed_bias = gains[2:], up_bias[None]
    early_ops = (feed_gains, feed_bias, first, start)
    up_w, up_parts = gather_dp(up_weight, down_order, [qkv_parts[-2]] + [None] * (bits - 2) + [qkv_w, (kv, early_ops)])
    down_own = jnp.concatenate([down_weight.T, out_own[:, pad:]], axis=1)
    down_w, _ = gather_dp(down_own, down_order, [up_parts[0]] + [None] * (bits - 2) + [(kv, up_w)])
    tail = shift(after(kv, down_w), "dp", 1)
    normed, g, branch, back, do, ffn_send, ffn_keep, ffn_sums = ffn(
        hids, gs, feed_gains, up_w, down_w, qkv_w, feed_bias, high[None], heads, chunk
    )
    attn_args = (spots, first, start, tail, kv, q, do, cos, sin, blk)
    *early, dtail_low, carry = attention(*attn_args)
    ahead_low = shift(dtail_low, "dp", -1)
    ffn_order = down_order[::-1]
    ffn_other = swap(after(ffn_send, tail), "dp", 1 << ffn_order[0])
    o, dq, dtail_high, dkv_low, dkv_high = attention(*attn_args, early=(carry, *early))
    ahead_high = shift(after(dtail_high, ahead_low, ffn_other), "dp", -1)
    post_args = (dq, cos, sin, normed, mixer_in, back, mixer_gain[None], qkv_w)
    ffn_first = ffn_keep.astype(f32) + ffn_other.astype(f32)
    ffn_send, ffn_keep = halves(ffn_first, chunk, ffn_order[1:], ffn_order[1])
    ffn_other = swap(ffn_send, "dp", 1 << ffn_order[1])
    early = post(0, spots, dkv_low, after(ahead_low, ffn_first), *post_args, early=(ffn_sums,))
    branch, mid_grad = mid(after(o, early[2]), dq, mixer_in, g, branch, qkv_w, down_w)
    hat, mix_send, mix_keep, sums = post(
        1, spots, dkv_high, ahead_high, *post_args, early=(*early, mid_grad), chunk=chunk
    )
    mix_order = ffn_order
    hat, mix_send, mix_keep, sums, ffn_other = lax.optimization_barrier((hat, mix_send, mix_keep, sums, ffn_other))
    mix_other = swap(mix_send, "dp", 1 << mix_order[0])
    hat_own, far = scatter_core(hat)
    landed_far = swap(far, "tensor", 2)
    branch_own, branch_far = scatter_core(branch)
    branch_across = swap(after(branch_far, landed_far), "tensor", 2)
    ffn_grads = ffn_keep.astype(f32) + after(ffn_other, far).astype(f32)
    for n in range(2, bits):
        ffn_send, ffn_keep = halves(ffn_grads, chunk, ffn_order[n:], ffn_order[n])
        ffn_other = swap(ffn_send, "dp", 1 << ffn_order[n])
        ffn_grads = ffn_keep.astype(f32) + ffn_other.astype(f32)
    mix_other = after(mix_other, far, branch_far, ffn_other).astype(f32)
    mix_grads = mix_keep.astype(f32) + mix_other[: mix_keep.shape[0]]
    sums = sums + (mix_other[-16:-8] + mix_other[-8:])
    for n in range(1, bits - 1):
        mix_grads, sums = scatter_step(mix_grads, chunk, mix_order[n:], mix_order[n], landed_far if n == 1 else None, sums)
    mix_send, mix_keep = halves(mix_grads, chunk, mix_order[-1:], mix_order[-1])
    one, two = two_parts(sums)
    mix_send = jnp.concatenate([mix_send, one.astype(bf16), two.astype(bf16)], axis=0)
    mix_other = swap(mix_send, "dp", 1 << mix_order[-1])
    ffn_other = after(ffn_other, mix_send)
    up_grad, down_grad = ffn_finish(ffn_keep, ffn_other)
    grad_hat = hat_own + after(landed_far, mix_send).astype(f32)
    mix_other = after(mix_other, up_grad, grad_hat)
    triple_grad, out_grad_t, sums = mix_finish(mix_keep, mix_other, one + two, W)
    result = hidden_in.astype(f32) + branch_own + branch_across.astype(f32) + out_bias
    own, inv_std = normalize(hidden_in.astype(f32))
    first_mean = jnp.mean(grad_hat, axis=-1, keepdims=True)
    second_mean = jnp.mean(grad_hat * own, axis=-1, keepdims=True)
    grad_hidden = out_grad.astype(f32) + inv_std * (grad_hat - first_mean - own * second_mean)
    norm_sums = sums + swap(sums, "tensor", 1)
    norm_sums = norm_sums + swap(after(norm_sums, branch_across), "tensor", 2)
    head_sums = sums[2, : 2 * W].reshape(heads, 2, HD)[:, 1].reshape(W)
    pair_grad = jnp.stack([sums[2, 2 * W : 3 * W], head_sums])
    return (
        result,
        grad_hidden,
        norm_sums[0],
        norm_sums[1],
        norm_sums[3],
        norm_sums[4],
        triple_grad,
        pair_grad,
        out_grad_t,
        up_grad,
        sums[5],
        down_grad,
        norm_sums[6],
    )


def solution(mesh):
    rows = P(("dp", "tensor"), None)
    in_specs = (
        rows, P("dp"), P(), P(), P(), P(), P("dp", None, "tensor"), P(None, "tensor"), P("tensor", "dp"),
        P("dp", "tensor"), P("tensor"), P("tensor", "dp"), P(), rows,
    )
    out_specs = (
        rows, rows, P(), P(), P(), P(), P("dp", None, "tensor"), P(None, "tensor"), P("tensor", "dp"),
        P("dp", "tensor"), P("tensor"), P("tensor", "dp"), P(),
    )
    return jax.shard_map(shards, mesh=mesh, in_specs=in_specs, out_specs=out_specs, check_vma=False)
```

```python
import functools
import math

import jax
import jax.numpy as jnp
from jax import lax
from jax.experimental import pallas as pl
from jax.experimental.pallas import tpu as pltpu
from jax.sharding import PartitionSpec as P

HD = 64
ROT = 16
DOC_MOST = 2048
EPSILON = 1e-05
NEG = -1e30
TQ = 256
TK = 256
NK = 2
TR = 512
FR = 512
PR = 1024
MR = 1024
bf16 = jnp.bfloat16
f32 = jnp.float32
NN = (((1,), (0,)), ((), ()))
NT = (((1,), (1,)), ((), ()))
TN = (((0,), (0,)), ((), ()))
TT = (((0,), (1,)), ((), ()))
VMEM_LIMIT = 56 * 2**20


def cost(us):
    return pl.CostEstimate(flops=int(us * 1.15e9), bytes_accessed=1000, transcendentals=0)


def mm(left, right, dims=NN):
    return lax.dot_general(left, right, dims, preferred_element_type=f32)


def swap(value, axis, mask):
    count = lax.axis_size(axis)
    return lax.ppermute(value, axis, [(i, i ^ mask) for i in range(count)])


def shift(value, axis, distance):
    count = lax.axis_size(axis)
    route = [(i, i + distance) for i in range(count) if 0 <= i + distance < count]
    return lax.ppermute(value, axis, route)


def bit_count(axis):
    return lax.axis_size(axis).bit_length() - 1


def after(value, *others):
    return lax.optimization_barrier((value, others))[0]


def gather_tensor(own):
    near = swap(own, "tensor", 1)
    far = swap(own, "tensor", 2)
    diagonal = swap(far, "tensor", 1)
    return [own, near, far, diagonal]


def scatter_core(kept, sent):
    near = swap(sent, "tensor", 1).astype(f32)
    total = kept.astype(f32) + near
    rows = kept.shape[0] // 2
    return total[:rows], total[rows:].astype(bf16)


def split(held, rows, left, bit):
    above = 1 << sum(b > bit for b in left)
    return held.reshape(above, 2, -1, held.shape[-1])


def gather_dp(own, order, gates=()):
    me = lax.axis_index("dp")
    rows, cols = own.shape
    held, done = own, []
    parts = []
    for n, bit in enumerate(order):
        if n == 0 and gates and gates[0] is not None:
            held = after(held, gates[0])
        other = swap(held, "dp", 1 << bit)
        if n + 1 < len(gates) and gates[n + 1] is not None:
            other = after(other, gates[n + 1])
        high = ((me >> bit) & 1) == 1
        above = 1 << sum(b > bit for b in done)
        one, two = held.reshape(above, -1, cols), other.reshape(above, -1, cols)
        held = jnp.concatenate([jnp.where(high, two, one), jnp.where(high, one, two)], axis=1).reshape(-1, cols)
        done.append(bit)
        parts.append(held)
    return held, parts


def two_parts(sums):
    first = lax.reduce_precision(sums, 8, 7)
    return first, lax.reduce_precision(sums - first, 8, 7)


def halves(held, rows, left, bit):
    cols = held.shape[1]
    pairs = split(held, rows, left, bit)
    high = ((lax.axis_index("dp") >> bit) & 1) == 1
    send = jnp.where(high, pairs[:, 0], pairs[:, 1]).astype(bf16).reshape(-1, cols)
    keep = jnp.where(high, pairs[:, 1], pairs[:, 0]).reshape(-1, cols)
    return send, keep


def scatter_step(held, rows, left, bit, landed=None, sums=None):
    send, keep = halves(held, rows, left, bit)
    count = send.shape[0]
    if sums is not None:
        first, second = two_parts(sums)
        send = jnp.concatenate([send, first.astype(bf16), second.astype(bf16)], axis=0)
    other = swap(send, "dp", 1 << bit)
    if landed is not None:
        other = after(other, landed)
    other = other.astype(f32)
    held = keep.astype(f32) + other[:count]
    if sums is None:
        return held
    return held, (first + second) + (other[count : count + 8] + other[count + 8 :])


def sum_over(value, axis):
    for bit in range(bit_count(axis)):
        value = value + swap(value, axis, 1 << bit)
    return value


def normalize(values):
    centred = values - jnp.mean(values, axis=-1, keepdims=True)
    inv_std = lax.rsqrt(jnp.mean(centred * centred, axis=-1, keepdims=True) + EPSILON)
    return (centred * inv_std, inv_std)


def rows_spec(cols, tile=TR):
    return pl.BlockSpec((tile, cols), lambda i: (i, 0))


def whole_spec(shape):
    return pl.BlockSpec(shape, lambda i: (0,) * len(shape))


def heads_spec(heads, cols=128, tile=TR):
    return pl.BlockSpec((heads, tile, cols), lambda i: (0, i, 0))


def piece_specs(count, rows, cols, tile=TR):
    per = rows // tile
    return [pl.BlockSpec((tile, cols), lambda i, p=p: (jnp.clip(i - p * per, 0, per - 1), 0)) for p in range(count)]


def pick(refs, rows):
    at = pl.program_id(0) // (rows // refs[0].shape[0])
    value = refs[0][...]
    for n, ref in enumerate(refs[1:]):
        value = jnp.where(at == n + 1, ref[...], value)
    return value


def rotation_rows(cos, sin):
    ones = jnp.ones((128 - ROT, cos.shape[1]), f32)
    return jnp.concatenate([cos, cos, ones], axis=0).T, jnp.concatenate([-sin, sin, ones * 0.0], axis=0).T


def rotate(x, cos_rows, sin_rows):
    lane = lax.broadcasted_iota(jnp.int32, x.shape, 1)
    partner = jnp.where(lane < ROT // 2, pltpu.roll(x, 128 - ROT // 2, 1), pltpu.roll(x, ROT // 2, 1))
    return x * cos_rows + partner * sin_rows


def pre_kernel(*refs, pieces, blk):
    hids, refs = refs[:pieces], refs[pieces:]
    gains_ref, w_ref, bias_ref, cos_ref, sin_ref, mixer_ref, kv_ref, q_ref = refs
    heads = kv_ref.shape[0]
    normed, _ = normalize(pick(hids, blk).astype(f32))
    mixer = (normed * gains_ref[0:1] + gains_ref[1:2]).astype(bf16)
    mixer_ref[...] = mixer
    proj = mm(mixer, w_ref[...]) + bias_ref[...]
    cos_rows, sin_rows = rotation_rows(cos_ref[...], sin_ref[...])
    lane = lax.broadcasted_iota(jnp.int32, (TR, 128), 1)
    for h in range(heads):
        kv_ref[h] = rotate(proj[:, h * 128 : (h + 1) * 128], cos_rows, sin_rows).astype(bf16)
        at = heads * 128 + (h // 2) * 128
        x = proj[:, at : at + 128]
        if h % 2:
            x = pltpu.roll(x, HD, 1)
        x = jnp.where(lane < HD, rotate(x, cos_rows, sin_rows) * (1.0 / math.sqrt(HD)), 0.0)
        q_ref[h] = x.astype(bf16)


def pre(hids, gains, w, bias, cos, sin, heads):
    blk, D = hids[0].shape
    T = blk * len(hids)
    return pl.pallas_call(
        functools.partial(pre_kernel, pieces=len(hids), blk=blk),
        grid=(T // TR,),
        in_specs=piece_specs(len(hids), blk, D) + [
            whole_spec(gains.shape),
            whole_spec(w.shape),
            whole_spec(bias.shape),
            pl.BlockSpec((8, TR), lambda i: (0, i)),
            pl.BlockSpec((8, TR), lambda i: (0, i)),
        ],
        out_specs=[rows_spec(D)] + [heads_spec(heads)] * 2,
        out_shape=[jax.ShapeDtypeStruct((T, D), bf16)] + [jax.ShapeDtypeStruct((heads, T, 128), bf16)] * 2,
        compiler_params=pltpu.CompilerParams(vmem_limit_bytes=VMEM_LIMIT),
        cost_estimate=cost(0.5),
        name="pre",
    )(*hids, gains, w, bias, cos, sin)


def gelu_parts(h):
    mag = jnp.abs(h) * (1.0 / math.sqrt(2.0))
    t = 1.0 / (1.0 + 0.3275911 * mag)
    poly = t * (0.254829592 + t * (-0.284496736 + t * (1.421413741 + t * (-1.453152027 + t * 1.061405429))))
    bell = jnp.exp(-0.5 * h * h)
    tail = 0.5 * poly * bell
    return (jnp.where(h >= 0, 1.0 - tail, tail), bell * (1.0 / math.sqrt(2.0 * math.pi)))


def store_halves(total, high, chunk, send_ref, keep_ref):
    count = total.shape[0] // chunk
    low, top = (
        jnp.concatenate([total[n * chunk : (n + 1) * chunk] for n in range(side, count, 2)], axis=0) for side in (0, 1)
    )
    send_ref[: total.shape[0] // 2] = jnp.where(high == 1, low, top).astype(bf16)
    keep_ref[...] = jnp.where(high == 1, top, low).astype(bf16)


def ffn_kernel(*refs, pieces, blk, chunk):
    hids, gs, refs = refs[:pieces], refs[pieces : 2 * pieces], refs[2 * pieces :]
    gains_ref, up_ref, down_ref, qkv_ref, bias_ref, high_ref, normed_ref, g_ref, branch_ref, back_ref, do_ref, send_ref, keep_ref, sums_ref, acc_ref = refs
    heads = do_ref.shape[0]
    F = bias_ref.shape[1]
    step = pl.program_id(0)
    normed, _ = normalize(pick(hids, blk).astype(f32))
    normed_ref[...] = normed.astype(bf16)
    feed = (normed * gains_ref[0:1] + gains_ref[1:2]).astype(bf16)
    g = pick(gs, blk)
    g_ref[...] = g
    up, down = up_ref[...], down_ref[:, :F]
    hidden = mm(feed, up) + bias_ref[...]
    cumulative, density = gelu_parts(hidden)
    act = (hidden * cumulative).astype(bf16)
    hg = (mm(g, down) * (cumulative + hidden * density)).astype(bf16)
    branch_ref[...] = mm(act, down, NT).astype(bf16)
    back = mm(hg, up, NT)
    back_ref[...] = (back * gains_ref[0:1]).astype(bf16)

    @pl.when(step == 0)
    def _():
        sums_ref[...] = jnp.zeros_like(sums_ref)
        acc_ref[...] = jnp.zeros_like(acc_ref)

    acc_ref[:, :F] += mm(feed, hg, TN)
    acc_ref[:, F:] += mm(g, act, TN)
    sums_ref[3:4] += jnp.sum(back * normed, axis=0, keepdims=True)
    sums_ref[4:5] += jnp.sum(back, axis=0, keepdims=True)
    sums_ref[5:6] += jnp.sum(hg.astype(f32), axis=0, keepdims=True)

    @pl.when(step < blk // FR)
    def _():
        sums_ref[6:7] += jnp.sum(g.astype(f32), axis=0, keepdims=True)

    @pl.when(step == pl.num_programs(0) - 1)
    def _():
        store_halves(acc_ref[...], high_ref[0], chunk, send_ref, keep_ref)

    do = jnp.concatenate([mm(g, qkv_ref[...]), mm(g, down_ref[:, F:])], axis=1)
    lane = lax.broadcasted_iota(jnp.int32, (FR, 128), 1)
    for h in range(heads):
        at = HD * (h + 1)
        x = do[:, at // 128 * 128 : at // 128 * 128 + 128]
        if at % 128 == 0:
            x = pltpu.roll(x, HD, 1)
        do_ref[h] = jnp.where(lane < HD, 0.0, x).astype(bf16)


def ffn(hids, gs, gains, up, down, qkv, bias, high, heads, chunk):
    blk, D = gs[0].shape
    T = blk * len(gs)
    F = bias.shape[1]
    rows = rows_spec(D, FR)
    return pl.pallas_call(
        functools.partial(ffn_kernel, pieces=len(gs), blk=blk, chunk=chunk),
        grid=(T // FR,),
        in_specs=piece_specs(len(gs), blk, D, FR) * 2
        + [whole_spec(gains.shape), whole_spec(up.shape), whole_spec(down.shape)]
        + [pl.BlockSpec((D, 128), lambda i: (0, qkv.shape[1] // 128 - 1)), whole_spec(bias.shape)]
        + [pl.BlockSpec(memory_space=pltpu.SMEM)],
        out_specs=[rows] * 4 + [heads_spec(heads, 128, FR)] + [whole_spec((D // 2, 2 * F))] * 2 + [whole_spec((8, D))],
        out_shape=[jax.ShapeDtypeStruct((T, D), bf16)] * 4
        + [
            jax.ShapeDtypeStruct((heads, T, 128), bf16),
            jax.ShapeDtypeStruct((D // 2, 2 * F), bf16),
            jax.ShapeDtypeStruct((D // 2, 2 * F), bf16),
            jax.ShapeDtypeStruct((8, D), f32),
        ],
        scratch_shapes=[pltpu.VMEM((D, 2 * F), f32)],
        compiler_params=pltpu.CompilerParams(vmem_limit_bytes=VMEM_LIMIT),
        cost_estimate=cost(0.5),
        name="ffn",
    )(*hids, *gs, gains, up, down, qkv, bias, high)


def attn_kernel(*refs, T, blk, heads, late):
    if late:
        (place_ref, first_ref, start_ref, tail_ref, kv_ref, q_ref, do_ref, cos_ref, sin_ref, carry_ref, o_in, dq_in,
         o_ref, dq_ref, dtail_ref, low_ref, high_ref, *refs) = refs
    else:
        (place_ref, first_ref, start_ref, tail_ref, kv_ref, q_ref, do_ref, cos_ref, sin_ref,
         o_ref, dq_ref, dtail_ref, carry_ref, *refs) = refs
    kv_scr, dkv_scr, s_scr, dp_scr, o_acc, dq_acc, qd_scr = refs
    half = T // 2
    base = half if late else 0
    t = place_ref[0]
    inner = (t & 1) * blk
    H = range(heads)

    def half_at(n):
        return pl.ds(pl.multiple_of((n ^ (t >> 1)) * half, half), half)

    for n, (ref, part) in enumerate([(tail_ref, 1), (kv_ref, 0), (kv_ref, 1)] if late else [(tail_ref, 0), (tail_ref, 1), (kv_ref, 0)]):
        kv_scr[:, n * half : (n + 1) * half] = ref[:, half_at(part), :]
    if late:
        dkv_scr[:, :T] = carry_ref[...]
        dkv_scr[:, T:] = jnp.zeros_like(dkv_scr[:, T:])
        o_ref[:, half_at(0)] = o_in[...]
        dq_ref[:, half_at(0)] = dq_in[...]
    else:
        dkv_scr[...] = jnp.zeros_like(dkv_scr)

    def place(row):
        return (row - base) ^ inner

    def q_tile(qi, c):
        q0 = pl.multiple_of(base + qi * TQ, TQ)
        qr = pl.multiple_of(q0 ^ (t * blk), TQ)
        out = qr if late else pl.multiple_of(place(q0), TQ)
        for h in H:
            qd_scr[h, :TQ] = q_ref[h, pl.ds(qr, TQ), :]
            qd_scr[h, TQ:] = do_ref[h, pl.ds(qr, TQ), :]
        start = start_ref[:, pl.ds(qr, TQ)]
        qidx = q0 + T + lax.broadcasted_iota(jnp.int32, (1, TQ), 1)
        first = first_ref[base // TQ + qi]
        stop = (q0 + T) // TK + TQ // TK
        count = stop - first

        def over(body, init):
            pairs = count // NK
            state = lax.fori_loop(0, pairs, lambda i, c: body(first + i * NK, c, NK), init)
            return lax.fori_loop(first + pairs * NK, stop, lambda i, c: body(i, c, 1), state)

        def pass1(ki, state, nk):
            rows = nk * TK
            slot = ki - first
            j = ki * TK + lax.broadcasted_iota(jnp.int32, (rows, TQ), 0)
            ok = (j >= start) & (j <= qidx)
            ats = [pl.multiple_of(place((ki + n) * TK), TK) for n in range(nk)]
            sdps = [mm(jnp.concatenate([kv_scr[h, pl.ds(at, TK), :] for at in ats], axis=0), qd_scr[h], NT) for h in H]
            stats = []
            for h in H:
                m8, l8, d8 = state[3 * h : 3 * h + 3]
                s = jnp.where(ok, sdps[h][:, :TQ], NEG)
                dp = sdps[h][:, TQ:]
                for n in range(nk):
                    s_scr[slot + n, h] = s[n * TK : (n + 1) * TK]
                    dp_scr[slot + n, h] = dp[n * TK : (n + 1) * TK]
                s3 = s.reshape(rows // 8, 8, TQ)
                m_new = jnp.maximum(m8, jnp.max(s3, axis=0))
                alpha = jnp.exp(m8 - m_new)
                e = jnp.exp(s3 - m_new[None])
                l8 = l8 * alpha + jnp.sum(e, axis=0)
                d8 = d8 * alpha + jnp.sum(e * dp.reshape(rows // 8, 8, TQ), axis=0)
                stats += [m_new, l8, d8]
            return tuple(stats)

        z8 = jnp.zeros((8, TQ), f32)
        state = over(pass1, (jnp.full((8, TQ), NEG, f32), z8, z8) * heads)
        lses, deltas = [], []
        for h in H:
            m8, l8, d8 = state[3 * h : 3 * h + 3]
            m = jnp.max(m8, axis=0, keepdims=True)
            w = jnp.exp(m8 - m)
            total = jnp.sum(l8 * w, axis=0, keepdims=True)
            lses.append(m + jnp.log(total))
            deltas.append(jnp.sum(d8 * w, axis=0, keepdims=True) / total)
        o_acc[...] = jnp.zeros_like(o_acc)
        dq_acc[...] = jnp.zeros_like(dq_acc)

        def pass2(ki, c2, nk):
            slot = ki - first
            ats = [pl.multiple_of(place((ki + n) * TK), TK) for n in range(nk)]
            for h in H:
                dq = dq_acc[h]
                o = o_acc[h]
                for n in range(nk):
                    p = jnp.exp(s_scr[slot + n, h] - lses[h])
                    ds = (p * (dp_scr[slot + n, h] - deltas[h])).astype(bf16)
                    p = p.astype(bf16)
                    dkv_scr[h, pl.ds(ats[n], TK), :] += mm(jnp.concatenate([ds, p], axis=1), qd_scr[h])
                    kvt = kv_scr[h, pl.ds(ats[n], TK), :].T
                    dq += mm(kvt[:HD], ds)
                    o += mm(kvt[HD:], p)
                dq_acc[h] = dq
                o_acc[h] = o
            return c2

        over(pass2, 0)
        cos = cos_ref[:, pl.ds(qr, TQ)]
        sin = sin_ref[:, pl.ds(qr, TQ)]
        for h in H:
            o_ref[h * HD : (h + 1) * HD, pl.ds(out, TQ)] = o_acc[h].astype(bf16)
            dq = dq_acc[h] * (1.0 / math.sqrt(HD))
            a, b = dq[: ROT // 2], dq[ROT // 2 : ROT]
            dq = jnp.concatenate([a * cos + b * sin, b * cos - a * sin, dq[ROT:]], axis=0)
            dq_ref[h * HD : (h + 1) * HD, pl.ds(out, TQ)] = dq.astype(bf16)
        return c

    lax.fori_loop(0, half // TQ, q_tile, 0)
    dtail_ref[...] = dkv_scr[:, :half].astype(bf16)
    if late:
        low_ref[...] = dkv_scr[:, half:T]
        high_ref[...] = dkv_scr[:, T:]
    else:
        carry_ref[...] = dkv_scr[:, half:]


def attention(place, first, start, tail, kv, q, do, cos, sin, blk, early=()):
    heads, T, _ = q.shape
    W = heads * HD
    late = len(early) > 0
    vmem = pl.BlockSpec(memory_space=pltpu.VMEM)
    smem = pl.BlockSpec(memory_space=pltpu.SMEM)
    slots = DOC_MOST // TK + TQ // TK
    span = T if late else T // 2
    outs = [((W, span), bf16), ((W, span), bf16), ((heads, T // 2, 128), bf16)]
    outs += [((heads, T // 2, 128), f32)] * 2 if late else [((heads, T, 128), f32)]
    return pl.pallas_call(
        functools.partial(attn_kernel, T=T, blk=blk, heads=heads, late=late),
        in_specs=[smem, smem] + [vmem] * (7 + len(early)),
        out_specs=[vmem] * len(outs),
        scratch_shapes=[
            pltpu.VMEM((heads, T + T // 2, 128), bf16),
            pltpu.VMEM((heads, T + T // 2, 128), f32),
            pltpu.VMEM((slots, heads, TK, TQ), f32),
            pltpu.VMEM((slots, heads, TK, TQ), f32),
            pltpu.VMEM((heads, HD, TQ), f32),
            pltpu.VMEM((heads, HD, TQ), f32),
            pltpu.VMEM((heads, 2 * TQ, 128), bf16),
        ],
        out_shape=[jax.ShapeDtypeStruct(*out) for out in outs],
        compiler_params=pltpu.CompilerParams(vmem_limit_bytes=40 * 2**20),
        cost_estimate=cost(0.1),
        name="attn",
    )(place, first, start, tail, kv, q, do, cos, sin, *early)


def mid_kernel(o_ref, dq_ref, mixer_ref, g_ref, branch_ref, qkv_ref, down_ref, kept_ref, sent_ref, grad_ref, acc_ref):
    W = o_ref.shape[0]
    pad = qkv_ref.shape[1] - HD
    step = pl.program_id(0)
    o = o_ref[...]
    rows = jnp.concatenate([jnp.zeros((pad, o.shape[1]), f32), o.astype(f32)], axis=0).T.astype(bf16)
    out = mm(rows[:, : pad + HD], qkv_ref[...], NT) + mm(rows[:, pad + HD :], down_ref[...], NT)
    out = (out + branch_ref[...].astype(f32)).astype(bf16)
    kept_ref[...], sent_ref[...] = out[: MR // 2], out[MR // 2 :]

    @pl.when(step == 0)
    def _():
        acc_ref[...] = jnp.zeros_like(acc_ref)

    acc_ref[:W] += mm(dq_ref[...], mixer_ref[...])
    acc_ref[W:] += mm(o, g_ref[...])

    @pl.when(step == pl.num_programs(0) - 1)
    def _():
        grad_ref[...] = acc_ref[...].T.astype(bf16)


def mid(o, dq, mixer, g, branch, qkv, down):
    T, D = mixer.shape
    W = o.shape[0]
    cols = pl.BlockSpec((W, MR), lambda i: (0, i))
    rows = rows_spec(D, MR)
    rest = W - HD
    return pl.pallas_call(
        mid_kernel,
        grid=(T // MR,),
        in_specs=[
            cols, cols, rows, rows, rows,
            pl.BlockSpec((D, 128), lambda i: (0, qkv.shape[1] // 128 - 1)),
            pl.BlockSpec((D, rest), lambda i: (0, down.shape[1] // rest - 1)),
        ],
        out_specs=[rows_spec(D, MR // 2)] * 2 + [whole_spec((D, 2 * W))],
        out_shape=[jax.ShapeDtypeStruct((T // 2, D), bf16)] * 2 + [jax.ShapeDtypeStruct((D, 2 * W), bf16)],
        scratch_shapes=[pltpu.VMEM((2 * W, D), f32)],
        compiler_params=pltpu.CompilerParams(vmem_limit_bytes=VMEM_LIMIT),
        cost_estimate=cost(0.1),
        name="mid",
    )(o, dq, mixer, g, branch, qkv, down)


def post_kernel(place_ref, dkv_ref, ahead_ref, dq_ref, cos_ref, sin_ref, normed_ref, mixer_ref, back_ref, gain_ref, w_ref, *refs, chunk):
    heads = dkv_ref.shape[0]
    W = heads * HD
    step = pl.program_id(0)
    late = chunk is not None
    if late:
        _, _, acc_in, sums_in, mid_ref, kept_ref, sent_ref, send_ref, keep_ref, sums_ref, acc_ref = refs
    else:
        acc_in = None
        sums_in, kept_ref, sent_ref, grad_ref, sums_ref, acc_ref = refs

    @pl.when(step == 0)
    def _():
        sums_ref[...] = sums_in[...]
        acc_ref[...] = jnp.zeros_like(acc_ref) if acc_in is None else acc_in[...]

    cos_rows, sin_rows = rotation_rows(cos_ref[...], sin_ref[...])
    kv = jnp.concatenate(
        [rotate(dkv_ref[h] + ahead_ref[h].astype(f32), cos_rows, -sin_rows).astype(bf16) for h in range(heads)], axis=1
    )
    acc_ref[...] += mm(mixer_ref[...], kv, TN)
    dq = dq_ref[...].astype(f32).T.astype(bf16)
    part = mm(kv, w_ref[:, : 2 * W], NT) + mm(dq, w_ref[:, 2 * W : 3 * W], NT)
    hat = (part * gain_ref[...] + back_ref[...].astype(f32)).astype(bf16)
    kept_ref[...], sent_ref[...] = hat[: PR // 2], hat[PR // 2 :]
    sums_ref[0:1] += jnp.sum(part * normed_ref[...].astype(f32), axis=0, keepdims=True)
    sums_ref[1:2] += jnp.sum(part, axis=0, keepdims=True)
    sums_ref[2:3, : 2 * W] += jnp.sum(kv.astype(f32), axis=0, keepdims=True)
    sums_ref[2:3, 2 * W : 3 * W] += jnp.sum(dq.astype(f32), axis=0, keepdims=True)

    @pl.when(step == pl.num_programs(0) - 1)
    def _():
        if late:
            total = jnp.concatenate([acc_ref[...], mid_ref[...].astype(f32)], axis=1)
            store_halves(total, place_ref[1], chunk, send_ref, keep_ref)
            one = sums_ref[...].astype(bf16).astype(f32)
            two = (sums_ref[...] - one).astype(bf16).astype(f32)
            sums_ref[...] = one + two
            send_ref[total.shape[0] // 2 :] = jnp.concatenate([one, two], axis=0).astype(bf16)
        else:
            grad_ref[...] = acc_ref[...]


def post(part, place, dkv, ahead, dq, cos, sin, normed, mixer, back, gain, w, early=(), chunk=None):
    T, D = mixer.shape
    heads = dkv.shape[0]
    W = heads * HD
    per = T // 2 // PR

    def at(i, place):
        return (part ^ (place[0] >> 1)) * per + i

    def inner(i, place):
        return i

    def rows(index):
        return pl.BlockSpec((PR, D), lambda i, place: (index(i, place), 0))

    def cols(count):
        return pl.BlockSpec((count, PR), lambda i, place: (0, at(i, place)))

    def fixed(shape):
        return pl.BlockSpec(shape, lambda i, place: (0,) * len(shape))

    half = pl.BlockSpec((heads, PR, 128), lambda i, place: (0, i, 0))
    late = len(early) > 1
    specs = [half, half, cols(W), cols(8), cols(8), rows(at), rows(at), rows(at), fixed(gain.shape), fixed(w.shape)]
    if late:
        specs += [pl.BlockSpec(memory_space=pl.ANY)] * 2 + [fixed((D, 2 * W)), fixed((8, D)), fixed((D, 2 * W))]
        grads = [fixed((D // 2 + 16, 4 * W)), fixed((D // 2, 4 * W))]
        shapes = [jax.ShapeDtypeStruct((D // 2 + 16, 4 * W), bf16), jax.ShapeDtypeStruct((D // 2, 4 * W), bf16)]
    else:
        specs += [fixed((8, D))]
        grads = [fixed((D, 2 * W))]
        shapes = [jax.ShapeDtypeStruct((D, 2 * W), f32)]
    return pl.pallas_call(
        functools.partial(post_kernel, chunk=chunk),
        grid_spec=pltpu.PrefetchScalarGridSpec(
            num_scalar_prefetch=1,
            grid=(per,),
            in_specs=specs,
            out_specs=[pl.BlockSpec((PR // 2, D), lambda i, place: (at(i, place), 0))] * 2 + grads + [fixed((8, D))],
            scratch_shapes=[pltpu.VMEM((D, 2 * W), f32)],
        ),
        out_shape=[
            jax.ShapeDtypeStruct((T // 2, D), bf16),
            jax.ShapeDtypeStruct((T // 2, D), bf16),
            *shapes,
            jax.ShapeDtypeStruct((8, D), f32),
        ],
        input_output_aliases={11: 0, 12: 1} if late else {},
        compiler_params=pltpu.CompilerParams(vmem_limit_bytes=VMEM_LIMIT),
        cost_estimate=cost(8 if late else 0.1),
        name="post",
    )(place, dkv, ahead, dq, cos, sin, normed, mixer, back, gain, w, *early)


def mix_finish_kernel(keep_ref, other_ref, own_ref, triple_ref, out_ref, sums_ref):
    rows = keep_ref.shape[0]
    W = out_ref.shape[0]
    other = other_ref[...].astype(f32)
    total = keep_ref[...] + other[:rows]
    sums_ref[...] = own_ref[...] + (other[rows : rows + 8] + other[rows + 8 :])
    triple_ref[0] = total[:, 2 * W : 3 * W]
    for n in range(2):
        triple_ref[1 + n] = jnp.concatenate(
            [total[:, at + n * HD : at + (n + 1) * HD] for at in range(0, 2 * W, 2 * HD)], axis=1
        )
    out_ref[...] = total[:, 3 * W :].T


def mix_finish(keep, other, own, W):
    rows = keep.shape[0]
    return pl.pallas_call(
        mix_finish_kernel,
        out_shape=[
            jax.ShapeDtypeStruct((3, rows, W), f32),
            jax.ShapeDtypeStruct((W, rows), f32),
            jax.ShapeDtypeStruct(own.shape, f32),
        ],
        cost_estimate=cost(0.1),
        name="mix_finish",
    )(keep, other, own)


def ffn_finish_kernel(keep_ref, other_ref, up_ref, down_ref):
    F = up_ref.shape[1]
    total = keep_ref[...] + other_ref[...].astype(f32)
    up_ref[...] = total[:, :F]
    down_ref[...] = total[:, F:]


def ffn_finish(keep, other):
    rows, cols = keep.shape
    F = cols // 2
    return pl.pallas_call(
        ffn_finish_kernel,
        out_shape=[jax.ShapeDtypeStruct((rows, F), f32)] * 2,
        cost_estimate=cost(0.1),
        name="ffn_finish",
    )(keep, other)


def shards(
    hidden_in, positions, mixer_gain, mixer_shift, feed_gain, feed_shift, triple_weight,
    pair_bias, output_weight, up_weight, up_bias, down_weight, out_bias, out_grad,
):
    T = positions.shape[0]
    blk, D = hidden_in.shape
    W = pair_bias.shape[1]
    heads = W // HD
    chunk = triple_weight.shape[0]
    t = lax.axis_index("tensor").astype(jnp.int32)

    F = up_weight.shape[1]
    bits = bit_count("dp")
    down_order = list(reversed(range(bits)))
    mixed_order = down_order[:-2] + [0, 1]
    q_w, k_w, v_w = (triple_weight[:, i].reshape(chunk, heads, HD) for i in range(3))
    kv_w = jnp.concatenate([k_w, v_w], axis=2).reshape(chunk, 2 * W)
    pad = (-W) % 128
    out_own = output_weight.T
    up_w, up_parts = gather_dp(up_weight, down_order)
    qkv_own = jnp.concatenate([kv_w, q_w.reshape(chunk, W), out_own[:, :pad]], axis=1)
    qkv_w, qkv_parts = gather_dp(qkv_own, down_order, [up_parts[0]])
    hids = gather_tensor(hidden_in)
    gs = gather_tensor(after(out_grad, hids[2]))

    pos = jnp.concatenate([lax.dynamic_slice(positions, ((r ^ t) * blk,), (blk,)) for r in range(T // blk)])
    inverse = 1.0 / 10000.0 ** (jnp.arange(ROT // 2, dtype=f32) * (2.0 / ROT))
    angles = pos.astype(f32)[None, :] * inverse[:, None]
    cos, sin = jnp.cos(angles), jnp.sin(angles)
    rows = jnp.arange(T, dtype=jnp.int32) ^ (t * blk)
    start = (rows + T - pos)[None]
    q_starts = jnp.arange(0, T, TQ, dtype=jnp.int32)
    first = (q_starts + T - positions[::TQ]) // TK

    gains = jnp.stack([mixer_gain, mixer_shift, feed_gain, feed_shift])
    v_bias = pair_bias[1].reshape(heads, HD)
    kv_bias = jnp.concatenate([jnp.zeros_like(v_bias), v_bias], axis=1).reshape(2 * W)
    bias = jnp.concatenate([kv_bias, pair_bias[0], jnp.zeros((pad,), f32)])[None]
    high = (lax.axis_index("dp") & 1).astype(jnp.int32)
    spots = jnp.stack([t, high])
    mixer_in, kv, q = pre(hids, gains, qkv_w, bias, cos, sin, heads)
    feed_gains, feed_bias = gains[2:], up_bias[None]
    early_ops = (feed_gains, feed_bias, first, start)
    down_own = jnp.concatenate([down_weight.T, out_own[:, pad:]], axis=1)
    down_w, _ = gather_dp(down_own, down_order, [qkv_parts[-2]] + [None] * (bits - 2) + [(gs[2], up_w, early_ops)])
    tail = shift(after(kv, down_w), "dp", 1)
    normed, g, branch, back, do, ffn_send, ffn_keep, ffn_sums = ffn(
        hids, gs, feed_gains, up_w, down_w, qkv_w, feed_bias, high[None], heads, chunk
    )
    attn_args = (spots, first, start, tail, kv, q, do, cos, sin, blk)
    *early, dtail_low, carry = attention(*attn_args)
    ahead_low = shift(dtail_low, "dp", -1)
    ffn_order = down_order[::-1]
    ffn_other = swap(after(ffn_send, tail), "dp", 1 << ffn_order[0])
    o, dq, dtail_high, dkv_low, dkv_high = attention(*attn_args, early=(carry, *early))
    ahead_high = shift(after(dtail_high, ahead_low, ffn_other), "dp", -1)
    post_args = (dq, cos, sin, normed, mixer_in, back, mixer_gain[None], qkv_w)
    ffn_first = ffn_keep.astype(f32) + ffn_other.astype(f32)
    ffn_send, ffn_keep = halves(ffn_first, chunk, ffn_order[1:], ffn_order[1])
    ffn_other = swap(ffn_send, "dp", 1 << ffn_order[1])
    early = post(0, spots, dkv_low, after(ahead_low, ffn_first), *post_args, early=(ffn_sums,))
    *branch, mid_grad = mid(after(o, early[3]), dq, mixer_in, g, branch, qkv_w, down_w)
    *hat, mix_send, mix_keep, sums = post(
        1, spots, dkv_high, ahead_high, *post_args, early=(*early, mid_grad), chunk=chunk
    )
    mix_order = ffn_order
    *hat, mix_send, mix_keep, sums, ffn_other = lax.optimization_barrier((*hat, mix_send, mix_keep, sums, ffn_other))
    mix_other = swap(mix_send, "dp", 1 << mix_order[0])
    hat_own, far = scatter_core(*hat)
    landed_far = swap(far, "tensor", 2)
    branch_own, branch_far = scatter_core(*branch)
    branch_across = swap(after(branch_far, landed_far), "tensor", 2)
    ffn_grads = ffn_keep.astype(f32) + after(ffn_other, far).astype(f32)
    for n in range(2, bits):
        ffn_send, ffn_keep = halves(ffn_grads, chunk, ffn_order[n:], ffn_order[n])
        ffn_other = swap(ffn_send, "dp", 1 << ffn_order[n])
        ffn_grads = ffn_keep.astype(f32) + ffn_other.astype(f32)
    mix_other = after(mix_other, far, branch_far, ffn_send).astype(f32)
    mix_grads = mix_keep.astype(f32) + mix_other[: mix_keep.shape[0]]
    sums = sums + (mix_other[-16:-8] + mix_other[-8:])
    for n in range(1, bits - 1):
        mix_grads, sums = scatter_step(mix_grads, chunk, mix_order[n:], mix_order[n], landed_far if n == 1 else None, sums)
    mix_send, mix_keep = halves(mix_grads, chunk, mix_order[-1:], mix_order[-1])
    one, two = two_parts(sums)
    mix_send = jnp.concatenate([mix_send, one.astype(bf16), two.astype(bf16)], axis=0)
    mix_other = swap(mix_send, "dp", 1 << mix_order[-1])
    ffn_other = after(ffn_other, mix_send)
    up_grad, down_grad = ffn_finish(ffn_keep, ffn_other)
    grad_hat = hat_own + after(landed_far, mix_send).astype(f32)
    own, inv_std = normalize(hidden_in.astype(f32))
    first_mean = jnp.mean(grad_hat, axis=-1, keepdims=True)
    second_mean = jnp.mean(grad_hat * own, axis=-1, keepdims=True)
    grad_hidden = out_grad.astype(f32) + inv_std * (grad_hat - first_mean - own * second_mean)
    mix_other = after(mix_other, up_grad, grad_hidden)
    triple_grad, out_grad_t, sums = mix_finish(mix_keep, mix_other, one + two, W)
    result = hidden_in.astype(f32) + branch_own + after(branch_across, sums).astype(f32) + out_bias
    norm_sums = sums + swap(sums, "tensor", 1)
    norm_sums = norm_sums + swap(norm_sums, "tensor", 2)
    head_sums = sums[2, : 2 * W].reshape(heads, 2, HD)[:, 1].reshape(W)
    pair_grad = jnp.stack([sums[2, 2 * W : 3 * W], head_sums])
    return (
        result,
        grad_hidden,
        norm_sums[0],
        norm_sums[1],
        norm_sums[3],
        norm_sums[4],
        jnp.transpose(triple_grad, (1, 0, 2)),
        pair_grad,
        out_grad_t,
        up_grad,
        sums[5],
        down_grad.T,
        norm_sums[6],
    )


def solution(mesh):
    rows = P(("dp", "tensor"), None)
    in_specs = (
        rows, P("dp"), P(), P(), P(), P(), P("dp", None, "tensor"), P(None, "tensor"), P("tensor", "dp"),
        P("dp", "tensor"), P("tensor"), P("tensor", "dp"), P(), rows,
    )
    out_specs = (
        rows, rows, P(), P(), P(), P(), P("dp", None, "tensor"), P(None, "tensor"), P("tensor", "dp"),
        P("dp", "tensor"), P("tensor"), P("tensor", "dp"), P(),
    )
    return jax.shard_map(shards, mesh=mesh, in_specs=in_specs, out_specs=out_specs, check_vma=False)
```

```python
import functools
import math

import jax
import jax.numpy as jnp
from jax import lax
from jax.experimental import pallas as pl
from jax.experimental.pallas import tpu as pltpu
from jax.sharding import PartitionSpec as P

HD = 64
ROT = 16
DOC_MOST = 2048
EPSILON = 1e-05
NEG = -1e30
TQ = 256
TK = 256
NK = 2
TR = 512
FR = 512
PR = 1024
MR = 1024
bf16 = jnp.bfloat16
f32 = jnp.float32
NN = (((1,), (0,)), ((), ()))
NT = (((1,), (1,)), ((), ()))
TN = (((0,), (0,)), ((), ()))
TT = (((0,), (1,)), ((), ()))
VMEM_LIMIT = 56 * 2**20


def cost(us):
    return pl.CostEstimate(flops=int(us * 1.15e9), bytes_accessed=1000, transcendentals=0)


def mm(left, right, dims=NN):
    return lax.dot_general(left, right, dims, preferred_element_type=f32)


def swap(value, axis, mask):
    count = lax.axis_size(axis)
    return lax.ppermute(value, axis, [(i, i ^ mask) for i in range(count)])


def shift(value, axis, distance):
    count = lax.axis_size(axis)
    route = [(i, i + distance) for i in range(count) if 0 <= i + distance < count]
    return lax.ppermute(value, axis, route)


def bit_count(axis):
    return lax.axis_size(axis).bit_length() - 1


def after(value, *others):
    return lax.optimization_barrier((value, others))[0]


def gather_tensor(own):
    near = swap(own, "tensor", 1)
    far = swap(own, "tensor", 2)
    diagonal = swap(far, "tensor", 1)
    return [own, near, far, diagonal]


def scatter_core(kept, sent):
    near = swap(sent, "tensor", 1).astype(f32)
    total = kept.astype(f32) + near
    rows = kept.shape[0] // 2
    return total[:rows], total[rows:].astype(bf16)


def split(held, rows, left, bit):
    above = 1 << sum(b > bit for b in left)
    return held.reshape(above, 2, -1, held.shape[-1])


def gather_dp(own, order, gates=()):
    me = lax.axis_index("dp")
    rows, cols = own.shape
    held, done = own, []
    parts = []
    for n, bit in enumerate(order):
        if n == 0 and gates and gates[0] is not None:
            held = after(held, gates[0])
        other = swap(held, "dp", 1 << bit)
        if n + 1 < len(gates) and gates[n + 1] is not None:
            other = after(other, gates[n + 1])
        high = ((me >> bit) & 1) == 1
        above = 1 << sum(b > bit for b in done)
        one, two = held.reshape(above, -1, cols), other.reshape(above, -1, cols)
        held = jnp.concatenate([jnp.where(high, two, one), jnp.where(high, one, two)], axis=1).reshape(-1, cols)
        done.append(bit)
        parts.append(held)
    return held, parts


def two_parts(sums):
    first = lax.reduce_precision(sums, 8, 7)
    return first, lax.reduce_precision(sums - first, 8, 7)


def halves(held, rows, left, bit):
    cols = held.shape[1]
    pairs = split(held, rows, left, bit)
    high = ((lax.axis_index("dp") >> bit) & 1) == 1
    send = jnp.where(high, pairs[:, 0], pairs[:, 1]).astype(bf16).reshape(-1, cols)
    keep = jnp.where(high, pairs[:, 1], pairs[:, 0]).reshape(-1, cols)
    return send, keep


def scatter_step(held, rows, left, bit, landed=None, sums=None):
    send, keep = halves(held, rows, left, bit)
    count = send.shape[0]
    if sums is not None:
        first, second = two_parts(sums)
        send = jnp.concatenate([send, first.astype(bf16), second.astype(bf16)], axis=0)
    other = swap(send, "dp", 1 << bit)
    if landed is not None:
        other = after(other, landed)
    other = other.astype(f32)
    held = keep.astype(f32) + other[:count]
    if sums is None:
        return held
    return held, (first + second) + (other[count : count + 8] + other[count + 8 :])


def sum_over(value, axis):
    for bit in range(bit_count(axis)):
        value = value + swap(value, axis, 1 << bit)
    return value


def normalize(values):
    centred = values - jnp.mean(values, axis=-1, keepdims=True)
    inv_std = lax.rsqrt(jnp.mean(centred * centred, axis=-1, keepdims=True) + EPSILON)
    return (centred * inv_std, inv_std)


def rows_spec(cols, tile=TR):
    return pl.BlockSpec((tile, cols), lambda i: (i, 0))


def whole_spec(shape):
    return pl.BlockSpec(shape, lambda i: (0,) * len(shape))


def heads_spec(heads, cols=128, tile=TR):
    return pl.BlockSpec((heads, tile, cols), lambda i: (0, i, 0))


def piece_specs(count, rows, cols, tile=TR):
    per = rows // tile
    return [pl.BlockSpec((tile, cols), lambda i, p=p: (jnp.clip(i - p * per, 0, per - 1), 0)) for p in range(count)]


def pick(refs, rows):
    at = pl.program_id(0) // (rows // refs[0].shape[0])
    value = refs[0][...]
    for n, ref in enumerate(refs[1:]):
        value = jnp.where(at == n + 1, ref[...], value)
    return value


def rotation_rows(cos, sin):
    ones = jnp.ones((128 - ROT, cos.shape[1]), f32)
    return jnp.concatenate([cos, cos, ones], axis=0).T, jnp.concatenate([-sin, sin, ones * 0.0], axis=0).T


def rotate(x, cos_rows, sin_rows):
    lane = lax.broadcasted_iota(jnp.int32, x.shape, 1)
    partner = jnp.where(lane < ROT // 2, pltpu.roll(x, 128 - ROT // 2, 1), pltpu.roll(x, ROT // 2, 1))
    return x * cos_rows + partner * sin_rows


def pre_kernel(*refs, pieces, blk):
    hids, refs = refs[:pieces], refs[pieces:]
    gains_ref, w_ref, bias_ref, cos_ref, sin_ref, mixer_ref, kv_ref, q_ref = refs
    heads = kv_ref.shape[0]
    normed, _ = normalize(pick(hids, blk).astype(f32))
    mixer = (normed * gains_ref[0:1] + gains_ref[1:2]).astype(bf16)
    mixer_ref[...] = mixer
    proj = mm(mixer, w_ref[...]) + bias_ref[...]
    cos_rows, sin_rows = rotation_rows(cos_ref[...], sin_ref[...])
    lane = lax.broadcasted_iota(jnp.int32, (TR, 128), 1)
    for h in range(heads):
        kv_ref[h] = rotate(proj[:, h * 128 : (h + 1) * 128], cos_rows, sin_rows).astype(bf16)
        at = heads * 128 + (h // 2) * 128
        x = proj[:, at : at + 128]
        if h % 2:
            x = pltpu.roll(x, HD, 1)
        x = jnp.where(lane < HD, rotate(x, cos_rows, sin_rows) * (1.0 / math.sqrt(HD)), 0.0)
        q_ref[h] = x.astype(bf16)


def pre(hids, gains, w, bias, cos, sin, heads):
    blk, D = hids[0].shape
    T = blk * len(hids)
    return pl.pallas_call(
        functools.partial(pre_kernel, pieces=len(hids), blk=blk),
        grid=(T // TR,),
        in_specs=piece_specs(len(hids), blk, D) + [
            whole_spec(gains.shape),
            whole_spec(w.shape),
            whole_spec(bias.shape),
            pl.BlockSpec((8, TR), lambda i: (0, i)),
            pl.BlockSpec((8, TR), lambda i: (0, i)),
        ],
        out_specs=[rows_spec(D)] + [heads_spec(heads)] * 2,
        out_shape=[jax.ShapeDtypeStruct((T, D), bf16)] + [jax.ShapeDtypeStruct((heads, T, 128), bf16)] * 2,
        compiler_params=pltpu.CompilerParams(vmem_limit_bytes=40 * 2**20),
        cost_estimate=cost(0.5),
        name="pre",
    )(*hids, gains, w, bias, cos, sin)


def gelu_parts(h):
    mag = jnp.abs(h) * (1.0 / math.sqrt(2.0))
    t = 1.0 / (1.0 + 0.3275911 * mag)
    poly = t * (0.254829592 + t * (-0.284496736 + t * (1.421413741 + t * (-1.453152027 + t * 1.061405429))))
    bell = jnp.exp(-0.5 * h * h)
    tail = 0.5 * poly * bell
    return (jnp.where(h >= 0, 1.0 - tail, tail), bell * (1.0 / math.sqrt(2.0 * math.pi)))


def store_halves(total, high, chunk, send_ref, keep_ref):
    count = total.shape[0] // chunk
    low, top = (
        jnp.concatenate([total[n * chunk : (n + 1) * chunk] for n in range(side, count, 2)], axis=0) for side in (0, 1)
    )
    send_ref[: total.shape[0] // 2] = jnp.where(high == 1, low, top).astype(bf16)
    keep_ref[...] = jnp.where(high == 1, top, low).astype(bf16)


def ffn_kernel(*refs, pieces, blk, chunk):
    hids, gs, refs = refs[:pieces], refs[pieces : 2 * pieces], refs[2 * pieces :]
    gains_ref, up_ref, down_ref, qkv_ref, bias_ref, high_ref, normed_ref, g_ref, branch_ref, back_ref, do_ref, send_ref, keep_ref, sums_ref, acc_ref = refs
    heads = do_ref.shape[0]
    F = bias_ref.shape[1]
    step = pl.program_id(0)
    normed, _ = normalize(pick(hids, blk).astype(f32))
    normed_ref[...] = normed.astype(bf16)
    feed = (normed * gains_ref[0:1] + gains_ref[1:2]).astype(bf16)
    g = pick(gs, blk)
    g_ref[...] = g
    up, down = up_ref[...], down_ref[:, :F]
    hidden = mm(feed, up) + bias_ref[...]
    cumulative, density = gelu_parts(hidden)
    act = (hidden * cumulative).astype(bf16)
    hg = (mm(g, down) * (cumulative + hidden * density)).astype(bf16)
    branch_ref[...] = mm(act, down, NT).astype(bf16)
    back = mm(hg, up, NT)
    back_ref[...] = (back * gains_ref[0:1]).astype(bf16)

    @pl.when(step == 0)
    def _():
        sums_ref[...] = jnp.zeros_like(sums_ref)
        acc_ref[...] = jnp.zeros_like(acc_ref)

    acc_ref[:, :F] += mm(feed, hg, TN)
    acc_ref[:, F:] += mm(g, act, TN)
    sums_ref[3:4] += jnp.sum(back * normed, axis=0, keepdims=True)
    sums_ref[4:5] += jnp.sum(back, axis=0, keepdims=True)
    sums_ref[5:6] += jnp.sum(hg.astype(f32), axis=0, keepdims=True)

    @pl.when(step < blk // FR)
    def _():
        sums_ref[6:7] += jnp.sum(g.astype(f32), axis=0, keepdims=True)

    @pl.when(step == pl.num_programs(0) - 1)
    def _():
        store_halves(acc_ref[...], high_ref[0], chunk, send_ref, keep_ref)

    do = jnp.concatenate([mm(g, qkv_ref[...]), mm(g, down_ref[:, F:])], axis=1)
    lane = lax.broadcasted_iota(jnp.int32, (FR, 128), 1)
    for h in range(heads):
        at = HD * (h + 1)
        x = do[:, at // 128 * 128 : at // 128 * 128 + 128]
        if at % 128 == 0:
            x = pltpu.roll(x, HD, 1)
        do_ref[h] = jnp.where(lane < HD, 0.0, x).astype(bf16)


def ffn(hids, gs, gains, up, down, qkv, bias, high, heads, chunk):
    blk, D = gs[0].shape
    T = blk * len(gs)
    F = bias.shape[1]
    rows = rows_spec(D, FR)
    return pl.pallas_call(
        functools.partial(ffn_kernel, pieces=len(gs), blk=blk, chunk=chunk),
        grid=(T // FR,),
        in_specs=piece_specs(len(gs), blk, D, FR) * 2
        + [whole_spec(gains.shape), whole_spec(up.shape), whole_spec(down.shape)]
        + [pl.BlockSpec((D, 128), lambda i: (0, qkv.shape[1] // 128 - 1)), whole_spec(bias.shape)]
        + [pl.BlockSpec(memory_space=pltpu.SMEM)],
        out_specs=[rows] * 4 + [heads_spec(heads, 128, FR)] + [whole_spec((D // 2, 2 * F))] * 2 + [whole_spec((8, D))],
        out_shape=[jax.ShapeDtypeStruct((T, D), bf16)] * 4
        + [
            jax.ShapeDtypeStruct((heads, T, 128), bf16),
            jax.ShapeDtypeStruct((D // 2, 2 * F), bf16),
            jax.ShapeDtypeStruct((D // 2, 2 * F), bf16),
            jax.ShapeDtypeStruct((8, D), f32),
        ],
        scratch_shapes=[pltpu.VMEM((D, 2 * F), f32)],
        compiler_params=pltpu.CompilerParams(vmem_limit_bytes=VMEM_LIMIT),
        cost_estimate=cost(0.5),
        name="ffn",
    )(*hids, *gs, gains, up, down, qkv, bias, high)


def attn_kernel(*refs, T, blk, heads, late):
    if late:
        (place_ref, first_ref, start_ref, tail_ref, kv_ref, q_ref, do_ref, cos_ref, sin_ref, carry_ref, o_in, dq_in,
         o_ref, dq_ref, dtail_ref, low_ref, high_ref, *refs) = refs
    else:
        (place_ref, first_ref, start_ref, tail_ref, kv_ref, q_ref, do_ref, cos_ref, sin_ref,
         o_ref, dq_ref, dtail_ref, carry_ref, *refs) = refs
    kv_scr, dkv_scr, s_scr, dp_scr, o_acc, dq_acc, qd_scr = refs
    half = T // 2
    base = half if late else 0
    t = place_ref[0]
    inner = (t & 1) * blk
    H = range(heads)

    def half_at(n):
        return pl.ds(pl.multiple_of((n ^ (t >> 1)) * half, half), half)

    for n, (ref, part) in enumerate([(tail_ref, 1), (kv_ref, 0), (kv_ref, 1)] if late else [(tail_ref, 0), (tail_ref, 1), (kv_ref, 0)]):
        kv_scr[:, n * half : (n + 1) * half] = ref[:, half_at(part), :]
    if late:
        dkv_scr[:, :T] = carry_ref[...]
        dkv_scr[:, T:] = jnp.zeros_like(dkv_scr[:, T:])
        o_ref[:, half_at(0)] = o_in[...]
        dq_ref[:, half_at(0)] = dq_in[...]
    else:
        dkv_scr[...] = jnp.zeros_like(dkv_scr)

    def place(row):
        return (row - base) ^ inner

    def q_tile(qi, c):
        q0 = pl.multiple_of(base + qi * TQ, TQ)
        qr = pl.multiple_of(q0 ^ (t * blk), TQ)
        out = qr if late else pl.multiple_of(place(q0), TQ)
        for h in H:
            qd_scr[h, :TQ] = q_ref[h, pl.ds(qr, TQ), :]
            qd_scr[h, TQ:] = do_ref[h, pl.ds(qr, TQ), :]
        start = start_ref[:, pl.ds(qr, TQ)]
        qidx = q0 + T + lax.broadcasted_iota(jnp.int32, (1, TQ), 1)
        first = first_ref[base // TQ + qi]
        stop = (q0 + T) // TK + TQ // TK
        count = stop - first

        def over(body, init):
            pairs = count // NK
            state = lax.fori_loop(0, pairs, lambda i, c: body(first + i * NK, c, NK), init)
            return lax.fori_loop(first + pairs * NK, stop, lambda i, c: body(i, c, 1), state)

        def pass1(ki, state, nk):
            rows = nk * TK
            slot = ki - first
            j = ki * TK + lax.broadcasted_iota(jnp.int32, (rows, TQ), 0)
            ok = (j >= start) & (j <= qidx)
            ats = [pl.multiple_of(place((ki + n) * TK), TK) for n in range(nk)]
            sdps = [mm(jnp.concatenate([kv_scr[h, pl.ds(at, TK), :] for at in ats], axis=0), qd_scr[h], NT) for h in H]
            stats = []
            for h in H:
                m8, l8, d8 = state[3 * h : 3 * h + 3]
                s = jnp.where(ok, sdps[h][:, :TQ], NEG)
                dp = sdps[h][:, TQ:]
                for n in range(nk):
                    s_scr[slot + n, h] = s[n * TK : (n + 1) * TK]
                    dp_scr[slot + n, h] = dp[n * TK : (n + 1) * TK]
                s3 = s.reshape(rows // 8, 8, TQ)
                m_new = jnp.maximum(m8, jnp.max(s3, axis=0))
                alpha = jnp.exp(m8 - m_new)
                e = jnp.exp(s3 - m_new[None])
                l8 = l8 * alpha + jnp.sum(e, axis=0)
                d8 = d8 * alpha + jnp.sum(e * dp.reshape(rows // 8, 8, TQ), axis=0)
                stats += [m_new, l8, d8]
            return tuple(stats)

        z8 = jnp.zeros((8, TQ), f32)
        state = over(pass1, (jnp.full((8, TQ), NEG, f32), z8, z8) * heads)
        lses, deltas = [], []
        for h in H:
            m8, l8, d8 = state[3 * h : 3 * h + 3]
            m = jnp.max(m8, axis=0, keepdims=True)
            w = jnp.exp(m8 - m)
            total = jnp.sum(l8 * w, axis=0, keepdims=True)
            lses.append(m + jnp.log(total))
            deltas.append(jnp.sum(d8 * w, axis=0, keepdims=True) / total)
        o_acc[...] = jnp.zeros_like(o_acc)
        dq_acc[...] = jnp.zeros_like(dq_acc)

        def pass2(ki, c2, nk):
            slot = ki - first
            ats = [pl.multiple_of(place((ki + n) * TK), TK) for n in range(nk)]
            for h in H:
                dq = dq_acc[h]
                o = o_acc[h]
                for n in range(nk):
                    p = jnp.exp(s_scr[slot + n, h] - lses[h])
                    ds = (p * (dp_scr[slot + n, h] - deltas[h])).astype(bf16)
                    p = p.astype(bf16)
                    dkv_scr[h, pl.ds(ats[n], TK), :] += mm(jnp.concatenate([ds, p], axis=1), qd_scr[h])
                    kvt = kv_scr[h, pl.ds(ats[n], TK), :].T
                    dq += mm(kvt[:HD], ds)
                    o += mm(kvt[HD:], p)
                dq_acc[h] = dq
                o_acc[h] = o
            return c2

        over(pass2, 0)
        cos = cos_ref[:, pl.ds(qr, TQ)]
        sin = sin_ref[:, pl.ds(qr, TQ)]
        for h in H:
            o_ref[h * HD : (h + 1) * HD, pl.ds(out, TQ)] = o_acc[h].astype(bf16)
            dq = dq_acc[h] * (1.0 / math.sqrt(HD))
            a, b = dq[: ROT // 2], dq[ROT // 2 : ROT]
            dq = jnp.concatenate([a * cos + b * sin, b * cos - a * sin, dq[ROT:]], axis=0)
            dq_ref[h * HD : (h + 1) * HD, pl.ds(out, TQ)] = dq.astype(bf16)
        return c

    lax.fori_loop(0, half // TQ, q_tile, 0)
    dtail_ref[...] = dkv_scr[:, :half].astype(bf16)
    if late:
        low_ref[...] = dkv_scr[:, half:T]
        high_ref[...] = dkv_scr[:, T:]
    else:
        carry_ref[...] = dkv_scr[:, half:]


def attention(place, first, start, tail, kv, q, do, cos, sin, blk, early=()):
    heads, T, _ = q.shape
    W = heads * HD
    late = len(early) > 0
    vmem = pl.BlockSpec(memory_space=pltpu.VMEM)
    smem = pl.BlockSpec(memory_space=pltpu.SMEM)
    slots = DOC_MOST // TK + TQ // TK
    span = T if late else T // 2
    outs = [((W, span), bf16), ((W, span), bf16), ((heads, T // 2, 128), bf16)]
    outs += [((heads, T // 2, 128), f32)] * 2 if late else [((heads, T, 128), f32)]
    return pl.pallas_call(
        functools.partial(attn_kernel, T=T, blk=blk, heads=heads, late=late),
        in_specs=[smem, smem] + [vmem] * (7 + len(early)),
        out_specs=[vmem] * len(outs),
        scratch_shapes=[
            pltpu.VMEM((heads, T + T // 2, 128), bf16),
            pltpu.VMEM((heads, T + T // 2, 128), f32),
            pltpu.VMEM((slots, heads, TK, TQ), f32),
            pltpu.VMEM((slots, heads, TK, TQ), f32),
            pltpu.VMEM((heads, HD, TQ), f32),
            pltpu.VMEM((heads, HD, TQ), f32),
            pltpu.VMEM((heads, 2 * TQ, 128), bf16),
        ],
        out_shape=[jax.ShapeDtypeStruct(*out) for out in outs],
        compiler_params=pltpu.CompilerParams(vmem_limit_bytes=36 * 2**20),
        cost_estimate=cost(0.1),
        name="attn",
    )(place, first, start, tail, kv, q, do, cos, sin, *early)


def mid_kernel(o_ref, dq_ref, mixer_ref, g_ref, branch_ref, qkv_ref, down_ref, kept_ref, sent_ref, grad_ref, acc_ref):
    W = o_ref.shape[0]
    pad = qkv_ref.shape[1] - HD
    step = pl.program_id(0)
    o = o_ref[...]
    rows = jnp.concatenate([jnp.zeros((pad, o.shape[1]), f32), o.astype(f32)], axis=0).T.astype(bf16)
    out = mm(rows[:, : pad + HD], qkv_ref[...], NT) + mm(rows[:, pad + HD :], down_ref[...], NT)
    out = (out + branch_ref[...].astype(f32)).astype(bf16)
    kept_ref[...], sent_ref[...] = out[: MR // 2], out[MR // 2 :]

    @pl.when(step == 0)
    def _():
        acc_ref[...] = jnp.zeros_like(acc_ref)

    acc_ref[:W] += mm(dq_ref[...], mixer_ref[...])
    acc_ref[W:] += mm(o, g_ref[...])

    @pl.when(step == pl.num_programs(0) - 1)
    def _():
        grad_ref[...] = acc_ref[...].T.astype(bf16)


def mid(o, dq, mixer, g, branch, qkv, down):
    T, D = mixer.shape
    W = o.shape[0]
    cols = pl.BlockSpec((W, MR), lambda i: (0, i))
    rows = rows_spec(D, MR)
    rest = W - HD
    return pl.pallas_call(
        mid_kernel,
        grid=(T // MR,),
        in_specs=[
            cols, cols, rows, rows, rows,
            pl.BlockSpec((D, 128), lambda i: (0, qkv.shape[1] // 128 - 1)),
            pl.BlockSpec((D, rest), lambda i: (0, down.shape[1] // rest - 1)),
        ],
        out_specs=[rows_spec(D, MR // 2)] * 2 + [whole_spec((D, 2 * W))],
        out_shape=[jax.ShapeDtypeStruct((T // 2, D), bf16)] * 2 + [jax.ShapeDtypeStruct((D, 2 * W), bf16)],
        scratch_shapes=[pltpu.VMEM((2 * W, D), f32)],
        compiler_params=pltpu.CompilerParams(vmem_limit_bytes=VMEM_LIMIT),
        cost_estimate=cost(0.1),
        name="mid",
    )(o, dq, mixer, g, branch, qkv, down)


def post_kernel(place_ref, dkv_ref, ahead_ref, dq_ref, cos_ref, sin_ref, normed_ref, mixer_ref, back_ref, gain_ref, w_ref, *refs, chunk):
    heads = dkv_ref.shape[0]
    W = heads * HD
    step = pl.program_id(0)
    late = chunk is not None
    if late:
        _, _, acc_in, sums_in, mid_ref, kept_ref, sent_ref, send_ref, keep_ref, sums_ref, acc_ref = refs
    else:
        acc_in = None
        sums_in, kept_ref, sent_ref, grad_ref, sums_ref, acc_ref = refs

    @pl.when(step == 0)
    def _():
        sums_ref[...] = sums_in[...]
        acc_ref[...] = jnp.zeros_like(acc_ref) if acc_in is None else acc_in[...]

    cos_rows, sin_rows = rotation_rows(cos_ref[...], sin_ref[...])
    kv = jnp.concatenate(
        [rotate(dkv_ref[h] + ahead_ref[h].astype(f32), cos_rows, -sin_rows).astype(bf16) for h in range(heads)], axis=1
    )
    acc_ref[...] += mm(mixer_ref[...], kv, TN)
    dq = dq_ref[...].astype(f32).T.astype(bf16)
    part = mm(kv, w_ref[:, : 2 * W], NT) + mm(dq, w_ref[:, 2 * W : 3 * W], NT)
    hat = (part * gain_ref[...] + back_ref[...].astype(f32)).astype(bf16)
    kept_ref[...], sent_ref[...] = hat[: PR // 2], hat[PR // 2 :]
    sums_ref[0:1] += jnp.sum(part * normed_ref[...].astype(f32), axis=0, keepdims=True)
    sums_ref[1:2] += jnp.sum(part, axis=0, keepdims=True)
    sums_ref[2:3, : 2 * W] += jnp.sum(kv.astype(f32), axis=0, keepdims=True)
    sums_ref[2:3, 2 * W : 3 * W] += jnp.sum(dq.astype(f32), axis=0, keepdims=True)

    @pl.when(step == pl.num_programs(0) - 1)
    def _():
        if late:
            total = jnp.concatenate([acc_ref[...], mid_ref[...].astype(f32)], axis=1)
            store_halves(total, place_ref[1], chunk, send_ref, keep_ref)
            one = sums_ref[...].astype(bf16).astype(f32)
            two = (sums_ref[...] - one).astype(bf16).astype(f32)
            sums_ref[...] = one + two
            send_ref[total.shape[0] // 2 :] = jnp.concatenate([one, two], axis=0).astype(bf16)
        else:
            grad_ref[...] = acc_ref[...]


def post(part, place, dkv, ahead, dq, cos, sin, normed, mixer, back, gain, w, early=(), chunk=None):
    T, D = mixer.shape
    heads = dkv.shape[0]
    W = heads * HD
    per = T // 2 // PR

    def at(i, place):
        return (part ^ (place[0] >> 1)) * per + i

    def inner(i, place):
        return i

    def rows(index):
        return pl.BlockSpec((PR, D), lambda i, place: (index(i, place), 0))

    def cols(count):
        return pl.BlockSpec((count, PR), lambda i, place: (0, at(i, place)))

    def fixed(shape):
        return pl.BlockSpec(shape, lambda i, place: (0,) * len(shape))

    half = pl.BlockSpec((heads, PR, 128), lambda i, place: (0, i, 0))
    late = len(early) > 1
    specs = [half, half, cols(W), cols(8), cols(8), rows(at), rows(at), rows(at), fixed(gain.shape), fixed(w.shape)]
    if late:
        specs += [pl.BlockSpec(memory_space=pl.ANY)] * 2 + [fixed((D, 2 * W)), fixed((8, D)), fixed((D, 2 * W))]
        grads = [fixed((D // 2 + 16, 4 * W)), fixed((D // 2, 4 * W))]
        shapes = [jax.ShapeDtypeStruct((D // 2 + 16, 4 * W), bf16), jax.ShapeDtypeStruct((D // 2, 4 * W), bf16)]
    else:
        specs += [fixed((8, D))]
        grads = [fixed((D, 2 * W))]
        shapes = [jax.ShapeDtypeStruct((D, 2 * W), f32)]
    return pl.pallas_call(
        functools.partial(post_kernel, chunk=chunk),
        grid_spec=pltpu.PrefetchScalarGridSpec(
            num_scalar_prefetch=1,
            grid=(per,),
            in_specs=specs,
            out_specs=[pl.BlockSpec((PR // 2, D), lambda i, place: (at(i, place), 0))] * 2 + grads + [fixed((8, D))],
            scratch_shapes=[pltpu.VMEM((D, 2 * W), f32)],
        ),
        out_shape=[
            jax.ShapeDtypeStruct((T // 2, D), bf16),
            jax.ShapeDtypeStruct((T // 2, D), bf16),
            *shapes,
            jax.ShapeDtypeStruct((8, D), f32),
        ],
        input_output_aliases={11: 0, 12: 1} if late else {},
        compiler_params=pltpu.CompilerParams(vmem_limit_bytes=VMEM_LIMIT),
        cost_estimate=cost(8 if late else 0.1),
        name="post",
    )(place, dkv, ahead, dq, cos, sin, normed, mixer, back, gain, w, *early)


def mix_finish_kernel(keep_ref, other_ref, own_ref, triple_ref, out_ref, sums_ref):
    rows = keep_ref.shape[0]
    W = out_ref.shape[0]
    other = other_ref[...].astype(f32)
    total = keep_ref[...] + other[:rows]
    sums_ref[...] = own_ref[...] + (other[rows : rows + 8] + other[rows + 8 :])
    triple_ref[0] = total[:, 2 * W : 3 * W]
    for n in range(2):
        triple_ref[1 + n] = jnp.concatenate(
            [total[:, at + n * HD : at + (n + 1) * HD] for at in range(0, 2 * W, 2 * HD)], axis=1
        )
    out_ref[...] = total[:, 3 * W :].T


def mix_finish(keep, other, own, W):
    rows = keep.shape[0]
    return pl.pallas_call(
        mix_finish_kernel,
        out_shape=[
            jax.ShapeDtypeStruct((3, rows, W), f32),
            jax.ShapeDtypeStruct((W, rows), f32),
            jax.ShapeDtypeStruct(own.shape, f32),
        ],
        cost_estimate=cost(0.1),
        name="mix_finish",
    )(keep, other, own)


def ffn_finish_kernel(keep_ref, other_ref, up_ref, down_ref):
    F = up_ref.shape[1]
    total = keep_ref[...] + other_ref[...].astype(f32)
    up_ref[...] = total[:, :F]
    down_ref[...] = total[:, F:]


def ffn_finish(keep, other):
    rows, cols = keep.shape
    F = cols // 2
    return pl.pallas_call(
        ffn_finish_kernel,
        out_shape=[jax.ShapeDtypeStruct((rows, F), f32)] * 2,
        cost_estimate=cost(0.1),
        name="ffn_finish",
    )(keep, other)


def shards(
    hidden_in, positions, mixer_gain, mixer_shift, feed_gain, feed_shift, triple_weight,
    pair_bias, output_weight, up_weight, up_bias, down_weight, out_bias, out_grad,
):
    T = positions.shape[0]
    blk, D = hidden_in.shape
    W = pair_bias.shape[1]
    heads = W // HD
    chunk = triple_weight.shape[0]
    t = lax.axis_index("tensor").astype(jnp.int32)

    F = up_weight.shape[1]
    bits = bit_count("dp")
    down_order = list(reversed(range(bits)))
    mixed_order = down_order[:-2] + [0, 1]
    q_w, k_w, v_w = (triple_weight[:, i].reshape(chunk, heads, HD) for i in range(3))
    kv_w = jnp.concatenate([k_w, v_w], axis=2).reshape(chunk, 2 * W)
    pad = (-W) % 128
    out_own = output_weight.T
    up_w, up_parts = gather_dp(up_weight, down_order)
    qkv_own = jnp.concatenate([kv_w, q_w.reshape(chunk, W), out_own[:, :pad]], axis=1)
    qkv_w, qkv_parts = gather_dp(qkv_own, down_order, [up_parts[0]])
    hids = gather_tensor(hidden_in)
    gs = gather_tensor(after(out_grad, hids[2]))

    pos = jnp.concatenate([lax.dynamic_slice(positions, ((r ^ t) * blk,), (blk,)) for r in range(T // blk)])
    inverse = 1.0 / 10000.0 ** (jnp.arange(ROT // 2, dtype=f32) * (2.0 / ROT))
    angles = pos.astype(f32)[None, :] * inverse[:, None]
    cos, sin = jnp.cos(angles), jnp.sin(angles)
    rows = jnp.arange(T, dtype=jnp.int32) ^ (t * blk)
    start = (rows + T - pos)[None]
    q_starts = jnp.arange(0, T, TQ, dtype=jnp.int32)
    first = (q_starts + T - positions[::TQ]) // TK

    gains = jnp.stack([mixer_gain, mixer_shift, feed_gain, feed_shift])
    v_bias = pair_bias[1].reshape(heads, HD)
    kv_bias = jnp.concatenate([jnp.zeros_like(v_bias), v_bias], axis=1).reshape(2 * W)
    bias = jnp.concatenate([kv_bias, pair_bias[0], jnp.zeros((pad,), f32)])[None]
    high = (lax.axis_index("dp") & 1).astype(jnp.int32)
    spots = jnp.stack([t, high])
    mixer_in, kv, q = pre(hids, gains, qkv_w, bias, cos, sin, heads)
    feed_gains, feed_bias = gains[2:], up_bias[None]
    early_ops = (feed_gains, feed_bias, first, start)
    down_own = jnp.concatenate([down_weight.T, out_own[:, pad:]], axis=1)
    down_w, _ = gather_dp(down_own, down_order, [qkv_parts[-2]] + [None] * (bits - 2) + [(gs[2], up_w, early_ops)])
    tail = shift(after(kv, down_w), "dp", 1)
    normed, g, branch, back, do, ffn_send, ffn_keep, ffn_sums = ffn(
        hids, gs, feed_gains, up_w, down_w, qkv_w, feed_bias, high[None], heads, chunk
    )
    attn_args = (spots, first, start, tail, kv, q, do, cos, sin, blk)
    *early, dtail_low, carry = attention(*attn_args)
    ahead_low = shift(dtail_low, "dp", -1)
    ffn_order = down_order[::-1]
    ffn_other = swap(after(ffn_send, tail), "dp", 1 << ffn_order[0])
    o, dq, dtail_high, dkv_low, dkv_high = attention(*attn_args, early=(carry, *early))
    ahead_high = shift(after(dtail_high, ahead_low, ffn_other), "dp", -1)
    post_args = (dq, cos, sin, normed, mixer_in, back, mixer_gain[None], qkv_w)
    ffn_first = ffn_keep.astype(f32) + ffn_other.astype(f32)
    ffn_send, ffn_keep = halves(ffn_first, chunk, ffn_order[1:], ffn_order[1])
    ffn_other = swap(ffn_send, "dp", 1 << ffn_order[1])
    early = post(0, spots, dkv_low, after(ahead_low, ffn_first), *post_args, early=(ffn_sums,))
    *branch, mid_grad = mid(after(o, early[3]), dq, mixer_in, g, branch, qkv_w, down_w)
    *hat, mix_send, mix_keep, sums = post(
        1, spots, dkv_high, ahead_high, *post_args, early=(*early, mid_grad), chunk=chunk
    )
    mix_order = ffn_order
    *hat, mix_send, mix_keep, sums, ffn_other = lax.optimization_barrier((*hat, mix_send, mix_keep, sums, ffn_other))
    mix_other = swap(mix_send, "dp", 1 << mix_order[0])
    hat_own, far = scatter_core(*hat)
    landed_far = swap(far, "tensor", 2)
    branch_own, branch_far = scatter_core(*branch)
    branch_across = swap(after(branch_far, landed_far), "tensor", 2)
    ffn_grads = ffn_keep.astype(f32) + after(ffn_other, far).astype(f32)
    for n in range(2, bits):
        ffn_send, ffn_keep = halves(ffn_grads, chunk, ffn_order[n:], ffn_order[n])
        ffn_other = swap(ffn_send, "dp", 1 << ffn_order[n])
        ffn_grads = ffn_keep.astype(f32) + ffn_other.astype(f32)
    mix_other = after(mix_other, far, branch_far, ffn_send).astype(f32)
    mix_grads = mix_keep.astype(f32) + mix_other[: mix_keep.shape[0]]
    sums = sums + (mix_other[-16:-8] + mix_other[-8:])
    for n in range(1, bits - 1):
        mix_grads, sums = scatter_step(mix_grads, chunk, mix_order[n:], mix_order[n], landed_far if n == 1 else None, sums)
    mix_send, mix_keep = halves(mix_grads, chunk, mix_order[-1:], mix_order[-1])
    one, two = two_parts(sums)
    mix_send = jnp.concatenate([mix_send, one.astype(bf16), two.astype(bf16)], axis=0)
    mix_other = swap(mix_send, "dp", 1 << mix_order[-1])
    ffn_other = after(ffn_other, mix_send)
    up_grad, down_grad = ffn_finish(ffn_keep, ffn_other)
    grad_hat = hat_own + after(landed_far, mix_send).astype(f32)
    own, inv_std = normalize(hidden_in.astype(f32))
    first_mean = jnp.mean(grad_hat, axis=-1, keepdims=True)
    second_mean = jnp.mean(grad_hat * own, axis=-1, keepdims=True)
    grad_hidden = out_grad.astype(f32) + inv_std * (grad_hat - first_mean - own * second_mean)
    mix_other = after(mix_other, up_grad, grad_hidden)
    triple_grad, out_grad_t, sums = mix_finish(mix_keep, mix_other, one + two, W)
    result = hidden_in.astype(f32) + branch_own + after(branch_across, sums).astype(f32) + out_bias
    norm_sums = sums + swap(sums, "tensor", 1)
    norm_sums = norm_sums + swap(norm_sums, "tensor", 2)
    head_sums = sums[2, : 2 * W].reshape(heads, 2, HD)[:, 1].reshape(W)
    pair_grad = jnp.stack([sums[2, 2 * W : 3 * W], head_sums])
    return (
        result,
        grad_hidden,
        norm_sums[0],
        norm_sums[1],
        norm_sums[3],
        norm_sums[4],
        jnp.transpose(triple_grad, (1, 0, 2)),
        pair_grad,
        out_grad_t,
        up_grad,
        sums[5],
        down_grad.T,
        norm_sums[6],
    )


def solution(mesh):
    rows = P(("dp", "tensor"), None)
    in_specs = (
        rows, P("dp"), P(), P(), P(), P(), P("dp", None, "tensor"), P(None, "tensor"), P("tensor", "dp"),
        P("dp", "tensor"), P("tensor"), P("tensor", "dp"), P(), rows,
    )
    out_specs = (
        rows, rows, P(), P(), P(), P(), P("dp", None, "tensor"), P(None, "tensor"), P("tensor", "dp"),
        P("dp", "tensor"), P("tensor"), P("tensor", "dp"), P(),
    )
    return jax.shard_map(shards, mesh=mesh, in_specs=in_specs, out_specs=out_specs, check_vma=False)
```

```python
import functools
import math

import jax
import jax.numpy as jnp
from jax import lax
from jax.experimental import pallas as pl
from jax.experimental.pallas import tpu as pltpu
from jax.sharding import PartitionSpec as P

HD = 64
ROT = 16
DOC_MOST = 2048
EPSILON = 1e-05
NEG = -1e30
TQ = 256
TK = 256
NK = 4
TR = 512
FR = 512
PR = 1024
MR = 1024
bf16 = jnp.bfloat16
f32 = jnp.float32
NN = (((1,), (0,)), ((), ()))
NT = (((1,), (1,)), ((), ()))
TN = (((0,), (0,)), ((), ()))
TT = (((0,), (1,)), ((), ()))
VMEM_LIMIT = 56 * 2**20


def cost(us):
    return pl.CostEstimate(flops=int(us * 1.15e9), bytes_accessed=1000, transcendentals=0)


def mm(left, right, dims=NN):
    return lax.dot_general(left, right, dims, preferred_element_type=f32)


def swap(value, axis, mask):
    count = lax.axis_size(axis)
    return lax.ppermute(value, axis, [(i, i ^ mask) for i in range(count)])


def shift(value, axis, distance):
    count = lax.axis_size(axis)
    route = [(i, i + distance) for i in range(count) if 0 <= i + distance < count]
    return lax.ppermute(value, axis, route)


def bit_count(axis):
    return lax.axis_size(axis).bit_length() - 1


def after(value, *others):
    return lax.optimization_barrier((value, others))[0]


def gather_tensor(own):
    near = swap(own, "tensor", 1)
    far = swap(own, "tensor", 2)
    diagonal = swap(far, "tensor", 1)
    return [own, near, far, diagonal]


def scatter_core(kept, sent):
    near = swap(sent, "tensor", 1).astype(f32)
    total = kept.astype(f32) + near
    rows = kept.shape[0] // 2
    return total[:rows], total[rows:].astype(bf16)


def split(held, rows, left, bit):
    above = 1 << sum(b > bit for b in left)
    return held.reshape(above, 2, -1, held.shape[-1])


def gather_dp(own, order, gates=()):
    me = lax.axis_index("dp")
    rows, cols = own.shape
    held, done = own, []
    parts = []
    for n, bit in enumerate(order):
        if n == 0 and gates and gates[0] is not None:
            held = after(held, gates[0])
        other = swap(held, "dp", 1 << bit)
        if n + 1 < len(gates) and gates[n + 1] is not None:
            other = after(other, gates[n + 1])
        high = ((me >> bit) & 1) == 1
        above = 1 << sum(b > bit for b in done)
        one, two = held.reshape(above, -1, cols), other.reshape(above, -1, cols)
        held = jnp.concatenate([jnp.where(high, two, one), jnp.where(high, one, two)], axis=1).reshape(-1, cols)
        done.append(bit)
        parts.append(held)
    return held, parts


def two_parts(sums):
    first = lax.reduce_precision(sums, 8, 7)
    return first, lax.reduce_precision(sums - first, 8, 7)


def halves(held, rows, left, bit):
    cols = held.shape[1]
    pairs = split(held, rows, left, bit)
    high = ((lax.axis_index("dp") >> bit) & 1) == 1
    send = jnp.where(high, pairs[:, 0], pairs[:, 1]).astype(bf16).reshape(-1, cols)
    keep = jnp.where(high, pairs[:, 1], pairs[:, 0]).reshape(-1, cols)
    return send, keep


def scatter_step(held, rows, left, bit, landed=None, sums=None):
    send, keep = halves(held, rows, left, bit)
    count = send.shape[0]
    if sums is not None:
        first, second = two_parts(sums)
        send = jnp.concatenate([send, first.astype(bf16), second.astype(bf16)], axis=0)
    other = swap(send, "dp", 1 << bit)
    if landed is not None:
        other = after(other, landed)
    other = other.astype(f32)
    held = keep.astype(f32) + other[:count]
    if sums is None:
        return held
    return held, (first + second) + (other[count : count + 8] + other[count + 8 :])


def sum_over(value, axis):
    for bit in range(bit_count(axis)):
        value = value + swap(value, axis, 1 << bit)
    return value


def normalize(values):
    centred = values - jnp.mean(values, axis=-1, keepdims=True)
    inv_std = lax.rsqrt(jnp.mean(centred * centred, axis=-1, keepdims=True) + EPSILON)
    return (centred * inv_std, inv_std)


def rows_spec(cols, tile=TR):
    return pl.BlockSpec((tile, cols), lambda i: (i, 0))


def whole_spec(shape):
    return pl.BlockSpec(shape, lambda i: (0,) * len(shape))


def heads_spec(heads, cols=128, tile=TR):
    return pl.BlockSpec((heads, tile, cols), lambda i: (0, i, 0))


def piece_specs(count, rows, cols, tile=TR):
    per = rows // tile
    return [pl.BlockSpec((tile, cols), lambda i, p=p: (jnp.clip(i - p * per, 0, per - 1), 0)) for p in range(count)]


def pick(refs, rows):
    at = pl.program_id(0) // (rows // refs[0].shape[0])
    value = refs[0][...]
    for n, ref in enumerate(refs[1:]):
        value = jnp.where(at == n + 1, ref[...], value)
    return value


def rotation_rows(cos, sin):
    ones = jnp.ones((128 - ROT, cos.shape[1]), f32)
    return jnp.concatenate([cos, cos, ones], axis=0).T, jnp.concatenate([-sin, sin, ones * 0.0], axis=0).T


def rotate(x, cos_rows, sin_rows):
    lane = lax.broadcasted_iota(jnp.int32, x.shape, 1)
    partner = jnp.where(lane < ROT // 2, pltpu.roll(x, 128 - ROT // 2, 1), pltpu.roll(x, ROT // 2, 1))
    return x * cos_rows + partner * sin_rows


def pre_kernel(*refs, pieces, blk):
    hids, refs = refs[:pieces], refs[pieces:]
    gains_ref, w_ref, bias_ref, cos_ref, sin_ref, mixer_ref, kv_ref, q_ref = refs
    heads = kv_ref.shape[0]
    normed, _ = normalize(pick(hids, blk).astype(f32))
    mixer = (normed * gains_ref[0:1] + gains_ref[1:2]).astype(bf16)
    mixer_ref[...] = mixer
    proj = mm(mixer, w_ref[...]) + bias_ref[...]
    cos_rows, sin_rows = rotation_rows(cos_ref[...], sin_ref[...])
    lane = lax.broadcasted_iota(jnp.int32, (TR, 128), 1)
    for h in range(heads):
        kv_ref[h] = rotate(proj[:, h * 128 : (h + 1) * 128], cos_rows, sin_rows).astype(bf16)
        at = heads * 128 + (h // 2) * 128
        x = proj[:, at : at + 128]
        if h % 2:
            x = pltpu.roll(x, HD, 1)
        x = jnp.where(lane < HD, rotate(x, cos_rows, sin_rows) * (1.0 / math.sqrt(HD)), 0.0)
        q_ref[h] = x.astype(bf16)


def pre(hids, gains, w, bias, cos, sin, heads):
    blk, D = hids[0].shape
    T = blk * len(hids)
    return pl.pallas_call(
        functools.partial(pre_kernel, pieces=len(hids), blk=blk),
        grid=(T // TR,),
        in_specs=piece_specs(len(hids), blk, D) + [
            whole_spec(gains.shape),
            whole_spec(w.shape),
            whole_spec(bias.shape),
            pl.BlockSpec((8, TR), lambda i: (0, i)),
            pl.BlockSpec((8, TR), lambda i: (0, i)),
        ],
        out_specs=[rows_spec(D)] + [heads_spec(heads)] * 2,
        out_shape=[jax.ShapeDtypeStruct((T, D), bf16)] + [jax.ShapeDtypeStruct((heads, T, 128), bf16)] * 2,
        compiler_params=pltpu.CompilerParams(vmem_limit_bytes=40 * 2**20),
        cost_estimate=cost(0.5),
        name="pre",
    )(*hids, gains, w, bias, cos, sin)


def gelu_parts(h):
    mag = jnp.abs(h) * (1.0 / math.sqrt(2.0))
    t = 1.0 / (1.0 + 0.3275911 * mag)
    poly = t * (0.254829592 + t * (-0.284496736 + t * (1.421413741 + t * (-1.453152027 + t * 1.061405429))))
    bell = jnp.exp(-0.5 * h * h)
    tail = 0.5 * poly * bell
    return (jnp.where(h >= 0, 1.0 - tail, tail), bell * (1.0 / math.sqrt(2.0 * math.pi)))


def store_halves(total, high, chunk, send_ref, keep_ref):
    count = total.shape[0] // chunk
    low, top = (
        jnp.concatenate([total[n * chunk : (n + 1) * chunk] for n in range(side, count, 2)], axis=0) for side in (0, 1)
    )
    send_ref[: total.shape[0] // 2] = jnp.where(high == 1, low, top).astype(bf16)
    keep_ref[...] = jnp.where(high == 1, top, low).astype(bf16)


def ffn_kernel(*refs, pieces, blk, chunk):
    hids, gs, refs = refs[:pieces], refs[pieces : 2 * pieces], refs[2 * pieces :]
    gains_ref, up_ref, down_ref, qkv_ref, bias_ref, high_ref, normed_ref, g_ref, branch_ref, back_ref, do_ref, send_ref, keep_ref, sums_ref, acc_ref = refs
    heads = do_ref.shape[0]
    F = bias_ref.shape[1]
    step = pl.program_id(0)
    normed, _ = normalize(pick(hids, blk).astype(f32))
    normed_ref[...] = normed.astype(bf16)
    feed = (normed * gains_ref[0:1] + gains_ref[1:2]).astype(bf16)
    g = pick(gs, blk)
    g_ref[...] = g
    up, down = up_ref[...], down_ref[:, :F]
    hidden = mm(feed, up) + bias_ref[...]
    cumulative, density = gelu_parts(hidden)
    act = (hidden * cumulative).astype(bf16)
    hg = (mm(g, down) * (cumulative + hidden * density)).astype(bf16)
    branch_ref[...] = mm(act, down, NT).astype(bf16)
    back = mm(hg, up, NT)
    back_ref[...] = (back * gains_ref[0:1]).astype(bf16)

    @pl.when(step == 0)
    def _():
        sums_ref[...] = jnp.zeros_like(sums_ref)
        acc_ref[...] = jnp.zeros_like(acc_ref)

    acc_ref[:, :F] += mm(feed, hg, TN)
    acc_ref[:, F:] += mm(g, act, TN)
    sums_ref[3:4] += jnp.sum(back * normed, axis=0, keepdims=True)
    sums_ref[4:5] += jnp.sum(back, axis=0, keepdims=True)
    sums_ref[5:6] += jnp.sum(hg.astype(f32), axis=0, keepdims=True)

    @pl.when(step < blk // FR)
    def _():
        sums_ref[6:7] += jnp.sum(g.astype(f32), axis=0, keepdims=True)

    @pl.when(step == pl.num_programs(0) - 1)
    def _():
        store_halves(acc_ref[...], high_ref[0], chunk, send_ref, keep_ref)

    do = jnp.concatenate([mm(g, qkv_ref[...]), mm(g, down_ref[:, F:])], axis=1)
    lane = lax.broadcasted_iota(jnp.int32, (FR, 128), 1)
    for h in range(heads):
        at = HD * (h + 1)
        x = do[:, at // 128 * 128 : at // 128 * 128 + 128]
        if at % 128 == 0:
            x = pltpu.roll(x, HD, 1)
        do_ref[h] = jnp.where(lane < HD, 0.0, x).astype(bf16)


def ffn(hids, gs, gains, up, down, qkv, bias, high, heads, chunk):
    blk, D = gs[0].shape
    T = blk * len(gs)
    F = bias.shape[1]
    rows = rows_spec(D, FR)
    return pl.pallas_call(
        functools.partial(ffn_kernel, pieces=len(gs), blk=blk, chunk=chunk),
        grid=(T // FR,),
        in_specs=piece_specs(len(gs), blk, D, FR) * 2
        + [whole_spec(gains.shape), whole_spec(up.shape), whole_spec(down.shape)]
        + [pl.BlockSpec((D, 128), lambda i: (0, qkv.shape[1] // 128 - 1)), whole_spec(bias.shape)]
        + [pl.BlockSpec(memory_space=pltpu.SMEM)],
        out_specs=[rows] * 4 + [heads_spec(heads, 128, FR)] + [whole_spec((D // 2, 2 * F))] * 2 + [whole_spec((8, D))],
        out_shape=[jax.ShapeDtypeStruct((T, D), bf16)] * 4
        + [
            jax.ShapeDtypeStruct((heads, T, 128), bf16),
            jax.ShapeDtypeStruct((D // 2, 2 * F), bf16),
            jax.ShapeDtypeStruct((D // 2, 2 * F), bf16),
            jax.ShapeDtypeStruct((8, D), f32),
        ],
        scratch_shapes=[pltpu.VMEM((D, 2 * F), f32)],
        compiler_params=pltpu.CompilerParams(vmem_limit_bytes=VMEM_LIMIT),
        cost_estimate=cost(0.5),
        name="ffn",
    )(*hids, *gs, gains, up, down, qkv, bias, high)


def attn_kernel(*refs, T, blk, heads, late):
    if late:
        (place_ref, first_ref, start_ref, tail_ref, kv_ref, q_ref, do_ref, cos_ref, sin_ref, carry_ref, o_in, dq_in,
         o_ref, dq_ref, dtail_ref, low_ref, high_ref, *refs) = refs
    else:
        (place_ref, first_ref, start_ref, tail_ref, kv_ref, q_ref, do_ref, cos_ref, sin_ref,
         o_ref, dq_ref, dtail_ref, carry_ref, *refs) = refs
    kv_scr, dkv_scr, s_scr, dp_scr, o_acc, dq_acc, qd_scr = refs
    half = T // 2
    base = half if late else 0
    t = place_ref[0]
    inner = (t & 1) * blk
    H = range(heads)

    def half_at(n):
        return pl.ds(pl.multiple_of((n ^ (t >> 1)) * half, half), half)

    for n, (ref, part) in enumerate([(tail_ref, 1), (kv_ref, 0), (kv_ref, 1)] if late else [(tail_ref, 0), (tail_ref, 1), (kv_ref, 0)]):
        kv_scr[:, n * half : (n + 1) * half] = ref[:, half_at(part), :]
    if late:
        dkv_scr[:, :T] = carry_ref[...]
        dkv_scr[:, T:] = jnp.zeros_like(dkv_scr[:, T:])
        o_ref[:, half_at(0)] = o_in[...]
        dq_ref[:, half_at(0)] = dq_in[...]
    else:
        dkv_scr[...] = jnp.zeros_like(dkv_scr)

    def place(row):
        return (row - base) ^ inner

    def q_tile(qi, c):
        q0 = pl.multiple_of(base + qi * TQ, TQ)
        qr = pl.multiple_of(q0 ^ (t * blk), TQ)
        out = qr if late else pl.multiple_of(place(q0), TQ)
        for h in H:
            qd_scr[h, :TQ] = q_ref[h, pl.ds(qr, TQ), :]
            qd_scr[h, TQ:] = do_ref[h, pl.ds(qr, TQ), :]
        start = start_ref[:, pl.ds(qr, TQ)]
        qidx = q0 + T + lax.broadcasted_iota(jnp.int32, (1, TQ), 1)
        first = first_ref[base // TQ + qi]
        stop = (q0 + T) // TK + TQ // TK
        count = stop - first

        def over(body, init):
            pairs = count // NK
            state = lax.fori_loop(0, pairs, lambda i, c: body(first + i * NK, c, NK), init)
            return lax.fori_loop(first + pairs * NK, stop, lambda i, c: body(i, c, 1), state)

        def pass1(ki, state, nk):
            rows = nk * TK
            slot = ki - first
            j = ki * TK + lax.broadcasted_iota(jnp.int32, (rows, TQ), 0)
            ok = (j >= start) & (j <= qidx)
            ats = [pl.multiple_of(place((ki + n) * TK), TK) for n in range(nk)]
            sdps = [mm(jnp.concatenate([kv_scr[h, pl.ds(at, TK), :] for at in ats], axis=0), qd_scr[h], NT) for h in H]
            stats = []
            for h in H:
                m8, l8, d8 = state[3 * h : 3 * h + 3]
                s = jnp.where(ok, sdps[h][:, :TQ], NEG)
                dp = sdps[h][:, TQ:]
                for n in range(nk):
                    s_scr[slot + n, h] = s[n * TK : (n + 1) * TK]
                    dp_scr[slot + n, h] = dp[n * TK : (n + 1) * TK]
                s3 = s.reshape(rows // 8, 8, TQ)
                m_new = jnp.maximum(m8, jnp.max(s3, axis=0))
                alpha = jnp.exp(m8 - m_new)
                e = jnp.exp(s3 - m_new[None])
                l8 = l8 * alpha + jnp.sum(e, axis=0)
                d8 = d8 * alpha + jnp.sum(e * dp.reshape(rows // 8, 8, TQ), axis=0)
                stats += [m_new, l8, d8]
            return tuple(stats)

        z8 = jnp.zeros((8, TQ), f32)
        state = over(pass1, (jnp.full((8, TQ), NEG, f32), z8, z8) * heads)
        lses, deltas = [], []
        for h in H:
            m8, l8, d8 = state[3 * h : 3 * h + 3]
            m = jnp.max(m8, axis=0, keepdims=True)
            w = jnp.exp(m8 - m)
            total = jnp.sum(l8 * w, axis=0, keepdims=True)
            lses.append(m + jnp.log(total))
            deltas.append(jnp.sum(d8 * w, axis=0, keepdims=True) / total)
        o_acc[...] = jnp.zeros_like(o_acc)
        dq_acc[...] = jnp.zeros_like(dq_acc)

        def pass2(ki, c2, nk):
            slot = ki - first
            ats = [pl.multiple_of(place((ki + n) * TK), TK) for n in range(nk)]
            for h in H:
                dq = dq_acc[h]
                o = o_acc[h]
                for n in range(nk):
                    p = jnp.exp(s_scr[slot + n, h] - lses[h])
                    ds = (p * (dp_scr[slot + n, h] - deltas[h])).astype(bf16)
                    p = p.astype(bf16)
                    dkv_scr[h, pl.ds(ats[n], TK), :] += mm(jnp.concatenate([ds, p], axis=1), qd_scr[h])
                    kvt = kv_scr[h, pl.ds(ats[n], TK), :].T
                    dq += mm(kvt[:HD], ds)
                    o += mm(kvt[HD:], p)
                dq_acc[h] = dq
                o_acc[h] = o
            return c2

        over(pass2, 0)
        cos = cos_ref[:, pl.ds(qr, TQ)]
        sin = sin_ref[:, pl.ds(qr, TQ)]
        for h in H:
            o_ref[h * HD : (h + 1) * HD, pl.ds(out, TQ)] = o_acc[h].astype(bf16)
            dq = dq_acc[h] * (1.0 / math.sqrt(HD))
            a, b = dq[: ROT // 2], dq[ROT // 2 : ROT]
            dq = jnp.concatenate([a * cos + b * sin, b * cos - a * sin, dq[ROT:]], axis=0)
            dq_ref[h * HD : (h + 1) * HD, pl.ds(out, TQ)] = dq.astype(bf16)
        return c

    lax.fori_loop(0, half // TQ, q_tile, 0)
    dtail_ref[...] = dkv_scr[:, :half].astype(bf16)
    if late:
        low_ref[...] = dkv_scr[:, half:T]
        high_ref[...] = dkv_scr[:, T:]
    else:
        carry_ref[...] = dkv_scr[:, half:]


def attention(place, first, start, tail, kv, q, do, cos, sin, blk, early=()):
    heads, T, _ = q.shape
    W = heads * HD
    late = len(early) > 0
    vmem = pl.BlockSpec(memory_space=pltpu.VMEM)
    smem = pl.BlockSpec(memory_space=pltpu.SMEM)
    slots = DOC_MOST // TK + TQ // TK
    span = T if late else T // 2
    outs = [((W, span), bf16), ((W, span), bf16), ((heads, T // 2, 128), bf16)]
    outs += [((heads, T // 2, 128), f32)] * 2 if late else [((heads, T, 128), f32)]
    return pl.pallas_call(
        functools.partial(attn_kernel, T=T, blk=blk, heads=heads, late=late),
        in_specs=[smem, smem] + [vmem] * (7 + len(early)),
        out_specs=[vmem] * len(outs),
        scratch_shapes=[
            pltpu.VMEM((heads, T + T // 2, 128), bf16),
            pltpu.VMEM((heads, T + T // 2, 128), f32),
            pltpu.VMEM((slots, heads, TK, TQ), f32),
            pltpu.VMEM((slots, heads, TK, TQ), f32),
            pltpu.VMEM((heads, HD, TQ), f32),
            pltpu.VMEM((heads, HD, TQ), f32),
            pltpu.VMEM((heads, 2 * TQ, 128), bf16),
        ],
        out_shape=[jax.ShapeDtypeStruct(*out) for out in outs],
        compiler_params=pltpu.CompilerParams(vmem_limit_bytes=36 * 2**20),
        cost_estimate=cost(0.1),
        name="attn",
    )(place, first, start, tail, kv, q, do, cos, sin, *early)


def mid_kernel(o_ref, dq_ref, mixer_ref, g_ref, branch_ref, qkv_ref, down_ref, kept_ref, sent_ref, grad_ref, acc_ref):
    W = o_ref.shape[0]
    pad = qkv_ref.shape[1] - HD
    step = pl.program_id(0)
    o = o_ref[...]
    rows = jnp.concatenate([jnp.zeros((pad, o.shape[1]), f32), o.astype(f32)], axis=0).T.astype(bf16)
    out = mm(rows[:, : pad + HD], qkv_ref[...], NT) + mm(rows[:, pad + HD :], down_ref[...], NT)
    out = (out + branch_ref[...].astype(f32)).astype(bf16)
    kept_ref[...], sent_ref[...] = out[: MR // 2], out[MR // 2 :]

    @pl.when(step == 0)
    def _():
        acc_ref[...] = jnp.zeros_like(acc_ref)

    acc_ref[:W] += mm(dq_ref[...], mixer_ref[...])
    acc_ref[W:] += mm(o, g_ref[...])

    @pl.when(step == pl.num_programs(0) - 1)
    def _():
        grad_ref[...] = acc_ref[...].T.astype(bf16)


def mid(o, dq, mixer, g, branch, qkv, down):
    T, D = mixer.shape
    W = o.shape[0]
    cols = pl.BlockSpec((W, MR), lambda i: (0, i))
    rows = rows_spec(D, MR)
    rest = W - HD
    return pl.pallas_call(
        mid_kernel,
        grid=(T // MR,),
        in_specs=[
            cols, cols, rows, rows, rows,
            pl.BlockSpec((D, 128), lambda i: (0, qkv.shape[1] // 128 - 1)),
            pl.BlockSpec((D, rest), lambda i: (0, down.shape[1] // rest - 1)),
        ],
        out_specs=[rows_spec(D, MR // 2)] * 2 + [whole_spec((D, 2 * W))],
        out_shape=[jax.ShapeDtypeStruct((T // 2, D), bf16)] * 2 + [jax.ShapeDtypeStruct((D, 2 * W), bf16)],
        scratch_shapes=[pltpu.VMEM((2 * W, D), f32)],
        compiler_params=pltpu.CompilerParams(vmem_limit_bytes=VMEM_LIMIT),
        cost_estimate=cost(0.1),
        name="mid",
    )(o, dq, mixer, g, branch, qkv, down)


def post_kernel(place_ref, dkv_ref, ahead_ref, dq_ref, cos_ref, sin_ref, normed_ref, mixer_ref, back_ref, gain_ref, w_ref, *refs, chunk):
    heads = dkv_ref.shape[0]
    W = heads * HD
    step = pl.program_id(0)
    late = chunk is not None
    if late:
        _, _, acc_in, sums_in, mid_ref, kept_ref, sent_ref, send_ref, keep_ref, sums_ref, acc_ref = refs
    else:
        acc_in = None
        sums_in, kept_ref, sent_ref, grad_ref, sums_ref, acc_ref = refs

    @pl.when(step == 0)
    def _():
        sums_ref[...] = sums_in[...]
        acc_ref[...] = jnp.zeros_like(acc_ref) if acc_in is None else acc_in[...]

    cos_rows, sin_rows = rotation_rows(cos_ref[...], sin_ref[...])
    kv = jnp.concatenate(
        [rotate(dkv_ref[h] + ahead_ref[h].astype(f32), cos_rows, -sin_rows).astype(bf16) for h in range(heads)], axis=1
    )
    acc_ref[...] += mm(mixer_ref[...], kv, TN)
    dq = dq_ref[...].astype(f32).T.astype(bf16)
    part = mm(kv, w_ref[:, : 2 * W], NT) + mm(dq, w_ref[:, 2 * W : 3 * W], NT)
    hat = (part * gain_ref[...] + back_ref[...].astype(f32)).astype(bf16)
    kept_ref[...], sent_ref[...] = hat[: PR // 2], hat[PR // 2 :]
    sums_ref[0:1] += jnp.sum(part * normed_ref[...].astype(f32), axis=0, keepdims=True)
    sums_ref[1:2] += jnp.sum(part, axis=0, keepdims=True)
    sums_ref[2:3, : 2 * W] += jnp.sum(kv.astype(f32), axis=0, keepdims=True)
    sums_ref[2:3, 2 * W : 3 * W] += jnp.sum(dq.astype(f32), axis=0, keepdims=True)

    @pl.when(step == pl.num_programs(0) - 1)
    def _():
        if late:
            total = jnp.concatenate([acc_ref[...], mid_ref[...].astype(f32)], axis=1)
            store_halves(total, place_ref[1], chunk, send_ref, keep_ref)
            one = sums_ref[...].astype(bf16).astype(f32)
            two = (sums_ref[...] - one).astype(bf16).astype(f32)
            sums_ref[...] = one + two
            send_ref[total.shape[0] // 2 :] = jnp.concatenate([one, two], axis=0).astype(bf16)
        else:
            grad_ref[...] = acc_ref[...]


def post(part, place, dkv, ahead, dq, cos, sin, normed, mixer, back, gain, w, early=(), chunk=None):
    T, D = mixer.shape
    heads = dkv.shape[0]
    W = heads * HD
    per = T // 2 // PR

    def at(i, place):
        return (part ^ (place[0] >> 1)) * per + i

    def inner(i, place):
        return i

    def rows(index):
        return pl.BlockSpec((PR, D), lambda i, place: (index(i, place), 0))

    def cols(count):
        return pl.BlockSpec((count, PR), lambda i, place: (0, at(i, place)))

    def fixed(shape):
        return pl.BlockSpec(shape, lambda i, place: (0,) * len(shape))

    half = pl.BlockSpec((heads, PR, 128), lambda i, place: (0, i, 0))
    late = len(early) > 1
    specs = [half, half, cols(W), cols(8), cols(8), rows(at), rows(at), rows(at), fixed(gain.shape), fixed(w.shape)]
    if late:
        specs += [pl.BlockSpec(memory_space=pl.ANY)] * 2 + [fixed((D, 2 * W)), fixed((8, D)), fixed((D, 2 * W))]
        grads = [fixed((D // 2 + 16, 4 * W)), fixed((D // 2, 4 * W))]
        shapes = [jax.ShapeDtypeStruct((D // 2 + 16, 4 * W), bf16), jax.ShapeDtypeStruct((D // 2, 4 * W), bf16)]
    else:
        specs += [fixed((8, D))]
        grads = [fixed((D, 2 * W))]
        shapes = [jax.ShapeDtypeStruct((D, 2 * W), f32)]
    return pl.pallas_call(
        functools.partial(post_kernel, chunk=chunk),
        grid_spec=pltpu.PrefetchScalarGridSpec(
            num_scalar_prefetch=1,
            grid=(per,),
            in_specs=specs,
            out_specs=[pl.BlockSpec((PR // 2, D), lambda i, place: (at(i, place), 0))] * 2 + grads + [fixed((8, D))],
            scratch_shapes=[pltpu.VMEM((D, 2 * W), f32)],
        ),
        out_shape=[
            jax.ShapeDtypeStruct((T // 2, D), bf16),
            jax.ShapeDtypeStruct((T // 2, D), bf16),
            *shapes,
            jax.ShapeDtypeStruct((8, D), f32),
        ],
        input_output_aliases={11: 0, 12: 1} if late else {},
        compiler_params=pltpu.CompilerParams(vmem_limit_bytes=VMEM_LIMIT),
        cost_estimate=cost(8 if late else 0.1),
        name="post",
    )(place, dkv, ahead, dq, cos, sin, normed, mixer, back, gain, w, *early)


def mix_finish_kernel(keep_ref, other_ref, own_ref, triple_ref, out_ref, sums_ref):
    rows = keep_ref.shape[0]
    W = out_ref.shape[0]
    other = other_ref[...].astype(f32)
    total = keep_ref[...] + other[:rows]
    sums_ref[...] = own_ref[...] + (other[rows : rows + 8] + other[rows + 8 :])
    triple_ref[0] = total[:, 2 * W : 3 * W]
    for n in range(2):
        triple_ref[1 + n] = jnp.concatenate(
            [total[:, at + n * HD : at + (n + 1) * HD] for at in range(0, 2 * W, 2 * HD)], axis=1
        )
    out_ref[...] = total[:, 3 * W :].T


def mix_finish(keep, other, own, W):
    rows = keep.shape[0]
    return pl.pallas_call(
        mix_finish_kernel,
        out_shape=[
            jax.ShapeDtypeStruct((3, rows, W), f32),
            jax.ShapeDtypeStruct((W, rows), f32),
            jax.ShapeDtypeStruct(own.shape, f32),
        ],
        cost_estimate=cost(0.1),
        name="mix_finish",
    )(keep, other, own)


def ffn_finish_kernel(keep_ref, other_ref, up_ref, down_ref):
    F = up_ref.shape[1]
    total = keep_ref[...] + other_ref[...].astype(f32)
    up_ref[...] = total[:, :F]
    down_ref[...] = total[:, F:]


def ffn_finish(keep, other):
    rows, cols = keep.shape
    F = cols // 2
    return pl.pallas_call(
        ffn_finish_kernel,
        out_shape=[jax.ShapeDtypeStruct((rows, F), f32)] * 2,
        cost_estimate=cost(0.1),
        name="ffn_finish",
    )(keep, other)


def shards(
    hidden_in, positions, mixer_gain, mixer_shift, feed_gain, feed_shift, triple_weight,
    pair_bias, output_weight, up_weight, up_bias, down_weight, out_bias, out_grad,
):
    T = positions.shape[0]
    blk, D = hidden_in.shape
    W = pair_bias.shape[1]
    heads = W // HD
    chunk = triple_weight.shape[0]
    t = lax.axis_index("tensor").astype(jnp.int32)

    F = up_weight.shape[1]
    bits = bit_count("dp")
    down_order = list(reversed(range(bits)))
    mixed_order = down_order[:-2] + [0, 1]
    q_w, k_w, v_w = (triple_weight[:, i].reshape(chunk, heads, HD) for i in range(3))
    kv_w = jnp.concatenate([k_w, v_w], axis=2).reshape(chunk, 2 * W)
    pad = (-W) % 128
    out_own = output_weight.T
    up_w, up_parts = gather_dp(up_weight, down_order)
    qkv_own = jnp.concatenate([kv_w, q_w.reshape(chunk, W), out_own[:, :pad]], axis=1)
    qkv_w, qkv_parts = gather_dp(qkv_own, down_order, [up_parts[0]])
    hids = gather_tensor(hidden_in)
    gs = gather_tensor(after(out_grad, hids[2]))

    pos = jnp.concatenate([lax.dynamic_slice(positions, ((r ^ t) * blk,), (blk,)) for r in range(T // blk)])
    inverse = 1.0 / 10000.0 ** (jnp.arange(ROT // 2, dtype=f32) * (2.0 / ROT))
    angles = pos.astype(f32)[None, :] * inverse[:, None]
    cos, sin = jnp.cos(angles), jnp.sin(angles)
    rows = jnp.arange(T, dtype=jnp.int32) ^ (t * blk)
    start = (rows + T - pos)[None]
    q_starts = jnp.arange(0, T, TQ, dtype=jnp.int32)
    first = (q_starts + T - positions[::TQ]) // TK

    gains = jnp.stack([mixer_gain, mixer_shift, feed_gain, feed_shift])
    v_bias = pair_bias[1].reshape(heads, HD)
    kv_bias = jnp.concatenate([jnp.zeros_like(v_bias), v_bias], axis=1).reshape(2 * W)
    bias = jnp.concatenate([kv_bias, pair_bias[0], jnp.zeros((pad,), f32)])[None]
    high = (lax.axis_index("dp") & 1).astype(jnp.int32)
    spots = jnp.stack([t, high])
    mixer_in, kv, q = pre(hids, gains, qkv_w, bias, cos, sin, heads)
    feed_gains, feed_bias = gains[2:], up_bias[None]
    early_ops = (feed_gains, feed_bias, first, start)
    down_own = jnp.concatenate([down_weight.T, out_own[:, pad:]], axis=1)
    down_w, _ = gather_dp(down_own, down_order, [qkv_parts[-2]] + [None] * (bits - 2) + [(gs[2], up_w, early_ops)])
    tail = shift(after(kv, down_w), "dp", 1)
    normed, g, branch, back, do, ffn_send, ffn_keep, ffn_sums = ffn(
        hids, gs, feed_gains, up_w, down_w, qkv_w, feed_bias, high[None], heads, chunk
    )
    attn_args = (spots, first, start, tail, kv, q, do, cos, sin, blk)
    *early, dtail_low, carry = attention(*attn_args)
    ahead_low = shift(dtail_low, "dp", -1)
    ffn_order = down_order[::-1]
    ffn_other = swap(after(ffn_send, tail), "dp", 1 << ffn_order[0])
    o, dq, dtail_high, dkv_low, dkv_high = attention(*attn_args, early=(carry, *early))
    ahead_high = shift(after(dtail_high, ahead_low, ffn_other), "dp", -1)
    post_args = (dq, cos, sin, normed, mixer_in, back, mixer_gain[None], qkv_w)
    ffn_first = ffn_keep.astype(f32) + ffn_other.astype(f32)
    ffn_send, ffn_keep = halves(ffn_first, chunk, ffn_order[1:], ffn_order[1])
    ffn_other = swap(ffn_send, "dp", 1 << ffn_order[1])
    early = post(0, spots, dkv_low, after(ahead_low, ffn_first), *post_args, early=(ffn_sums,))
    *branch, mid_grad = mid(after(o, early[3]), dq, mixer_in, g, branch, qkv_w, down_w)
    *hat, mix_send, mix_keep, sums = post(
        1, spots, dkv_high, ahead_high, *post_args, early=(*early, mid_grad), chunk=chunk
    )
    mix_order = ffn_order
    *hat, mix_send, mix_keep, sums, ffn_other = lax.optimization_barrier((*hat, mix_send, mix_keep, sums, ffn_other))
    mix_other = swap(mix_send, "dp", 1 << mix_order[0])
    hat_own, far = scatter_core(*hat)
    landed_far = swap(far, "tensor", 2)
    branch_own, branch_far = scatter_core(*branch)
    branch_across = swap(after(branch_far, landed_far), "tensor", 2)
    ffn_grads = ffn_keep.astype(f32) + after(ffn_other, far).astype(f32)
    for n in range(2, bits):
        ffn_send, ffn_keep = halves(ffn_grads, chunk, ffn_order[n:], ffn_order[n])
        ffn_other = swap(ffn_send, "dp", 1 << ffn_order[n])
        ffn_grads = ffn_keep.astype(f32) + ffn_other.astype(f32)
    mix_other = after(mix_other, far, branch_far, ffn_send).astype(f32)
    mix_grads = mix_keep.astype(f32) + mix_other[: mix_keep.shape[0]]
    sums = sums + (mix_other[-16:-8] + mix_other[-8:])
    for n in range(1, bits - 1):
        mix_grads, sums = scatter_step(mix_grads, chunk, mix_order[n:], mix_order[n], landed_far if n == 1 else None, sums)
    mix_send, mix_keep = halves(mix_grads, chunk, mix_order[-1:], mix_order[-1])
    one, two = two_parts(sums)
    mix_send = jnp.concatenate([mix_send, one.astype(bf16), two.astype(bf16)], axis=0)
    mix_other = swap(mix_send, "dp", 1 << mix_order[-1])
    ffn_other = after(ffn_other, mix_send)
    up_grad, down_grad = ffn_finish(ffn_keep, ffn_other)
    grad_hat = hat_own + after(landed_far, mix_send).astype(f32)
    own, inv_std = normalize(hidden_in.astype(f32))
    first_mean = jnp.mean(grad_hat, axis=-1, keepdims=True)
    second_mean = jnp.mean(grad_hat * own, axis=-1, keepdims=True)
    grad_hidden = out_grad.astype(f32) + inv_std * (grad_hat - first_mean - own * second_mean)
    mix_other = after(mix_other, up_grad, grad_hidden)
    triple_grad, out_grad_t, sums = mix_finish(mix_keep, mix_other, one + two, W)
    result = hidden_in.astype(f32) + branch_own + after(branch_across, sums).astype(f32) + out_bias
    norm_sums = sums + swap(sums, "tensor", 1)
    norm_sums = norm_sums + swap(norm_sums, "tensor", 2)
    head_sums = sums[2, : 2 * W].reshape(heads, 2, HD)[:, 1].reshape(W)
    pair_grad = jnp.stack([sums[2, 2 * W : 3 * W], head_sums])
    return (
        result,
        grad_hidden,
        norm_sums[0],
        norm_sums[1],
        norm_sums[3],
        norm_sums[4],
        jnp.transpose(triple_grad, (1, 0, 2)),
        pair_grad,
        out_grad_t,
        up_grad,
        sums[5],
        down_grad.T,
        norm_sums[6],
    )


def solution(mesh):
    rows = P(("dp", "tensor"), None)
    in_specs = (
        rows, P("dp"), P(), P(), P(), P(), P("dp", None, "tensor"), P(None, "tensor"), P("tensor", "dp"),
        P("dp", "tensor"), P("tensor"), P("tensor", "dp"), P(), rows,
    )
    out_specs = (
        rows, rows, P(), P(), P(), P(), P("dp", None, "tensor"), P(None, "tensor"), P("tensor", "dp"),
        P("dp", "tensor"), P("tensor"), P("tensor", "dp"), P(),
    )
    return jax.shard_map(shards, mesh=mesh, in_specs=in_specs, out_specs=out_specs, check_vma=False)
```

```python
import functools
import math

import jax
import jax.numpy as jnp
from jax import lax
from jax.experimental import pallas as pl
from jax.experimental.pallas import tpu as pltpu
from jax.sharding import PartitionSpec as P

HD = 64
ROT = 16
DOC_MOST = 2048
EPSILON = 1e-05
NEG = -1e30
TQ = 256
TK = 256
NK = 4
TR = 512
FR = 512
PR = 1024
MR = 1024
bf16 = jnp.bfloat16
f32 = jnp.float32
NN = (((1,), (0,)), ((), ()))
NT = (((1,), (1,)), ((), ()))
TN = (((0,), (0,)), ((), ()))
TT = (((0,), (1,)), ((), ()))
VMEM_LIMIT = 56 * 2**20


def cost(us):
    return pl.CostEstimate(flops=int(us * 1.15e9), bytes_accessed=1000, transcendentals=0)


def mm(left, right, dims=NN):
    return lax.dot_general(left, right, dims, preferred_element_type=f32)


def swap(value, axis, mask):
    count = lax.axis_size(axis)
    return lax.ppermute(value, axis, [(i, i ^ mask) for i in range(count)])


def shift(value, axis, distance):
    count = lax.axis_size(axis)
    route = [(i, i + distance) for i in range(count) if 0 <= i + distance < count]
    return lax.ppermute(value, axis, route)


def bit_count(axis):
    return lax.axis_size(axis).bit_length() - 1


def after(value, *others):
    return lax.optimization_barrier((value, others))[0]


def gather_tensor(own):
    near = swap(own, "tensor", 1)
    far = swap(own, "tensor", 2)
    diagonal = swap(far, "tensor", 1)
    return [own, near, far, diagonal]


def scatter_core(kept, sent):
    near = swap(sent, "tensor", 1).astype(f32)
    total = kept.astype(f32) + near
    rows = kept.shape[0] // 2
    return total[:rows], total[rows:].astype(bf16)


def split(held, rows, left, bit):
    above = 1 << sum(b > bit for b in left)
    return held.reshape(above, 2, -1, held.shape[-1])


def gather_dp(own, order, gates=()):
    me = lax.axis_index("dp")
    rows, cols = own.shape
    held, done = own, []
    parts = []
    for n, bit in enumerate(order):
        if n == 0 and gates and gates[0] is not None:
            held = after(held, gates[0])
        other = swap(held, "dp", 1 << bit)
        if n + 1 < len(gates) and gates[n + 1] is not None:
            other = after(other, gates[n + 1])
        high = ((me >> bit) & 1) == 1
        above = 1 << sum(b > bit for b in done)
        one, two = held.reshape(above, -1, cols), other.reshape(above, -1, cols)
        held = jnp.concatenate([jnp.where(high, two, one), jnp.where(high, one, two)], axis=1).reshape(-1, cols)
        done.append(bit)
        parts.append(held)
    return held, parts


def two_parts(sums):
    first = lax.reduce_precision(sums, 8, 7)
    return first, lax.reduce_precision(sums - first, 8, 7)


def halves(held, rows, left, bit):
    cols = held.shape[1]
    pairs = split(held, rows, left, bit)
    high = ((lax.axis_index("dp") >> bit) & 1) == 1
    send = jnp.where(high, pairs[:, 0], pairs[:, 1]).astype(bf16).reshape(-1, cols)
    keep = jnp.where(high, pairs[:, 1], pairs[:, 0]).reshape(-1, cols)
    return send, keep


def scatter_step(held, rows, left, bit, landed=None, sums=None):
    send, keep = halves(held, rows, left, bit)
    count = send.shape[0]
    if sums is not None:
        first, second = two_parts(sums)
        send = jnp.concatenate([send, first.astype(bf16), second.astype(bf16)], axis=0)
    other = swap(send, "dp", 1 << bit)
    if landed is not None:
        other = after(other, landed)
    other = other.astype(f32)
    held = keep.astype(f32) + other[:count]
    if sums is None:
        return held
    return held, (first + second) + (other[count : count + 8] + other[count + 8 :])


def sum_over(value, axis):
    for bit in range(bit_count(axis)):
        value = value + swap(value, axis, 1 << bit)
    return value


def normalize(values):
    centred = values - jnp.mean(values, axis=-1, keepdims=True)
    inv_std = lax.rsqrt(jnp.mean(centred * centred, axis=-1, keepdims=True) + EPSILON)
    return (centred * inv_std, inv_std)


def rows_spec(cols, tile=TR):
    return pl.BlockSpec((tile, cols), lambda i: (i, 0))


def whole_spec(shape):
    return pl.BlockSpec(shape, lambda i: (0,) * len(shape))


def heads_spec(heads, cols=128, tile=TR):
    return pl.BlockSpec((heads, tile, cols), lambda i: (0, i, 0))


def piece_specs(count, rows, cols, tile=TR):
    per = rows // tile
    return [pl.BlockSpec((tile, cols), lambda i, p=p: (jnp.clip(i - p * per, 0, per - 1), 0)) for p in range(count)]


def pick(refs, rows):
    at = pl.program_id(0) // (rows // refs[0].shape[0])
    value = refs[0][...]
    for n, ref in enumerate(refs[1:]):
        value = jnp.where(at == n + 1, ref[...], value)
    return value


def rotation_rows(cos, sin):
    ones = jnp.ones((128 - ROT, cos.shape[1]), f32)
    return jnp.concatenate([cos, cos, ones], axis=0).T, jnp.concatenate([-sin, sin, ones * 0.0], axis=0).T


def rotate(x, cos_rows, sin_rows):
    lane = lax.broadcasted_iota(jnp.int32, x.shape, 1)
    partner = jnp.where(lane < ROT // 2, pltpu.roll(x, 128 - ROT // 2, 1), pltpu.roll(x, ROT // 2, 1))
    return x * cos_rows + partner * sin_rows


def pre_kernel(*refs, pieces, blk):
    hids, refs = refs[:pieces], refs[pieces:]
    gains_ref, w_ref, bias_ref, cos_ref, sin_ref, mixer_ref, kv_ref, q_ref = refs
    heads = kv_ref.shape[0]
    normed, _ = normalize(pick(hids, blk).astype(f32))
    mixer = (normed * gains_ref[0:1] + gains_ref[1:2]).astype(bf16)
    mixer_ref[...] = mixer
    proj = mm(mixer, w_ref[...]) + bias_ref[...]
    cos_rows, sin_rows = rotation_rows(cos_ref[...], sin_ref[...])
    lane = lax.broadcasted_iota(jnp.int32, (TR, 128), 1)
    for h in range(heads):
        kv_ref[h] = rotate(proj[:, h * 128 : (h + 1) * 128], cos_rows, sin_rows).astype(bf16)
        at = heads * 128 + (h // 2) * 128
        x = proj[:, at : at + 128]
        if h % 2:
            x = pltpu.roll(x, HD, 1)
        x = jnp.where(lane < HD, rotate(x, cos_rows, sin_rows) * (1.0 / math.sqrt(HD)), 0.0)
        q_ref[h] = x.astype(bf16)


def pre(hids, gains, w, bias, cos, sin, heads):
    blk, D = hids[0].shape
    T = blk * len(hids)
    return pl.pallas_call(
        functools.partial(pre_kernel, pieces=len(hids), blk=blk),
        grid=(T // TR,),
        in_specs=piece_specs(len(hids), blk, D) + [
            whole_spec(gains.shape),
            whole_spec(w.shape),
            whole_spec(bias.shape),
            pl.BlockSpec((8, TR), lambda i: (0, i)),
            pl.BlockSpec((8, TR), lambda i: (0, i)),
        ],
        out_specs=[rows_spec(D)] + [heads_spec(heads)] * 2,
        out_shape=[jax.ShapeDtypeStruct((T, D), bf16)] + [jax.ShapeDtypeStruct((heads, T, 128), bf16)] * 2,
        compiler_params=pltpu.CompilerParams(vmem_limit_bytes=40 * 2**20),
        cost_estimate=cost(0.5),
        name="pre",
    )(*hids, gains, w, bias, cos, sin)


def gelu_parts(h):
    mag = jnp.abs(h) * (1.0 / math.sqrt(2.0))
    t = 1.0 / (1.0 + 0.3275911 * mag)
    poly = t * (0.254829592 + t * (-0.284496736 + t * (1.421413741 + t * (-1.453152027 + t * 1.061405429))))
    bell = jnp.exp(-0.5 * h * h)
    tail = 0.5 * poly * bell
    return (jnp.where(h >= 0, 1.0 - tail, tail), bell * (1.0 / math.sqrt(2.0 * math.pi)))


def store_halves(total, high, chunk, send_ref, keep_ref):
    count = total.shape[0] // chunk
    low, top = (
        jnp.concatenate([total[n * chunk : (n + 1) * chunk] for n in range(side, count, 2)], axis=0) for side in (0, 1)
    )
    send_ref[: total.shape[0] // 2] = jnp.where(high == 1, low, top).astype(bf16)
    keep_ref[...] = jnp.where(high == 1, top, low).astype(bf16)


def ffn_kernel(*refs, pieces, blk, chunk):
    hids, gs, refs = refs[:pieces], refs[pieces : 2 * pieces], refs[2 * pieces :]
    gains_ref, up_ref, down_ref, qkv_ref, bias_ref, high_ref, normed_ref, g_ref, branch_ref, back_ref, do_ref, send_ref, keep_ref, sums_ref, acc_ref = refs
    heads = do_ref.shape[0]
    F = bias_ref.shape[1]
    step = pl.program_id(0)
    normed, _ = normalize(pick(hids, blk).astype(f32))
    normed_ref[...] = normed.astype(bf16)
    feed = (normed * gains_ref[0:1] + gains_ref[1:2]).astype(bf16)
    g = pick(gs, blk)
    g_ref[...] = g
    up, down = up_ref[...], down_ref[:, :F]
    hidden = mm(feed, up) + bias_ref[...]
    cumulative, density = gelu_parts(hidden)
    act = (hidden * cumulative).astype(bf16)
    hg = (mm(g, down) * (cumulative + hidden * density)).astype(bf16)
    branch_ref[...] = mm(act, down, NT).astype(bf16)
    back = mm(hg, up, NT)
    back_ref[...] = (back * gains_ref[0:1]).astype(bf16)

    @pl.when(step == 0)
    def _():
        sums_ref[...] = jnp.zeros_like(sums_ref)
        acc_ref[...] = jnp.zeros_like(acc_ref)

    acc_ref[:, :F] += mm(feed, hg, TN)
    acc_ref[:, F:] += mm(g, act, TN)
    sums_ref[3:4] += jnp.sum(back * normed, axis=0, keepdims=True)
    sums_ref[4:5] += jnp.sum(back, axis=0, keepdims=True)
    sums_ref[5:6] += jnp.sum(hg.astype(f32), axis=0, keepdims=True)

    @pl.when(step < blk // FR)
    def _():
        sums_ref[6:7] += jnp.sum(g.astype(f32), axis=0, keepdims=True)

    @pl.when(step == pl.num_programs(0) - 1)
    def _():
        store_halves(acc_ref[...], high_ref[0], chunk, send_ref, keep_ref)

    do = jnp.concatenate([mm(g, qkv_ref[...]), mm(g, down_ref[:, F:])], axis=1)
    lane = lax.broadcasted_iota(jnp.int32, (FR, 128), 1)
    for h in range(heads):
        at = HD * (h + 1)
        x = do[:, at // 128 * 128 : at // 128 * 128 + 128]
        if at % 128 == 0:
            x = pltpu.roll(x, HD, 1)
        do_ref[h] = jnp.where(lane < HD, 0.0, x).astype(bf16)


def ffn(hids, gs, gains, up, down, qkv, bias, high, heads, chunk):
    blk, D = gs[0].shape
    T = blk * len(gs)
    F = bias.shape[1]
    rows = rows_spec(D, FR)
    return pl.pallas_call(
        functools.partial(ffn_kernel, pieces=len(gs), blk=blk, chunk=chunk),
        grid=(T // FR,),
        in_specs=piece_specs(len(gs), blk, D, FR) * 2
        + [whole_spec(gains.shape), whole_spec(up.shape), whole_spec(down.shape)]
        + [pl.BlockSpec((D, 128), lambda i: (0, qkv.shape[1] // 128 - 1)), whole_spec(bias.shape)]
        + [pl.BlockSpec(memory_space=pltpu.SMEM)],
        out_specs=[rows] * 4 + [heads_spec(heads, 128, FR)] + [whole_spec((D // 2, 2 * F))] * 2 + [whole_spec((8, D))],
        out_shape=[jax.ShapeDtypeStruct((T, D), bf16)] * 4
        + [
            jax.ShapeDtypeStruct((heads, T, 128), bf16),
            jax.ShapeDtypeStruct((D // 2, 2 * F), bf16),
            jax.ShapeDtypeStruct((D // 2, 2 * F), bf16),
            jax.ShapeDtypeStruct((8, D), f32),
        ],
        scratch_shapes=[pltpu.VMEM((D, 2 * F), f32)],
        compiler_params=pltpu.CompilerParams(vmem_limit_bytes=VMEM_LIMIT),
        cost_estimate=cost(0.5),
        name="ffn",
    )(*hids, *gs, gains, up, down, qkv, bias, high)


def attn_kernel(*refs, T, blk, heads, late):
    if late:
        (place_ref, first_ref, start_ref, tail_ref, kv_ref, q_ref, do_ref, cos_ref, sin_ref, carry_ref, o_in, dq_in,
         o_ref, dq_ref, dtail_ref, low_ref, high_ref, *refs) = refs
    else:
        (place_ref, first_ref, start_ref, tail_ref, kv_ref, q_ref, do_ref, cos_ref, sin_ref,
         o_ref, dq_ref, dtail_ref, carry_ref, *refs) = refs
    kv_scr, dkv_scr, s_scr, dp_scr, o_acc, dq_acc, qd_scr = refs
    half = T // 2
    base = half if late else 0
    t = place_ref[0]
    inner = (t & 1) * blk
    H = range(heads)

    def half_at(n):
        return pl.ds(pl.multiple_of((n ^ (t >> 1)) * half, half), half)

    for n, (ref, part) in enumerate([(tail_ref, 1), (kv_ref, 0), (kv_ref, 1)] if late else [(tail_ref, 0), (tail_ref, 1), (kv_ref, 0)]):
        kv_scr[:, n * half : (n + 1) * half] = ref[:, half_at(part), :]
    if late:
        dkv_scr[:, :T] = carry_ref[...]
        dkv_scr[:, T:] = jnp.zeros_like(dkv_scr[:, T:])
        o_ref[:, half_at(0)] = o_in[...]
        dq_ref[:, half_at(0)] = dq_in[...]
    else:
        dkv_scr[...] = jnp.zeros_like(dkv_scr)

    def place(row):
        return (row - base) ^ inner

    def q_tile(qi, c):
        q0 = pl.multiple_of(base + qi * TQ, TQ)
        qr = pl.multiple_of(q0 ^ (t * blk), TQ)
        out = qr if late else pl.multiple_of(place(q0), TQ)
        for h in H:
            qd_scr[h, :TQ] = q_ref[h, pl.ds(qr, TQ), :]
            qd_scr[h, TQ:] = do_ref[h, pl.ds(qr, TQ), :]
        start = start_ref[:, pl.ds(qr, TQ)]
        qidx = q0 + T + lax.broadcasted_iota(jnp.int32, (1, TQ), 1)
        first = first_ref[base // TQ + qi]
        stop = (q0 + T) // TK + TQ // TK
        count = stop - first

        def over(body, init):
            pairs = count // NK
            state = lax.fori_loop(0, pairs, lambda i, c: body(first + i * NK, c, NK), init)
            return lax.fori_loop(first + pairs * NK, stop, lambda i, c: body(i, c, 1), state)

        def pass1(ki, state, nk):
            rows = nk * TK
            slot = ki - first
            j = ki * TK + lax.broadcasted_iota(jnp.int32, (rows, TQ), 0)
            ok = (j >= start) & (j <= qidx)
            ats = [pl.multiple_of(place((ki + n) * TK), TK) for n in range(nk)]
            sdps = [mm(jnp.concatenate([kv_scr[h, pl.ds(at, TK), :] for at in ats], axis=0), qd_scr[h], NT) for h in H]
            stats = []
            for h in H:
                m8, l8, d8 = state[3 * h : 3 * h + 3]
                s = jnp.where(ok, sdps[h][:, :TQ], NEG)
                dp = sdps[h][:, TQ:]
                for n in range(nk):
                    s_scr[slot + n, h] = s[n * TK : (n + 1) * TK]
                    dp_scr[slot + n, h] = dp[n * TK : (n + 1) * TK]
                s3 = s.reshape(rows // 8, 8, TQ)
                m_new = jnp.maximum(m8, jnp.max(s3, axis=0))
                alpha = jnp.exp(m8 - m_new)
                e = jnp.exp(s3 - m_new[None])
                l8 = l8 * alpha + jnp.sum(e, axis=0)
                d8 = d8 * alpha + jnp.sum(e * dp.reshape(rows // 8, 8, TQ), axis=0)
                stats += [m_new, l8, d8]
            return tuple(stats)

        z8 = jnp.zeros((8, TQ), f32)
        state = over(pass1, (jnp.full((8, TQ), NEG, f32), z8, z8) * heads)
        lses, deltas = [], []
        for h in H:
            m8, l8, d8 = state[3 * h : 3 * h + 3]
            m = jnp.max(m8, axis=0, keepdims=True)
            w = jnp.exp(m8 - m)
            total = jnp.sum(l8 * w, axis=0, keepdims=True)
            lses.append(m + jnp.log(total))
            deltas.append(jnp.sum(d8 * w, axis=0, keepdims=True) / total)
        o_acc[...] = jnp.zeros_like(o_acc)
        dq_acc[...] = jnp.zeros_like(dq_acc)

        def pass2(ki, c2, nk):
            slot = ki - first
            ats = [pl.multiple_of(place((ki + n) * TK), TK) for n in range(nk)]
            for h in H:
                dq = dq_acc[h]
                o = o_acc[h]
                for n in range(nk):
                    p = jnp.exp(s_scr[slot + n, h] - lses[h])
                    ds = (p * (dp_scr[slot + n, h] - deltas[h])).astype(bf16)
                    p = p.astype(bf16)
                    dkv_scr[h, pl.ds(ats[n], TK), :] += mm(jnp.concatenate([ds, p], axis=1), qd_scr[h])
                    kvt = kv_scr[h, pl.ds(ats[n], TK), :].T
                    dq += mm(kvt[:HD], ds)
                    o += mm(kvt[HD:], p)
                dq_acc[h] = dq
                o_acc[h] = o
            return c2

        over(pass2, 0)
        cos = cos_ref[:, pl.ds(qr, TQ)]
        sin = sin_ref[:, pl.ds(qr, TQ)]
        for h in H:
            o_ref[h * HD : (h + 1) * HD, pl.ds(out, TQ)] = o_acc[h].astype(bf16)
            dq = dq_acc[h] * (1.0 / math.sqrt(HD))
            a, b = dq[: ROT // 2], dq[ROT // 2 : ROT]
            dq = jnp.concatenate([a * cos + b * sin, b * cos - a * sin, dq[ROT:]], axis=0)
            dq_ref[h * HD : (h + 1) * HD, pl.ds(out, TQ)] = dq.astype(bf16)
        return c

    lax.fori_loop(0, half // TQ, q_tile, 0)
    dtail_ref[...] = dkv_scr[:, :half].astype(bf16)
    if late:
        low_ref[...] = dkv_scr[:, half:T]
        high_ref[...] = dkv_scr[:, T:]
    else:
        carry_ref[...] = dkv_scr[:, half:]


def attention(place, first, start, tail, kv, q, do, cos, sin, blk, early=()):
    heads, T, _ = q.shape
    W = heads * HD
    late = len(early) > 0
    vmem = pl.BlockSpec(memory_space=pltpu.VMEM)
    smem = pl.BlockSpec(memory_space=pltpu.SMEM)
    slots = DOC_MOST // TK + TQ // TK
    span = T if late else T // 2
    outs = [((W, span), bf16), ((W, span), bf16), ((heads, T // 2, 128), bf16)]
    outs += [((heads, T // 2, 128), f32)] * 2 if late else [((heads, T, 128), f32)]
    return pl.pallas_call(
        functools.partial(attn_kernel, T=T, blk=blk, heads=heads, late=late),
        in_specs=[smem, smem] + [vmem] * (7 + len(early)),
        out_specs=[vmem] * len(outs),
        scratch_shapes=[
            pltpu.VMEM((heads, T + T // 2, 128), bf16),
            pltpu.VMEM((heads, T + T // 2, 128), f32),
            pltpu.VMEM((slots, heads, TK, TQ), f32),
            pltpu.VMEM((slots, heads, TK, TQ), f32),
            pltpu.VMEM((heads, HD, TQ), f32),
            pltpu.VMEM((heads, HD, TQ), f32),
            pltpu.VMEM((heads, 2 * TQ, 128), bf16),
        ],
        out_shape=[jax.ShapeDtypeStruct(*out) for out in outs],
        compiler_params=pltpu.CompilerParams(vmem_limit_bytes=36 * 2**20),
        cost_estimate=cost(0.1),
        name="attn",
    )(place, first, start, tail, kv, q, do, cos, sin, *early)


def mid_kernel(o_ref, dq_ref, mixer_ref, g_ref, branch_ref, qkv_ref, down_ref, kept_ref, sent_ref, grad_ref, acc_ref):
    W = o_ref.shape[0]
    pad = qkv_ref.shape[1] - HD
    step = pl.program_id(0)
    o = o_ref[...]
    rows = jnp.concatenate([jnp.zeros((pad, o.shape[1]), f32), o.astype(f32)], axis=0).T.astype(bf16)
    out = mm(rows[:, : pad + HD], qkv_ref[...], NT) + mm(rows[:, pad + HD :], down_ref[...], NT)
    out = (out + branch_ref[...].astype(f32)).astype(bf16)
    kept_ref[...], sent_ref[...] = out[: MR // 2], out[MR // 2 :]

    @pl.when(step == 0)
    def _():
        acc_ref[...] = jnp.zeros_like(acc_ref)

    acc_ref[:W] += mm(dq_ref[...], mixer_ref[...])
    acc_ref[W:] += mm(o, g_ref[...])

    @pl.when(step == pl.num_programs(0) - 1)
    def _():
        grad_ref[...] = acc_ref[...].T.astype(bf16)


def mid(o, dq, mixer, g, branch, qkv, down):
    T, D = mixer.shape
    W = o.shape[0]
    cols = pl.BlockSpec((W, MR), lambda i: (0, i))
    rows = rows_spec(D, MR)
    rest = W - HD
    return pl.pallas_call(
        mid_kernel,
        grid=(T // MR,),
        in_specs=[
            cols, cols, rows, rows, rows,
            pl.BlockSpec((D, 128), lambda i: (0, qkv.shape[1] // 128 - 1)),
            pl.BlockSpec((D, rest), lambda i: (0, down.shape[1] // rest - 1)),
        ],
        out_specs=[rows_spec(D, MR // 2)] * 2 + [whole_spec((D, 2 * W))],
        out_shape=[jax.ShapeDtypeStruct((T // 2, D), bf16)] * 2 + [jax.ShapeDtypeStruct((D, 2 * W), bf16)],
        scratch_shapes=[pltpu.VMEM((2 * W, D), f32)],
        compiler_params=pltpu.CompilerParams(vmem_limit_bytes=VMEM_LIMIT),
        cost_estimate=cost(0.1),
        name="mid",
    )(o, dq, mixer, g, branch, qkv, down)


def post_kernel(place_ref, dkv_ref, ahead_ref, dq_ref, cos_ref, sin_ref, normed_ref, mixer_ref, back_ref, gain_ref, w_ref, *refs, chunk):
    heads = dkv_ref.shape[0]
    W = heads * HD
    step = pl.program_id(0)
    late = chunk is not None
    if late:
        _, _, acc_in, sums_in, mid_ref, kept_ref, sent_ref, send_ref, keep_ref, sums_ref, acc_ref = refs
    else:
        acc_in = None
        sums_in, kept_ref, sent_ref, grad_ref, sums_ref, acc_ref = refs

    @pl.when(step == 0)
    def _():
        sums_ref[...] = sums_in[...]
        acc_ref[...] = jnp.zeros_like(acc_ref) if acc_in is None else acc_in[...]

    cos_rows, sin_rows = rotation_rows(cos_ref[...], sin_ref[...])
    kv = jnp.concatenate(
        [rotate(dkv_ref[h] + ahead_ref[h].astype(f32), cos_rows, -sin_rows).astype(bf16) for h in range(heads)], axis=1
    )
    acc_ref[...] += mm(mixer_ref[...], kv, TN)
    dq = dq_ref[...].astype(f32).T.astype(bf16)
    part = mm(kv, w_ref[:, : 2 * W], NT) + mm(dq, w_ref[:, 2 * W : 3 * W], NT)
    hat = (part * gain_ref[...] + back_ref[...].astype(f32)).astype(bf16)
    kept_ref[...], sent_ref[...] = hat[: PR // 2], hat[PR // 2 :]
    sums_ref[0:1] += jnp.sum(part * normed_ref[...].astype(f32), axis=0, keepdims=True)
    sums_ref[1:2] += jnp.sum(part, axis=0, keepdims=True)
    sums_ref[2:3, : 2 * W] += jnp.sum(kv.astype(f32), axis=0, keepdims=True)
    sums_ref[2:3, 2 * W : 3 * W] += jnp.sum(dq.astype(f32), axis=0, keepdims=True)

    @pl.when(step == pl.num_programs(0) - 1)
    def _():
        if late:
            total = jnp.concatenate([acc_ref[...], mid_ref[...].astype(f32)], axis=1)
            store_halves(total, place_ref[1], chunk, send_ref, keep_ref)
            one = sums_ref[...].astype(bf16).astype(f32)
            two = (sums_ref[...] - one).astype(bf16).astype(f32)
            sums_ref[...] = one + two
            send_ref[total.shape[0] // 2 :] = jnp.concatenate([one, two], axis=0).astype(bf16)
        else:
            grad_ref[...] = acc_ref[...]


def post(part, place, dkv, ahead, dq, cos, sin, normed, mixer, back, gain, w, early=(), chunk=None):
    T, D = mixer.shape
    heads = dkv.shape[0]
    W = heads * HD
    per = T // 2 // PR

    def at(i, place):
        return (part ^ (place[0] >> 1)) * per + i

    def inner(i, place):
        return i

    def rows(index):
        return pl.BlockSpec((PR, D), lambda i, place: (index(i, place), 0))

    def cols(count):
        return pl.BlockSpec((count, PR), lambda i, place: (0, at(i, place)))

    def fixed(shape):
        return pl.BlockSpec(shape, lambda i, place: (0,) * len(shape))

    half = pl.BlockSpec((heads, PR, 128), lambda i, place: (0, i, 0))
    late = len(early) > 1
    specs = [half, half, cols(W), cols(8), cols(8), rows(at), rows(at), rows(at), fixed(gain.shape), fixed(w.shape)]
    if late:
        specs += [pl.BlockSpec(memory_space=pl.ANY)] * 2 + [fixed((D, 2 * W)), fixed((8, D)), fixed((D, 2 * W))]
        grads = [fixed((D // 2 + 16, 4 * W)), fixed((D // 2, 4 * W))]
        shapes = [jax.ShapeDtypeStruct((D // 2 + 16, 4 * W), bf16), jax.ShapeDtypeStruct((D // 2, 4 * W), bf16)]
    else:
        specs += [fixed((8, D))]
        grads = [fixed((D, 2 * W))]
        shapes = [jax.ShapeDtypeStruct((D, 2 * W), f32)]
    return pl.pallas_call(
        functools.partial(post_kernel, chunk=chunk),
        grid_spec=pltpu.PrefetchScalarGridSpec(
            num_scalar_prefetch=1,
            grid=(per,),
            in_specs=specs,
            out_specs=[pl.BlockSpec((PR // 2, D), lambda i, place: (at(i, place), 0))] * 2 + grads + [fixed((8, D))],
            scratch_shapes=[pltpu.VMEM((D, 2 * W), f32)],
        ),
        out_shape=[
            jax.ShapeDtypeStruct((T // 2, D), bf16),
            jax.ShapeDtypeStruct((T // 2, D), bf16),
            *shapes,
            jax.ShapeDtypeStruct((8, D), f32),
        ],
        input_output_aliases={11: 0, 12: 1} if late else {},
        compiler_params=pltpu.CompilerParams(vmem_limit_bytes=VMEM_LIMIT),
        cost_estimate=cost(8 if late else 0.1),
        name="post",
    )(place, dkv, ahead, dq, cos, sin, normed, mixer, back, gain, w, *early)


def mix_finish_kernel(keep_ref, other_ref, own_ref, triple_ref, out_ref, sums_ref):
    rows = keep_ref.shape[0]
    W = out_ref.shape[0]
    other = other_ref[...].astype(f32)
    total = keep_ref[...] + other[:rows]
    sums_ref[...] = own_ref[...] + (other[rows : rows + 8] + other[rows + 8 :])
    triple_ref[0] = total[:, 2 * W : 3 * W]
    for n in range(2):
        triple_ref[1 + n] = jnp.concatenate(
            [total[:, at + n * HD : at + (n + 1) * HD] for at in range(0, 2 * W, 2 * HD)], axis=1
        )
    out_ref[...] = total[:, 3 * W :].T


def mix_finish(keep, other, own, W):
    rows = keep.shape[0]
    return pl.pallas_call(
        mix_finish_kernel,
        out_shape=[
            jax.ShapeDtypeStruct((3, rows, W), f32),
            jax.ShapeDtypeStruct((W, rows), f32),
            jax.ShapeDtypeStruct(own.shape, f32),
        ],
        cost_estimate=cost(0.1),
        name="mix_finish",
    )(keep, other, own)


def ffn_finish_kernel(keep_ref, other_ref, up_ref, down_ref):
    F = up_ref.shape[1]
    total = keep_ref[...] + other_ref[...].astype(f32)
    up_ref[...] = total[:, :F]
    down_ref[...] = total[:, F:]


def ffn_finish(keep, other):
    rows, cols = keep.shape
    F = cols // 2
    return pl.pallas_call(
        ffn_finish_kernel,
        out_shape=[jax.ShapeDtypeStruct((rows, F), f32)] * 2,
        cost_estimate=cost(0.1),
        name="ffn_finish",
    )(keep, other)


def shards(
    hidden_in, positions, mixer_gain, mixer_shift, feed_gain, feed_shift, triple_weight,
    pair_bias, output_weight, up_weight, up_bias, down_weight, out_bias, out_grad,
):
    T = positions.shape[0]
    blk, D = hidden_in.shape
    W = pair_bias.shape[1]
    heads = W // HD
    chunk = triple_weight.shape[0]
    t = lax.axis_index("tensor").astype(jnp.int32)

    F = up_weight.shape[1]
    bits = bit_count("dp")
    down_order = list(reversed(range(bits)))
    mixed_order = down_order[:-2] + [0, 1]
    q_w, k_w, v_w = (triple_weight[:, i].reshape(chunk, heads, HD) for i in range(3))
    kv_w = jnp.concatenate([k_w, v_w], axis=2).reshape(chunk, 2 * W)
    pad = (-W) % 128
    out_own = output_weight.T
    up_w, up_parts = gather_dp(up_weight, down_order)
    qkv_own = jnp.concatenate([kv_w, q_w.reshape(chunk, W), out_own[:, :pad]], axis=1)
    qkv_w, qkv_parts = gather_dp(qkv_own, down_order, [up_parts[0]])
    hids = gather_tensor(hidden_in)
    gs = gather_tensor(after(out_grad, hids[2]))

    pos = jnp.concatenate([lax.dynamic_slice(positions, ((r ^ t) * blk,), (blk,)) for r in range(T // blk)])
    inverse = 1.0 / 10000.0 ** (jnp.arange(ROT // 2, dtype=f32) * (2.0 / ROT))
    angles = pos.astype(f32)[None, :] * inverse[:, None]
    cos, sin = jnp.cos(angles), jnp.sin(angles)
    rows = jnp.arange(T, dtype=jnp.int32) ^ (t * blk)
    start = (rows + T - pos)[None]
    q_starts = jnp.arange(0, T, TQ, dtype=jnp.int32)
    first = (q_starts + T - positions[::TQ]) // TK

    gains = jnp.stack([mixer_gain, mixer_shift, feed_gain, feed_shift])
    v_bias = pair_bias[1].reshape(heads, HD)
    kv_bias = jnp.concatenate([jnp.zeros_like(v_bias), v_bias], axis=1).reshape(2 * W)
    bias = jnp.concatenate([kv_bias, pair_bias[0], jnp.zeros((pad,), f32)])[None]
    high = (lax.axis_index("dp") & 1).astype(jnp.int32)
    spots = jnp.stack([t, high])
    mixer_in, kv, q = pre(hids, gains, qkv_w, bias, cos, sin, heads)
    feed_gains, feed_bias = gains[2:], up_bias[None]
    early_ops = (feed_gains, feed_bias, first, start)
    down_own = jnp.concatenate([down_weight.T, out_own[:, pad:]], axis=1)
    down_w, _ = gather_dp(down_own, down_order, [qkv_parts[-2]] + [None] * (bits - 2) + [(up_w, early_ops), gs[2]])
    tail = shift(after(kv, down_w), "dp", 1)
    normed, g, branch, back, do, ffn_send, ffn_keep, ffn_sums = ffn(
        hids, gs, feed_gains, up_w, down_w, qkv_w, feed_bias, high[None], heads, chunk
    )
    attn_args = (spots, first, start, tail, kv, q, do, cos, sin, blk)
    *early, dtail_low, carry = attention(*attn_args)
    ahead_low = shift(dtail_low, "dp", -1)
    ffn_order = down_order[::-1]
    ffn_other = swap(after(ffn_send, tail), "dp", 1 << ffn_order[0])
    o, dq, dtail_high, dkv_low, dkv_high = attention(*attn_args, early=(carry, *early))
    ahead_high = shift(after(dtail_high, ahead_low, ffn_other), "dp", -1)
    post_args = (dq, cos, sin, normed, mixer_in, back, mixer_gain[None], qkv_w)
    ffn_first = ffn_keep.astype(f32) + ffn_other.astype(f32)
    ffn_send, ffn_keep = halves(ffn_first, chunk, ffn_order[1:], ffn_order[1])
    ffn_other = swap(ffn_send, "dp", 1 << ffn_order[1])
    early = post(0, spots, dkv_low, after(ahead_low, ffn_first), *post_args, early=(ffn_sums,))
    *branch, mid_grad = mid(after(o, early[3]), dq, mixer_in, g, branch, qkv_w, down_w)
    *hat, mix_send, mix_keep, sums = post(
        1, spots, dkv_high, ahead_high, *post_args, early=(*early, mid_grad), chunk=chunk
    )
    mix_order = ffn_order
    *hat, mix_send, mix_keep, sums, ffn_other = lax.optimization_barrier((*hat, mix_send, mix_keep, sums, ffn_other))
    mix_other = swap(mix_send, "dp", 1 << mix_order[0])
    hat_own, far = scatter_core(*hat)
    landed_far = swap(far, "tensor", 2)
    branch_own, branch_far = scatter_core(*branch)
    branch_across = swap(after(branch_far, landed_far), "tensor", 2)
    ffn_grads = ffn_keep.astype(f32) + after(ffn_other, far).astype(f32)
    for n in range(2, bits):
        ffn_send, ffn_keep = halves(ffn_grads, chunk, ffn_order[n:], ffn_order[n])
        ffn_other = swap(ffn_send, "dp", 1 << ffn_order[n])
        ffn_grads = ffn_keep.astype(f32) + ffn_other.astype(f32)
    mix_other = after(mix_other, far, branch_far, ffn_send).astype(f32)
    mix_grads = mix_keep.astype(f32) + mix_other[: mix_keep.shape[0]]
    sums = sums + (mix_other[-16:-8] + mix_other[-8:])
    for n in range(1, bits - 1):
        mix_grads, sums = scatter_step(mix_grads, chunk, mix_order[n:], mix_order[n], landed_far if n == 1 else None, sums)
    mix_send, mix_keep = halves(mix_grads, chunk, mix_order[-1:], mix_order[-1])
    one, two = two_parts(sums)
    mix_send = jnp.concatenate([mix_send, one.astype(bf16), two.astype(bf16)], axis=0)
    mix_other = swap(mix_send, "dp", 1 << mix_order[-1])
    ffn_other = after(ffn_other, mix_send)
    up_grad, down_grad = ffn_finish(ffn_keep, ffn_other)
    grad_hat = hat_own + after(landed_far, mix_send).astype(f32)
    own, inv_std = normalize(hidden_in.astype(f32))
    first_mean = jnp.mean(grad_hat, axis=-1, keepdims=True)
    second_mean = jnp.mean(grad_hat * own, axis=-1, keepdims=True)
    grad_hidden = out_grad.astype(f32) + inv_std * (grad_hat - first_mean - own * second_mean)
    mix_other = after(mix_other, up_grad, grad_hidden)
    triple_grad, out_grad_t, sums = mix_finish(mix_keep, mix_other, one + two, W)
    result = hidden_in.astype(f32) + branch_own + after(branch_across, sums).astype(f32) + out_bias
    norm_sums = sums + swap(sums, "tensor", 1)
    norm_sums = norm_sums + swap(norm_sums, "tensor", 2)
    head_sums = sums[2, : 2 * W].reshape(heads, 2, HD)[:, 1].reshape(W)
    pair_grad = jnp.stack([sums[2, 2 * W : 3 * W], head_sums])
    return (
        result,
        grad_hidden,
        norm_sums[0],
        norm_sums[1],
        norm_sums[3],
        norm_sums[4],
        jnp.transpose(triple_grad, (1, 0, 2)),
        pair_grad,
        out_grad_t,
        up_grad,
        sums[5],
        down_grad.T,
        norm_sums[6],
    )


def solution(mesh):
    rows = P(("dp", "tensor"), None)
    in_specs = (
        rows, P("dp"), P(), P(), P(), P(), P("dp", None, "tensor"), P(None, "tensor"), P("tensor", "dp"),
        P("dp", "tensor"), P("tensor"), P("tensor", "dp"), P(), rows,
    )
    out_specs = (
        rows, rows, P(), P(), P(), P(), P("dp", None, "tensor"), P(None, "tensor"), P("tensor", "dp"),
        P("dp", "tensor"), P("tensor"), P("tensor", "dp"), P(),
    )
    return jax.shard_map(shards, mesh=mesh, in_specs=in_specs, out_specs=out_specs, check_vma=False)
```
